128 devices in a mesh: replica: 8 (over x, core), tensor: 16 (over z, y).
Axes of the slice: x: 4, y: 4, z: 4, core: 2. Of those that a mesh axis runs over, the one named last changes fastest.
Arguments:
- gated_hidden: bfloat16 [2, 1024, 14336], P(None, 'replica', 'tensor'), may hold values from -6 to 6
- coded_weight: bfloat16 [14336, 8192], P('tensor'), may hold values from -6 to 6, as said below
- block_exponent: int32 [448, 8192], P('tensor'), may hold values from 117 to 120
- stream_input: bfloat16 [2, 1024, 8192], P(None, 'replica', 'tensor'), may hold values from -6 to 6
- lower_layer: bfloat16 [1024, 8192], P('replica', 'tensor'), may hold values from -6 to 6
- middle_layer: bfloat16 [1024, 8192], P('replica', 'tensor'), may hold values from -6 to 6
- prior_lower: bfloat16 [1024, 8192], P('replica', 'tensor'), may hold values from -6 to 6
- prior_middle: bfloat16 [1024, 8192], P('replica', 'tensor'), may hold values from -6 to 6
- prior_upper: bfloat16 [1024, 8192], P('replica', 'tensor'), may hold values from -6 to 6
- accepted: int32 [1024], P('replica'), may hold values from 0 to 2, as said below
- draft_input_weight: float32 [3, 8192, 8192], P(None, 'tensor', 'replica'), may hold values from -0.44194174 to 0.44194174
- draft_gain: float32 [8192], P('replica'), may hold values from 0.5 to 2
Outputs:
- upper_layer: bfloat16 [2, 1024, 8192], P(None, 'replica', 'tensor')
- new_weight: bfloat16 [3, 8192, 8192], P(None, 'tensor', 'replica')
The draws below stay inside these ranges and needn't reach their ends.
Inputs may be any that keep to these rules, and one draw needn't show every extreme that they name: `coded_weight`: the values of the FP4 E2M1 grid: 0, 0.5, 1, 1.5, 2, 3, 4, 6 and their negatives. The accepted lengths of the 128 rows of one replica (aligned blocks of 128 rows) sum to at most 192, and to exactly that in at least one block.
All inputs are finite; a program needn't handle non-finite values.
Results may differ from the reference program's by a relative error of at most 0.005.
Values may be sent and summed in bfloat16 or wider, within the bound.
No kernel may reach another device: no remote copies, remote signals or barrier semaphores. Data moves between devices by JAX's collectives and lax.ppermute only.
A program may use at most 128 MiB of HBM per device.

```python
import math
import jax
import jax.numpy as jnp
from jax import lax

D = 8192
FF = 14336
ROWS = 128
BATCH = 1024
N_REPLICA = 8


def draw_coded_weight(key, part):
    key = jax.random.fold_in(key, 3)
    codes = jax.random.randint(key, (FF, D), 0, 16)
    magnitude = codes % 8
    sign = jnp.where(codes >= 8, -1.0, 1.0).astype(jnp.float32)
    exponent = (magnitude // 2).astype(jnp.float32)
    mantissa = (magnitude % 2).astype(jnp.float32)
    value = jnp.where(exponent == 0.0, 0.5 * mantissa, jnp.exp2(exponent - 1.0) * (1.0 + 0.5 * mantissa))
    return (sign * value).astype(jnp.bfloat16)


def draw_accepted(key, part):
    key = jax.random.fold_in(key, 5)
    first_key, second_key, third_key, fourth_key = jax.random.split(key, 4)
    twos = jax.random.randint(first_key, (N_REPLICA,), ROWS // 4, ROWS // 2 + 1)
    zeros = jax.random.randint(second_key, (N_REPLICA,), 0, ROWS // 4 + 1)
    heaviest_group = jax.random.randint(third_key, (), 0, N_REPLICA)
    chosen = jnp.arange(N_REPLICA) == heaviest_group
    twos = jnp.where(chosen, ROWS // 2, twos)
    zeros = jnp.where(chosen, 0, zeros)
    places = jnp.arange(ROWS)[None, :]
    values = jnp.where(places < twos[:, None], 2, jnp.where(places < twos[:, None] + zeros[:, None], 0, 1)).astype(jnp.int32)
    block_keys = jax.random.split(fourth_key, N_REPLICA)
    shuffled = jax.vmap(lambda block_key, block: jax.random.permutation(block_key, block))(block_keys, values)
    return shuffled.reshape(-1).astype(jnp.int32)


def draw_draft_input_weight(key, part):
    key = jax.random.fold_in(key, 7)
    first_key, second_key, third_key = jax.random.split(key, 3)
    base = jax.random.truncated_normal(first_key, -4.0, 4.0, (3, D, D), jnp.float32)
    row_scale = jnp.exp(jax.random.uniform(second_key, (3, D, 1), jnp.float32) * math.log(10.0)) / 4.6
    column_scale = jnp.exp(jax.random.uniform(third_key, (1, 1, D), jnp.float32) * math.log(10.0)) / 3.9
    rise = 1.732
    ramp = jnp.exp(jnp.arange(D, dtype=jnp.float32) / D * math.log(rise))
    return (base * row_scale * column_scale * ramp / math.sqrt(3.0 * D)).astype(jnp.float32)


def place_ends(drawn, own_key, smallest, top_value):
    spot = [jax.random.randint(jax.random.fold_in(own_key, axis), (), 0, length) for axis, length in enumerate(drawn.shape)]
    widest = drawn.shape.index(max(drawn.shape))
    beside = spot[:widest] + [(spot[widest] + 1) % drawn.shape[widest]] + spot[widest + 1:]
    return drawn.at[tuple(spot)].set(smallest).at[tuple(beside)].set(top_value)


def steps_of(stream_key, shape, cuts, low, top_value):
    factor_of, own = 1.0, jax.random.fold_in(stream_key, 6)
    for axis_at, shards_of in cuts:
        steps = jnp.exp(jax.random.uniform(jax.random.fold_in(own, axis_at), (shards_of,), jnp.float32, low / len(cuts), top_value / len(cuts)))
        factor_of = factor_of * jnp.repeat(steps, shape[axis_at] // shards_of).reshape([-1 if axis == axis_at else 1 for axis in range(len(shape))])
    return factor_of


def centred(rng, dims, scale, reach, cuts=(), kind=jnp.bfloat16):
    array = jax.random.normal(rng, dims, jnp.float32) * scale
    if len(cuts) > 0:
        array = steps_of(rng, dims, cuts, -0.22, 0.18) * array
    return jnp.clip(array, min=-reach, max=reach).astype(kind)


def setup_inputs(seed: int = 0) -> dict:
    keys = jax.random.split(jax.random.key(seed), 13)
    gated_hidden = centred(keys[0], (2, BATCH, FF), 1.0, 6.0, ((1, 8), (2, 16)))
    coded_weight = draw_coded_weight(jax.random.fold_in(keys[12], 71), 0)
    block_exponent = place_ends(jax.random.randint(keys[2], (FF // 32, D), 117, 121), jax.random.fold_in(keys[2], 1), 117, 120).astype(jnp.int32)
    stream_input = centred(keys[3], (2, BATCH, D), 1.0, 6.0, ((1, 8), (2, 16)))
    lower_layer = centred(keys[4], (BATCH, D), 1.0, 6.0, ((0, 8), (1, 16)))
    middle_layer = centred(keys[5], (BATCH, D), 1.0, 6.0, ((0, 8), (1, 16)))
    prior_lower = centred(keys[6], (BATCH, D), 1.0, 6.0, ((0, 8), (1, 16)))
    prior_middle = centred(keys[7], (BATCH, D), 1.0, 6.0, ((0, 8), (1, 16)))
    prior_upper = centred(keys[8], (BATCH, D), 1.0, 6.0, ((0, 8), (1, 16)))
    accepted = draw_accepted(jax.random.fold_in(keys[12], 71), 0)
    draft_input_weight = draw_draft_input_weight(jax.random.fold_in(keys[12], 71), 0)
    draft_gain = jnp.clip(jnp.exp(math.log(2.0) - 1.3862944 * jax.random.uniform(keys[11], (D,), jnp.float32) ** steps_of(keys[11], (D,), ((0, 8),), -0.2, 0.2)), 0.5, 2.0)
    return dict(gated_hidden=gated_hidden, coded_weight=coded_weight, block_exponent=block_exponent, stream_input=stream_input, lower_layer=lower_layer, middle_layer=middle_layer, prior_lower=prior_lower, prior_middle=prior_middle, prior_upper=prior_upper, accepted=accepted, draft_input_weight=draft_input_weight, draft_gain=draft_gain)


step_rate = 8.0
epsilon = 1e-06

def dequantize(coded_weight, block_exponent):
    units, width = coded_weight.shape
    factor = jnp.exp2(block_exponent.astype(jnp.float32) - 127.0).astype(jnp.bfloat16)
    blocks = coded_weight.reshape(units // 32, 32, width) * factor[:, None, :]
    return blocks.reshape(units, width)

def reference(gated_hidden, coded_weight, block_exponent, stream_input, lower_layer, middle_layer, prior_lower, prior_middle, prior_upper, accepted, draft_input_weight, draft_gain):
    weight_down = dequantize(coded_weight, block_exponent)
    steps, batch, units = gated_hidden.shape
    width = coded_weight.shape[1]
    mixed = jnp.dot(gated_hidden.reshape(steps * batch, units), weight_down, preferred_element_type=jnp.float32)
    upper_layer = (stream_input.astype(jnp.float32) + mixed.reshape(steps, batch, width)).astype(jnp.bfloat16)
    first = jnp.concatenate([prior_lower, prior_middle, prior_upper], axis=1)
    second = jnp.concatenate([lower_layer, middle_layer, upper_layer[0]], axis=1)
    features = jnp.concatenate([first, second], axis=0).astype(jnp.float32)
    targets = upper_layer.reshape(steps * batch, width).astype(jnp.float32)
    token_position = jnp.arange(steps * batch, dtype=jnp.int32) // batch
    live = (token_position < jnp.concatenate([accepted, accepted]).astype(jnp.int32)).astype(jnp.float32)
    flat_weight = draft_input_weight.reshape(3 * width, width)
    drafted = jnp.dot(features, flat_weight, precision=lax.Precision.HIGHEST, preferred_element_type=jnp.float32)
    scale = lax.rsqrt(lax.optimization_barrier(jnp.sum(drafted * drafted, axis=1)) / width + epsilon)
    output = draft_gain * drafted * scale[:, None]
    error = draft_gain * (live[:, None] * (output - targets) / (steps * batch))
    inner = lax.optimization_barrier(jnp.sum(error * drafted, axis=1))
    loss_gradient = scale[:, None] * error - drafted * (scale ** 3 * inner / width)[:, None]
    update_step = jnp.dot(features.T, loss_gradient, precision=lax.Precision.HIGHEST, preferred_element_type=jnp.float32)
    new_weight = (draft_input_weight - step_rate * update_step.reshape(3, width, width)).astype(jnp.bfloat16)
    return (upper_layer, new_weight)
```

```python
import functools

import jax
import jax.numpy as jnp
from jax import lax
from jax.experimental import pallas as pl
from jax.experimental.pallas import tpu as pltpu
from jax.sharding import PartitionSpec as P

step_rate = 8.0
epsilon = 1e-06
side = 4
cores = 2
block_units = 32
f32 = jnp.float32
bf16 = jnp.bfloat16
mesh_axes = ("replica", "tensor")
vmem = 56 * 1024 * 1024


def coordinates(device):
    replica, tensor = divmod(device, side * side)
    x, c = divmod(replica, cores)
    z, y = divmod(tensor, side)
    return x, c, z, y


def device_at(x, c, z, y):
    return ((x % side) * cores + c % cores) * side * side + (z % side) * side + y % side


def moved(target):
    return [(d, target(*coordinates(d))) for d in range(side * cores * side * side)]


def along_first(shift):
    return moved(
        lambda x, c, z, y: device_at(x, c, z + shift * (c == 0), y + shift * (c == 1))
    )


def along_second(shift):
    return moved(
        lambda x, c, z, y: device_at(x, c, z + shift * (c == 1), y + shift * (c == 0))
    )


def along_x(shift):
    return moved(lambda x, c, z, y: device_at(x + shift, c, z, y))


def other_core():
    return moved(lambda x, c, z, y: device_at(x, 1 - c, z, y))


def send(array, pairs):
    return lax.ppermute(array, mesh_axes, pairs)


def plus(*terms):
    return functools.reduce(jnp.add, [term.astype(f32) for term in terms])


def relative_tables():
    replica, tensor = lax.axis_index("replica"), lax.axis_index("tensor")
    x, c = replica // cores, replica % cores
    z, y = tensor // side, tensor % side
    step = jnp.arange(side * side, dtype=jnp.int32)
    first, second = step // side, step % side
    zs = (z + jnp.where(c == 0, first, second)) % side
    ys = (y + jnp.where(c == 0, second, first)) % side
    block = zs * side + ys
    late = jnp.where(ys // cores == c, 0, side) + (zs - x) % side
    return block.astype(jnp.int32), late.astype(jnp.int32)


def piece_specs(rows, columns):
    def spec(k):
        return pl.BlockSpec(
            (1, rows, columns), lambda i, *tables: (jnp.clip(i - 2 * k, 0, 1), 0, 0)
        )

    return [spec(k) for k in range(8)]


def piece_shapes(rows, columns):
    return [jax.ShapeDtypeStruct((2, rows, columns), bf16)] * 8


def store_piece(i, value, pieces):
    for k in range(8):

        @pl.when(i // 2 == k)
        def _():
            pieces[k][0] = value


def down_kernel(block_ref, tokens_ref, coded_ref, exponent_ref, *pieces):
    i = pl.program_id(0)
    units, columns = coded_ref.shape
    factor = jnp.exp2(exponent_ref[...].astype(f32) - 127.0).astype(bf16)
    weight = coded_ref[...].reshape(units // block_units, block_units, columns)
    weight = (weight * factor[:, None, :]).reshape(units, columns)
    total = jnp.dot(tokens_ref[...], weight, preferred_element_type=f32)
    store_piece(i, total.astype(bf16), pieces)


def down_pieces(block, tokens, coded_weight, block_exponent):
    rows, units = tokens.shape
    width = coded_weight.shape[1] // (side * side)
    return pl.pallas_call(
        down_kernel,
        grid_spec=pltpu.PrefetchScalarGridSpec(
            num_scalar_prefetch=1,
            grid=(side * side,),
            in_specs=[
                pl.BlockSpec((rows, units), lambda i, block: (0, 0)),
                pl.BlockSpec((units, width), lambda i, block: (0, block[i])),
                pl.BlockSpec((units // block_units, width), lambda i, block: (0, block[i])),
            ],
            out_specs=piece_specs(rows, width),
        ),
        out_shape=piece_shapes(rows, width),
        compiler_params=pltpu.CompilerParams(vmem_limit_bytes=vmem),
        name="down_projection",
    )(block, tokens, coded_weight, block_exponent)


def early_kernel(block_ref, pair_ref, third_ref, weight_ref, early_ref, features_ref):
    i = pl.program_id(0)
    width = third_ref.shape[2]
    layers = pair_ref[0]
    features_ref[0] = layers
    early_ref[0] = jnp.dot(
        layers[:, :width], weight_ref[0], preferred_element_type=f32
    ) + jnp.dot(layers[:, width:], weight_ref[1], preferred_element_type=f32)

    @pl.when(block_ref[i] % 2 == 0)
    def _():
        early_ref[0] += jnp.dot(third_ref[0], weight_ref[2], preferred_element_type=f32)


def early_projection(block, gathered, weight):
    replicas, slots, _ = gathered.shape
    layers, width, columns = weight.shape
    blocks = side * side
    return pl.pallas_call(
        early_kernel,
        grid_spec=pltpu.PrefetchScalarGridSpec(
            num_scalar_prefetch=1,
            grid=(blocks,),
            in_specs=[
                pl.BlockSpec(
                    (1, slots, 2 * width), lambda i, block: (block[i] // 2, 0, block[i] % 2)
                ),
                pl.BlockSpec((1, slots, width), lambda i, block: (block[i] // 2, 0, 4)),
                pl.BlockSpec((layers, width, columns), lambda i, block: (0, 0, 0)),
            ],
            out_specs=[
                pl.BlockSpec((1, slots, columns), lambda i, block: (i, 0, 0)),
                pl.BlockSpec((1, slots, 2 * width), lambda i, block: (i, 0, 0)),
            ],
        ),
        out_shape=[
            jax.ShapeDtypeStruct((blocks, slots, columns), f32),
            jax.ShapeDtypeStruct((blocks, slots, layers * width), bf16),
        ],
        compiler_params=pltpu.CompilerParams(vmem_limit_bytes=vmem),
        name="early_projection",
    )(block, gathered, gathered, weight)


def late_kernel(
    block_ref, late_ref, early_ref, third_ref, late_third_ref, weight_ref, _, features_ref, *pieces
):
    i = pl.program_id(0)
    is_late = block_ref[i] % 2 == 1

    @pl.when(is_late)
    def _():
        features_ref[0] = late_third_ref[0]
        total = early_ref[0] + jnp.dot(
            late_third_ref[0], weight_ref[0], preferred_element_type=f32
        )
        store_piece(i, total.astype(bf16), pieces)

    @pl.when(jnp.logical_not(is_late))
    def _():
        features_ref[0] = third_ref[0]
        store_piece(i, early_ref[0].astype(bf16), pieces)


def late_projection(block, late, early, gathered, late_third, weight, features):
    blocks, slots, columns = early.shape
    layers, width, _ = weight.shape
    outs = pl.pallas_call(
        late_kernel,
        grid_spec=pltpu.PrefetchScalarGridSpec(
            num_scalar_prefetch=2,
            grid=(blocks,),
            in_specs=[
                pl.BlockSpec((1, slots, columns), lambda i, block, late: (i, 0, 0)),
                pl.BlockSpec((1, slots, width), lambda i, block, late: (block[i] // 2, 0, 4)),
                pl.BlockSpec((1, slots, width), lambda i, block, late: (late[i], 0, 0)),
                pl.BlockSpec((1, width, columns), lambda i, block, late: (2, 0, 0)),
                pl.BlockSpec(memory_space=pl.ANY),
            ],
            out_specs=[pl.BlockSpec((1, slots, width), lambda i, block, late: (i, 0, 2))]
            + piece_specs(slots, columns),
        ),
        out_shape=[jax.ShapeDtypeStruct(features.shape, bf16)] + piece_shapes(slots, columns),
        input_output_aliases={6: 0},
        compiler_params=pltpu.CompilerParams(vmem_limit_bytes=vmem),
        name="late_projection",
    )(block, late, early, gathered, late_third, weight, features)
    return outs[0], outs[1:]


def reduce_blocks(pieces):
    rows = pieces[0].shape[1]
    half = rows // 2
    near_right = send(pieces[4], along_first(1))
    near_left = send(pieces[5], along_first(-1))
    direct_right = send(pieces[3], along_first(1))
    direct_left = send(pieces[6], along_first(-1))
    far_right = send(plus(pieces[2], near_right).astype(bf16), along_first(1))
    far_left = send(plus(pieces[7], near_left).astype(bf16), along_first(-1))
    low = plus(pieces[0], far_right, direct_left)
    high = plus(pieces[1], far_left, direct_right)
    own, next_one, opposite, last_one = low[0], low[1], high[0], high[1]
    near_right = send(opposite[:half].astype(bf16), along_second(1))
    near_left = send(opposite[half:].astype(bf16), along_second(-1))
    right = jnp.concatenate([next_one[:half] + near_right.astype(f32), next_one[half:]])
    left = jnp.concatenate([last_one[:half], last_one[half:] + near_left.astype(f32)])
    from_left = send(right.astype(bf16), along_second(1))
    from_right = send(left.astype(bf16), along_second(-1))
    return plus(own, from_left, from_right)


def gather_ring(own, along):
    half = own.shape[0] // 2
    previous = send(own, along(1))
    following = send(own, along(-1))
    opposite_low = send(previous[:half], along(1))
    opposite_high = send(following[half:], along(-1))
    return [own, following, opposite_low, opposite_high, previous]


def body(
    gated_hidden,
    coded_weight,
    block_exponent,
    stream_input,
    lower_layer,
    middle_layer,
    prior_lower,
    prior_middle,
    prior_upper,
    accepted,
    draft_input_weight,
    draft_gain,
):
    steps, rows, unit_count = gated_hidden.shape
    feature_slice = stream_input.shape[2]
    out_slice = draft_input_weight.shape[2]
    replicas = lax.axis_size("replica")
    tensors = lax.axis_size("tensor")
    width = feature_slice * tensors
    slots_all = steps * rows * replicas
    slots = rows * 3 // 4
    block, late = relative_tables()

    with jax.named_scope("down"):
        pieces = down_pieces(
            block, gated_hidden.reshape(steps * rows, unit_count), coded_weight, block_exponent
        )

    with jax.named_scope("select"):
        place = jnp.arange(rows, dtype=jnp.int32)
        before = place[:, None] <= place[None, :]
        first_live = (accepted >= 1).astype(jnp.int32)
        second_live = (accepted >= 2).astype(jnp.int32)
        first_slot = jnp.sum(jnp.where(before, first_live[:, None], 0), axis=0) - 1
        second_slot = 2 * slots - jnp.sum(jnp.where(before, second_live[:, None], 0), axis=0)
        first_slot = jnp.where(first_live == 1, first_slot, -1)
        second_slot = jnp.where(second_live == 1, second_slot, -1)
        slot = jnp.arange(2 * slots, dtype=jnp.int32)[:, None]
        select = (slot == jnp.concatenate([first_slot, second_slot])[None, :]).astype(bf16)

        def pick(chosen, first, second):
            return jnp.dot(
                chosen, jnp.concatenate([first, second]), preferred_element_type=f32
            ).astype(bf16)

        layers = pick(
            select,
            jnp.concatenate([prior_lower, prior_middle], axis=1),
            jnp.concatenate([lower_layer, middle_layer], axis=1),
        )
        third = jnp.dot(
            select[:slots, :rows], prior_upper, preferred_element_type=f32
        ).astype(bf16)
        payload = jnp.concatenate([layers[:slots], layers[slots:], third], axis=1)
    gathered = lax.all_gather(payload, "replica", axis=0, tiled=False)
    weight = draft_input_weight.astype(bf16)

    with jax.named_scope("early"):
        early, features = early_projection(block, gathered, weight)

    with jax.named_scope("reduce_down"):
        summed = reduce_blocks(pieces)
    upper_rows = (
        stream_input.astype(f32) + summed.reshape(steps, rows, feature_slice)
    ).astype(bf16)
    upper_layer = upper_rows

    with jax.named_scope("late"):
        third = pick(select[slots:], prior_upper, upper_rows[0])
        near = [third] + [send(third, along_x(-shift)) for shift in (1, 2, 3)]
        near = jnp.stack(near)
        late_third = jnp.concatenate([near, send(near, other_core())])
        features, pieces = late_projection(
            block, late, early, gathered, late_third, weight, features
        )

    with jax.named_scope("targets"):
        chosen = pick(select, upper_rows[0], upper_rows[1])
        parity = lax.axis_index("tensor") % 2
        even, odd = chosen[:slots], chosen[slots:]
        got = []
        for turn in range(2):
            pairs = []
            for d in range(replicas * tensors):
                r, t = divmod(d, tensors)
                pairs.append((d, (t // 2) * tensors + 2 * r + (t + turn) % 2))
            got.append(send(jnp.where((parity + turn) % 2 == 0, even, odd), pairs))
        targets = jnp.concatenate(
            [jnp.where(parity == 0, got[0], got[1]), jnp.where(parity == 0, got[1], got[0])],
            axis=1,
        ).astype(f32)

    with jax.named_scope("reduce_draft"):
        drafted = reduce_blocks(pieces)

    with jax.named_scope("norm"):
        gain = draft_gain[None, :]
        scaled = gain * drafted
        sums = jnp.stack(
            [
                jnp.sum(drafted * drafted, axis=1),
                jnp.sum(scaled * scaled, axis=1),
                jnp.sum(scaled * targets, axis=1),
            ]
        )
        sums = sums + send(sums, other_core())
        sums = sums + send(sums, along_x(1)) + send(sums, along_x(2)) + send(sums, along_x(3))
        scale = lax.rsqrt(sums[0] / width + epsilon)
        inner = (scale * sums[1] - sums[2]) / slots_all
        error = gain * (scaled * scale[:, None] - targets) / slots_all
        slope = (scale[:, None] * error - drafted * (scale**3 * inner / width)[:, None]).astype(
            bf16
        )

    with jax.named_scope("gather_slope"):
        ring = jnp.concatenate(gather_ring(slope, along_second))
        slopes = jnp.concatenate(gather_ring(ring, along_first))

    with jax.named_scope("step"):
        inputs = features.reshape(-1, 3, feature_slice)
        update_step = jnp.einsum("zag,zh->agh", inputs, slopes, preferred_element_type=f32)
        new_weight = (draft_input_weight - step_rate * update_step).astype(bf16)
    return (upper_layer, new_weight)


def solution(mesh):
    return jax.shard_map(
        body,
        mesh=mesh,
        in_specs=(
            P(None, "replica", "tensor"),
            P("tensor", None),
            P("tensor", None),
            P(None, "replica", "tensor"),
            P("replica", "tensor"),
            P("replica", "tensor"),
            P("replica", "tensor"),
            P("replica", "tensor"),
            P("replica", "tensor"),
            P("replica"),
            P(None, "tensor", "replica"),
            P("replica"),
        ),
        out_specs=(P(None, "replica", "tensor"), P(None, "tensor", "replica")),
        check_vma=False,
    )
```

```python
import functools

import jax
import jax.numpy as jnp
from jax import lax
from jax.experimental import pallas as pl
from jax.experimental.pallas import tpu as pltpu
from jax.sharding import PartitionSpec as P

step_rate = 8.0
epsilon = 1e-06
side = 4
cores = 2
block_units = 32
f32 = jnp.float32
bf16 = jnp.bfloat16
mesh_axes = ("replica", "tensor")
vmem = 56 * 1024 * 1024


def coordinates(device):
    replica, tensor = divmod(device, side * side)
    x, c = divmod(replica, cores)
    z, y = divmod(tensor, side)
    return x, c, z, y


def device_at(x, c, z, y):
    return ((x % side) * cores + c % cores) * side * side + (z % side) * side + y % side


def moved(target):
    return [(d, target(*coordinates(d))) for d in range(side * cores * side * side)]


def along_first(shift):
    return moved(
        lambda x, c, z, y: device_at(x, c, z + shift * (c == 0), y + shift * (c == 1))
    )


def along_second(shift):
    return moved(
        lambda x, c, z, y: device_at(x, c, z + shift * (c == 1), y + shift * (c == 0))
    )


def along_x(shift):
    return moved(lambda x, c, z, y: device_at(x + shift, c, z, y))


def other_core():
    return moved(lambda x, c, z, y: device_at(x, 1 - c, z, y))


def send(array, pairs):
    return lax.ppermute(array, mesh_axes, pairs)


def plus(*terms):
    return functools.reduce(jnp.add, [term.astype(f32) for term in terms])


def other_core_rows():
    return moved(lambda x, c, z, y: device_at(x, 1 - c, y, z))


def row_block(c, tensor):
    z, y = tensor // side, tensor % side
    return z * side + y if c == 0 else y * side + z


def turned(pieces, places):
    for bit in (1, 2):
        moves = places // bit % 2 == 1
        pieces = [
            jnp.where(moves, pieces[(j - bit) % side], pieces[j]) for j in range(side)
        ]
    return pieces


def place():
    replica, tensor = lax.axis_index("replica"), lax.axis_index("tensor")
    x, c = replica // cores, replica % cores
    z, y = tensor // side, tensor % side
    return x, c, jnp.where(c == 0, z, y), jnp.where(c == 0, y, z)


def down_kernel(block_ref, tokens_ref, coded_ref, exponent_ref, *pieces):
    i = pl.program_id(0)
    units, columns = coded_ref.shape
    factor = jnp.exp2(exponent_ref[...].astype(f32) - 127.0).astype(bf16)
    weight = coded_ref[...].reshape(units // block_units, block_units, columns)
    weight = (weight * factor[:, None, :]).reshape(units, columns)
    total = jnp.dot(tokens_ref[...], weight, preferred_element_type=f32)
    for k in range(len(pieces)):

        @pl.when(i // 2 == k)
        def _():
            pieces[k][0] = total.astype(pieces[k].dtype)


def down_pieces(blocks, tokens, coded_weight, block_exponent, kind):
    rows, units = tokens.shape
    width = coded_weight.shape[1] // (side * side)
    count = blocks.shape[0]

    def piece(k):
        return pl.BlockSpec(
            (1, rows, width), lambda i, blocks: (jnp.clip(i - 2 * k, 0, 1), 0, 0)
        )

    return pl.pallas_call(
        down_kernel,
        grid_spec=pltpu.PrefetchScalarGridSpec(
            num_scalar_prefetch=1,
            grid=(count,),
            in_specs=[
                pl.BlockSpec((rows, units), lambda i, blocks: (0, 0)),
                pl.BlockSpec((units, width), lambda i, blocks: (0, blocks[i])),
                pl.BlockSpec((units // block_units, width), lambda i, blocks: (0, blocks[i])),
            ],
            out_specs=[piece(k) for k in range(count // 2)],
        ),
        out_shape=[jax.ShapeDtypeStruct((2, rows, width), kind)] * (count // 2),
        compiler_params=pltpu.CompilerParams(vmem_limit_bytes=vmem),
        cost_estimate=pl.CostEstimate(
            flops=2 * rows * units * width * count,
            bytes_accessed=3 * units * width * count,
            transcendentals=0,
        ),
        name="down_projection",
    )(blocks, tokens, coded_weight, block_exponent)


def reduce_blocks(near, direct, own, q):
    low_right = send(near[0], along_first(1))
    high_left = send(near[1], along_first(-1))
    high_right = send(direct[1], along_first(1))
    low_left = send(direct[2], along_first(-1))
    low_right = send(plus(direct[0], low_right).astype(bf16), along_first(1))
    high_left = send(plus(direct[3], high_left).astype(bf16), along_first(-1))
    summed = jnp.concatenate(
        [plus(own[0], low_right, low_left), plus(own[1], high_left, high_right)]
    )
    halved = summed.astype(bf16)

    def at(array, shift):
        return lax.dynamic_index_in_dim(array, (q + shift) % side, 0, keepdims=False)

    parts = [send(at(halved, shift), along_second(shift)) for shift in (1, 3, 2)]
    return plus(at(summed, 0), *parts)


def body(
    gated_hidden,
    coded_weight,
    block_exponent,
    stream_input,
    lower_layer,
    middle_layer,
    prior_lower,
    prior_middle,
    prior_upper,
    accepted,
    draft_input_weight,
    draft_gain,
):
    steps, rows, unit_count = gated_hidden.shape
    feature_slice = stream_input.shape[2]
    out_slice = draft_input_weight.shape[2]
    replicas = lax.axis_size("replica")
    tensors = lax.axis_size("tensor")
    width = feature_slice * tensors
    slots_all = steps * rows * replicas
    slots = rows * 3 // 4
    x, c, p, q = place()

    with jax.named_scope("down"):
        tokens = gated_hidden.reshape(steps * rows, unit_count)
        second = jnp.arange(side, dtype=jnp.int32)

        def columns(shift):
            first = (p + shift) % side
            return jnp.where(c == 0, first * side + second, second * side + first)

        near = down_pieces(columns(2), tokens, coded_weight, block_exponent, bf16)
        near, accepted = lax.optimization_barrier((near, accepted))

    with jax.named_scope("select"):
        row = jnp.arange(rows, dtype=jnp.int32)
        before = row[:, None] <= row[None, :]
        first_live = (accepted >= 1).astype(jnp.int32)
        second_live = (accepted >= 2).astype(jnp.int32)
        first_slot = jnp.sum(jnp.where(before, first_live[:, None], 0), axis=0) - 1
        second_slot = 2 * slots - jnp.sum(jnp.where(before, second_live[:, None], 0), axis=0)
        first_slot = jnp.where(first_live == 1, first_slot, -1)
        second_slot = jnp.where(second_live == 1, second_slot, -1)
        slot = jnp.arange(2 * slots, dtype=jnp.int32)[:, None]
        select = (slot == jnp.concatenate([first_slot, second_slot])[None, :]).astype(bf16)

        def pick(chosen, first, second):
            return jnp.dot(
                chosen, jnp.concatenate([first, second]), preferred_element_type=f32
            ).astype(bf16)

        pair = pick(
            select,
            jnp.concatenate([prior_lower, prior_middle], axis=1),
            jnp.concatenate([lower_layer, middle_layer], axis=1),
        )
        front = jnp.dot(
            select[:slots, :rows], prior_upper, preferred_element_type=f32
        ).astype(bf16)
        folded = jnp.concatenate([front[: slots // 2], front[slots // 2 :]], axis=1)
        payload = jnp.concatenate([pair, folded])
    gathered = lax.all_gather(payload, "replica", axis=0, tiled=True)

    with jax.named_scope("down"):
        others, payload = lax.optimization_barrier(
            (jnp.concatenate([columns(1), columns(3)]), payload)
        )
        direct = down_pieces(others, tokens, coded_weight, block_exponent, bf16)
        direct, draft_weight = lax.optimization_barrier((direct, draft_input_weight))
        rounded = draft_weight.astype(bf16)
        mine, rounded = lax.optimization_barrier((columns(0), rounded))
        own = down_pieces(mine, tokens, coded_weight, block_exponent, f32)

    with jax.named_scope("reduce_down"):
        summed = reduce_blocks(near, direct, own, q)
    upper_layer = (
        stream_input.astype(f32) + summed.reshape(steps, rows, feature_slice)
    ).astype(bf16)

    with jax.named_scope("back"):
        back = pick(select[slots:], prior_upper, upper_layer[0])
        chips = [back] + [send(back, along_x(-shift)) for shift in (1, 2, 3)]
        chips = jnp.stack(turned(chips, x))
        others = send(chips, other_core())
        backs = jnp.stack(
            [jnp.where(c == 0, chips, others), jnp.where(c == 0, others, chips)], axis=1
        ).reshape(replicas, slots, feature_slice)

    with jax.named_scope("targets"):
        chosen = pick(select, upper_layer[0], upper_layer[1])
        parity = lax.axis_index("tensor") % 2
        even, odd = chosen[:slots], chosen[slots:]
        got = []
        for turn in range(2):
            routes = []
            for d in range(replicas * tensors):
                r, t = divmod(d, tensors)
                owner = t // 2
                taken = row_block(owner % cores, 2 * r + (t + turn) % 2)
                routes.append((d, owner * tensors + taken))
            got.append(send(jnp.where((parity + turn) % 2 == 0, even, odd), routes))

    with jax.named_scope("early"):
        gathered, upper_layer = lax.optimization_barrier((gathered, upper_layer))
        early = jnp.dot(
            gathered,
            rounded[:2].reshape(2 * feature_slice, out_slice),
            preferred_element_type=f32,
        )
        gathered = gathered.reshape(replicas, -1, 2 * feature_slice)
        stride = gathered.shape[1]
        pairs, fronts = gathered[:, : 2 * slots], gathered[:, 2 * slots :]
        fronts = jnp.concatenate(
            [fronts[:, :, :feature_slice], fronts[:, :, feature_slice:]], axis=1
        )

    with jax.named_scope("late"):
        backs, got, early = lax.optimization_barrier((backs, got, early))
        thirds = jnp.concatenate([fronts, backs], axis=1).reshape(-1, feature_slice)

        def drafted_piece(third_weight, shift, half, kind):
            replica = 2 * ((p + shift) % side) + half
            total = lax.dynamic_slice_in_dim(early, replica * stride, 2 * slots, axis=0) + jnp.dot(
                lax.dynamic_slice_in_dim(thirds, replica * 2 * slots, 2 * slots, axis=0),
                third_weight,
                preferred_element_type=f32,
            )
            return total.astype(kind).reshape(2, slots, out_slice)

        third_weight = rounded[2]
        near = [drafted_piece(third_weight, 2, half, bf16) for half in range(2)]
        near, third_weight = lax.optimization_barrier((near, third_weight))
        direct = [
            drafted_piece(third_weight, shift, half, bf16) for shift in (1, 3) for half in range(2)
        ]
        direct, third_weight = lax.optimization_barrier((direct, third_weight))
        own = [drafted_piece(third_weight, 0, half, f32) for half in range(2)]

    with jax.named_scope("reduce_draft"):
        drafted = reduce_blocks(near, direct, own, q)

    with jax.named_scope("norm"):
        front_rows = q % 2 == 0
        targets = jnp.concatenate(
            [jnp.where(front_rows, got[0], got[1]), jnp.where(front_rows, got[1], got[0])],
            axis=1,
        ).astype(f32)
        gain = draft_gain[None, :]
        scaled = gain * drafted
        sums = jnp.stack(
            [
                jnp.sum(drafted * drafted, axis=1),
                jnp.sum(scaled * scaled, axis=1),
                jnp.sum(scaled * targets, axis=1),
            ]
        )
        sums = sums + send(sums, other_core_rows())
        sums = sums + send(sums, along_x(1)) + send(sums, along_x(2)) + send(sums, along_x(3))
        scale = lax.rsqrt(sums[0] / width + epsilon)
        inner = (scale * sums[1] - sums[2]) / slots_all
        error = gain * (scaled * scale[:, None] - targets) / slots_all
        slope = (scale[:, None] * error - drafted * (scale**3 * inner / width)[:, None]).astype(
            bf16
        )

    with jax.named_scope("gather_slope"):
        ring = [slope] + [send(slope, along_second(-shift)) for shift in (1, 2, 3)]
        ring = jnp.concatenate(turned(ring, q))
        previous = send(ring, along_first(1))
        following = send(ring, along_first(-1))
        previous, following, low, high = lax.optimization_barrier(
            (previous, following, previous[: 2 * slots], following[2 * slots :])
        )
        low = send(low, along_first(1))
        high = send(high, along_first(-1))

    with jax.named_scope("step"):
        features = jnp.concatenate([pairs.reshape(-1, 2 * feature_slice), thirds], axis=1)

        def product(shift, slopes):
            start = (p + shift) % side * side * slots
            inputs = lax.dynamic_slice_in_dim(features, start, side * slots, axis=0)
            return lax.dot_general(
                inputs, slopes, (((0,), (0,)), ((), ())), preferred_element_type=f32
            )

        total = lax.optimization_barrier(product(0, ring))
        total = lax.optimization_barrier(total + product(1, following))
        total = lax.optimization_barrier(total + product(3, previous))
        total = total + product(2, jnp.concatenate([low, high]))
        new_weight = (draft_input_weight.reshape(total.shape) - step_rate * total).astype(bf16)
        new_weight = new_weight.reshape(draft_input_weight.shape)
    return (upper_layer, new_weight)


def solution(mesh):
    return jax.shard_map(
        body,
        mesh=mesh,
        in_specs=(
            P(None, "replica", "tensor"),
            P("tensor", None),
            P("tensor", None),
            P(None, "replica", "tensor"),
            P("replica", "tensor"),
            P("replica", "tensor"),
            P("replica", "tensor"),
            P("replica", "tensor"),
            P("replica", "tensor"),
            P("replica"),
            P(None, "tensor", "replica"),
            P("replica"),
        ),
        out_specs=(P(None, "replica", "tensor"), P(None, "tensor", "replica")),
        check_vma=False,
    )
```

```python
import functools

import jax
import jax.numpy as jnp
from jax import lax
from jax.experimental import pallas as pl
from jax.experimental.pallas import tpu as pltpu
from jax.sharding import PartitionSpec as P

step_rate = 8.0
epsilon = 1e-06
side = 4
cores = 2
block_units = 32
f32 = jnp.float32
bf16 = jnp.bfloat16
mesh_axes = ("replica", "tensor")
vmem = 40 * 1024 * 1024
ahead = 4


def coordinates(device):
    replica, tensor = divmod(device, side * side)
    x, c = divmod(replica, cores)
    z, y = divmod(tensor, side)
    return x, c, z, y


def device_at(x, c, z, y):
    return ((x % side) * cores + c % cores) * side * side + (z % side) * side + y % side


def moved(target):
    return [(d, target(*coordinates(d))) for d in range(side * cores * side * side)]


def along_first(shift):
    return moved(
        lambda x, c, z, y: device_at(x, c, z + shift * (c == 0), y + shift * (c == 1))
    )


def along_second(shift):
    return moved(
        lambda x, c, z, y: device_at(x, c, z + shift * (c == 1), y + shift * (c == 0))
    )


def along_x(shift):
    return moved(lambda x, c, z, y: device_at(x + shift, c, z, y))


def other_core():
    return moved(lambda x, c, z, y: device_at(x, 1 - c, z, y))


def send(array, pairs):
    return lax.ppermute(array, mesh_axes, pairs)


def plus(*terms):
    return functools.reduce(jnp.add, [term.astype(f32) for term in terms])


def other_core_rows():
    return moved(lambda x, c, z, y: device_at(x, 1 - c, y, z))


def row_block(c, tensor):
    z, y = tensor // side, tensor % side
    return z * side + y if c == 0 else y * side + z


def turned(pieces, places):
    for bit in (1, 2):
        moves = places // bit % 2 == 1
        pieces = [
            jnp.where(moves, pieces[(j - bit) % side], pieces[j]) for j in range(side)
        ]
    return pieces


def place():
    replica, tensor = lax.axis_index("replica"), lax.axis_index("tensor")
    x, c = replica // cores, replica % cores
    z, y = tensor // side, tensor % side
    return x, c, jnp.where(c == 0, z, y), jnp.where(c == 0, y, z)


def down_kernel(
    count, blocks_ref, tokens_ref, coded_ref, exponent_ref, *refs
):
    pieces, (coded, exponent, coded_sem, exponent_sem) = refs[: count // 2], refs[count // 2 :]
    _, units, columns = coded.shape

    def copies(i):
        start = pl.multiple_of(blocks_ref[i] * columns, columns)
        taken = (slice(None), pl.ds(start, columns))
        return (
            pltpu.make_async_copy(coded_ref.at[taken], coded.at[i], coded_sem.at[i]),
            pltpu.make_async_copy(exponent_ref.at[taken], exponent.at[i], exponent_sem.at[i]),
        )

    for i in range(min(ahead, count)):
        for copy in copies(i):
            copy.start()
    for i in range(count):
        for copy in copies(i):
            copy.wait()
        if i + ahead < count:
            for copy in copies(i + ahead):
                copy.start()
        factor = jnp.exp2(exponent[i].astype(f32) - 127.0).astype(bf16)
        weight = coded[i].reshape(units // block_units, block_units, columns)
        weight = (weight * factor[:, None, :]).reshape(units, columns)
        total = jnp.dot(tokens_ref[...], weight, preferred_element_type=f32)
        pieces[i // 2][i % 2] = total.astype(pieces[i // 2].dtype)


def down_pieces(blocks, tokens, coded_weight, block_exponent, kind):
    rows, units = tokens.shape
    width = coded_weight.shape[1] // (side * side)
    count = blocks.shape[0]
    anywhere = pl.BlockSpec(memory_space=pl.ANY)
    return pl.pallas_call(
        functools.partial(down_kernel, count),
        in_specs=[
            pl.BlockSpec(memory_space=pltpu.SMEM),
            pl.BlockSpec(memory_space=pltpu.VMEM),
            anywhere,
            anywhere,
        ],
        out_specs=[pl.BlockSpec(memory_space=pltpu.VMEM)] * (count // 2),
        out_shape=[jax.ShapeDtypeStruct((2, rows, width), kind)] * (count // 2),
        scratch_shapes=[
            pltpu.VMEM((count, units, width), bf16),
            pltpu.VMEM((count, units // block_units, width), jnp.int32),
            pltpu.SemaphoreType.DMA((count,)),
            pltpu.SemaphoreType.DMA((count,)),
        ],
        compiler_params=pltpu.CompilerParams(vmem_limit_bytes=vmem),
        cost_estimate=pl.CostEstimate(
            flops=2 * rows * units * width * count,
            bytes_accessed=3 * units * width * count,
            transcendentals=0,
        ),
        name="down_projection",
    )(blocks, tokens, coded_weight, block_exponent)


def reduce_blocks(near, direct, own, q):
    low_right = send(near[0], along_first(1))
    high_left = send(near[1], along_first(-1))
    high_right = send(direct[1], along_first(1))
    low_left = send(direct[2], along_first(-1))
    low_right = send(plus(direct[0], low_right).astype(bf16), along_first(1))
    high_left = send(plus(direct[3], high_left).astype(bf16), along_first(-1))
    summed = jnp.concatenate(
        [plus(own[0], low_right, low_left), plus(own[1], high_left, high_right)]
    )
    halved = summed.astype(bf16)

    def at(array, shift):
        return lax.dynamic_index_in_dim(array, (q + shift) % side, 0, keepdims=False)

    parts = [send(at(halved, shift), along_second(shift)) for shift in (1, 3, 2)]
    return plus(at(summed, 0), *parts), summed


def body(
    gated_hidden,
    coded_weight,
    block_exponent,
    stream_input,
    lower_layer,
    middle_layer,
    prior_lower,
    prior_middle,
    prior_upper,
    accepted,
    draft_input_weight,
    draft_gain,
):
    steps, rows, unit_count = gated_hidden.shape
    feature_slice = stream_input.shape[2]
    out_slice = draft_input_weight.shape[2]
    replicas = lax.axis_size("replica")
    tensors = lax.axis_size("tensor")
    width = feature_slice * tensors
    slots_all = steps * rows * replicas
    slots = rows * 3 // 4
    x, c, p, q = place()

    with jax.named_scope("down"):
        tokens = gated_hidden.reshape(steps * rows, unit_count)
        second = jnp.arange(side, dtype=jnp.int32)

        def columns(shift):
            first = (p + shift) % side
            return jnp.where(c == 0, first * side + second, second * side + first)

        near = down_pieces(columns(2), tokens, coded_weight, block_exponent, bf16)
        near, accepted = lax.optimization_barrier((near, accepted))

    with jax.named_scope("select"):
        row = jnp.arange(rows, dtype=jnp.int32)
        before = row[:, None] <= row[None, :]
        first_live = (accepted >= 1).astype(jnp.int32)
        second_live = (accepted >= 2).astype(jnp.int32)
        first_slot = jnp.sum(jnp.where(before, first_live[:, None], 0), axis=0) - 1
        second_slot = 2 * slots - jnp.sum(jnp.where(before, second_live[:, None], 0), axis=0)
        first_slot = jnp.where(first_live == 1, first_slot, -1)
        second_slot = jnp.where(second_live == 1, second_slot, -1)
        slot = jnp.arange(2 * slots, dtype=jnp.int32)[:, None]
        select = (slot == jnp.concatenate([first_slot, second_slot])[None, :]).astype(bf16)

        def pick(chosen, first, second):
            return jnp.dot(
                chosen, jnp.concatenate([first, second]), preferred_element_type=f32
            ).astype(bf16)

        pair = pick(
            select,
            jnp.concatenate([prior_lower, prior_middle], axis=1),
            jnp.concatenate([lower_layer, middle_layer], axis=1),
        )
        front = jnp.dot(
            select[:slots, :rows], prior_upper, preferred_element_type=f32
        ).astype(bf16)
        folded = jnp.concatenate([front[: slots // 2], front[slots // 2 :]], axis=1)
        payload = jnp.concatenate([pair, folded])
    gathered = lax.all_gather(payload, "replica", axis=0, tiled=True)

    with jax.named_scope("down"):
        others, payload = lax.optimization_barrier(
            (jnp.concatenate([columns(1), columns(3)]), payload)
        )
        direct = down_pieces(others, tokens, coded_weight, block_exponent, bf16)
        direct, mine = lax.optimization_barrier((direct, columns(0)))
        own = down_pieces(mine, tokens, coded_weight, block_exponent, f32)

    with jax.named_scope("reduce_down"):
        mixed, first_sum = reduce_blocks(near, direct, own, q)
    first_sum, draft_weight = lax.optimization_barrier((first_sum, draft_input_weight))
    rounded = draft_weight.astype(bf16)
    mixed, rounded = lax.optimization_barrier((mixed, rounded))
    upper_layer = (
        stream_input.astype(f32) + mixed.reshape(steps, rows, feature_slice)
    ).astype(bf16)

    with jax.named_scope("back"):
        back = pick(select[slots:], prior_upper, upper_layer[0])
        chosen = pick(select, upper_layer[0], upper_layer[1])
        parity = lax.axis_index("tensor") % 2
        even, odd = chosen[:slots], chosen[slots:]
        posted = [
            jnp.where((parity + turn) % 2 == 0, even, odd) for turn in range(2)
        ]
        gathered, _ = lax.optimization_barrier((gathered, (back, posted)))
        chips = [back] + [send(back, along_x(-shift)) for shift in (1, 2, 3)]

    with jax.named_scope("targets"):
        got = []
        for turn in range(2):
            routes = []
            for d in range(replicas * tensors):
                r, t = divmod(d, tensors)
                owner = t // 2
                taken = row_block(owner % cores, 2 * r + (t + turn) % 2)
                routes.append((d, owner * tensors + taken))
            got.append(send(posted[turn], routes))

    with jax.named_scope("early"):
        early = jnp.dot(
            gathered,
            rounded[:2].reshape(2 * feature_slice, out_slice),
            preferred_element_type=f32,
        )
        gathered = gathered.reshape(replicas, -1, 2 * feature_slice)
        stride = gathered.shape[1]
        pairs, fronts = gathered[:, : 2 * slots], gathered[:, 2 * slots :]
        fronts = jnp.concatenate(
            [fronts[:, :, :feature_slice], fronts[:, :, feature_slice:]], axis=1
        )
        fronts, early, chips = lax.optimization_barrier((fronts, early, chips))

    with jax.named_scope("back"):
        chips = jnp.stack(turned(chips, x))
        others = send(chips, other_core())
        backs = jnp.stack(
            [jnp.where(c == 0, chips, others), jnp.where(c == 0, others, chips)], axis=1
        ).reshape(replicas, slots, feature_slice)

    with jax.named_scope("late"):
        backs, got = lax.optimization_barrier((backs, got))
        thirds = jnp.concatenate([fronts, backs], axis=1).reshape(-1, feature_slice)

        def drafted_piece(third_weight, shift, half, kind):
            replica = 2 * ((p + shift) % side) + half
            total = lax.dynamic_slice_in_dim(early, replica * stride, 2 * slots, axis=0) + jnp.dot(
                lax.dynamic_slice_in_dim(thirds, replica * 2 * slots, 2 * slots, axis=0),
                third_weight,
                preferred_element_type=f32,
            )
            return total.astype(kind).reshape(2, slots, out_slice)

        third_weight = rounded[2]
        near = [drafted_piece(third_weight, 2, half, bf16) for half in range(2)]
        near, third_weight = lax.optimization_barrier((near, third_weight))
        direct = [
            drafted_piece(third_weight, shift, half, bf16) for shift in (1, 3) for half in range(2)
        ]
        direct, third_weight = lax.optimization_barrier((direct, third_weight))
        own = [drafted_piece(third_weight, 0, half, f32) for half in range(2)]

    with jax.named_scope("reduce_draft"):
        drafted, _ = reduce_blocks(near, direct, own, q)

    with jax.named_scope("norm"):
        front_rows = q % 2 == 0
        targets = jnp.concatenate(
            [jnp.where(front_rows, got[0], got[1]), jnp.where(front_rows, got[1], got[0])],
            axis=1,
        ).astype(f32)
        gain = draft_gain[None, :]
        scaled = gain * drafted
        sums = jnp.stack(
            [
                jnp.sum(drafted * drafted, axis=1),
                jnp.sum(scaled * scaled, axis=1),
                jnp.sum(scaled * targets, axis=1),
            ]
        )
        sums = sums + send(sums, other_core_rows())
        sums = sums + send(sums, along_x(1)) + send(sums, along_x(2)) + send(sums, along_x(3))
        scale = lax.rsqrt(sums[0] / width + epsilon)
        inner = (scale * sums[1] - sums[2]) / slots_all
        error = gain * (scaled * scale[:, None] - targets) / slots_all
        slope = (scale[:, None] * error - drafted * (scale**3 * inner / width)[:, None]).astype(
            bf16
        )

    with jax.named_scope("gather_slope"):
        ring = [slope] + [send(slope, along_second(-shift)) for shift in (1, 2, 3)]
        ring = jnp.concatenate(turned(ring, q))
        upper_half, lower_half = ring[: 2 * slots], ring[2 * slots :]
        previous_upper = send(upper_half, along_first(1))
        following_lower = send(lower_half, along_first(-1))
        previous_lower = send(lower_half, along_first(1))
        following_upper = send(upper_half, along_first(-1))
        low = send(previous_upper, along_first(1))
        high = send(following_lower, along_first(-1))

    with jax.named_scope("step"):
        features = jnp.concatenate([pairs.reshape(-1, 2 * feature_slice), thirds], axis=1)

        def product(shift, slopes):
            start = (p + shift) % side * side * slots
            inputs = lax.dynamic_slice_in_dim(features, start, side * slots, axis=0)
            return lax.dot_general(
                inputs, slopes, (((0,), (0,)), ((), ())), preferred_element_type=f32
            )

        total = lax.optimization_barrier(product(0, ring))
        following = jnp.concatenate([following_upper, following_lower])
        previous = jnp.concatenate([previous_upper, previous_lower])
        total = lax.optimization_barrier(total + product(1, following))
        total = lax.optimization_barrier(total + product(3, previous))
        total = total + product(2, jnp.concatenate([low, high]))
        new_weight = (draft_input_weight.reshape(total.shape) - step_rate * total).astype(bf16)
        new_weight = new_weight.reshape(draft_input_weight.shape)
    return (upper_layer, new_weight)


def solution(mesh):
    return jax.shard_map(
        body,
        mesh=mesh,
        in_specs=(
            P(None, "replica", "tensor"),
            P("tensor", None),
            P("tensor", None),
            P(None, "replica", "tensor"),
            P("replica", "tensor"),
            P("replica", "tensor"),
            P("replica", "tensor"),
            P("replica", "tensor"),
            P("replica", "tensor"),
            P("replica"),
            P(None, "tensor", "replica"),
            P("replica"),
        ),
        out_specs=(P(None, "replica", "tensor"), P(None, "tensor", "replica")),
        check_vma=False,
    )
```

```python
import functools

import jax
import jax.numpy as jnp
from jax import lax
from jax.experimental import pallas as pl
from jax.experimental.pallas import tpu as pltpu
from jax.sharding import PartitionSpec as P

step_rate = 8.0
epsilon = 1e-06
side = 4
cores = 2
block_units = 32
f32 = jnp.float32
bf16 = jnp.bfloat16
mesh_axes = ("replica", "tensor")
vmem = 24 * 1024 * 1024
ahead = 4


def coordinates(device):
    replica, tensor = divmod(device, side * side)
    x, c = divmod(replica, cores)
    z, y = divmod(tensor, side)
    return x, c, z, y


def device_at(x, c, z, y):
    return ((x % side) * cores + c % cores) * side * side + (z % side) * side + y % side


def moved(target):
    return [(d, target(*coordinates(d))) for d in range(side * cores * side * side)]


def along_first(shift):
    return moved(
        lambda x, c, z, y: device_at(x, c, z + shift * (c == 0), y + shift * (c == 1))
    )


def along_second(shift):
    return moved(
        lambda x, c, z, y: device_at(x, c, z + shift * (c == 1), y + shift * (c == 0))
    )


def along_x(shift):
    return moved(lambda x, c, z, y: device_at(x + shift, c, z, y))


def other_core():
    return moved(lambda x, c, z, y: device_at(x, 1 - c, z, y))


def send(array, pairs):
    return lax.ppermute(array, mesh_axes, pairs)


def plus(*terms):
    return functools.reduce(jnp.add, [term.astype(f32) for term in terms])


def other_replica(chips_on, cores_on):
    return moved(
        lambda x, c, z, y: device_at(x + chips_on, c + cores_on, *((y, z) if cores_on else (z, y)))
    )


def row_block(c, tensor):
    z, y = tensor // side, tensor % side
    return z * side + y if c == 0 else y * side + z


def turned(pieces, places):
    for bit in (1, 2):
        moves = places // bit % 2 == 1
        pieces = [
            jnp.where(moves, pieces[(j - bit) % side], pieces[j]) for j in range(side)
        ]
    return pieces


def place():
    replica, tensor = lax.axis_index("replica"), lax.axis_index("tensor")
    x, c = replica // cores, replica % cores
    z, y = tensor // side, tensor % side
    return x, c, jnp.where(c == 0, z, y), jnp.where(c == 0, y, z)


def down_kernel(
    count, blocks_ref, tokens_ref, coded_ref, exponent_ref, *refs
):
    pieces, (coded, exponent, coded_sem, exponent_sem) = refs[: count // 2], refs[count // 2 :]
    _, units, columns = coded.shape

    def copies(i):
        start = pl.multiple_of(blocks_ref[i] * columns, columns)
        taken = (slice(None), pl.ds(start, columns))
        return (
            pltpu.make_async_copy(coded_ref.at[taken], coded.at[i], coded_sem.at[i]),
            pltpu.make_async_copy(exponent_ref.at[taken], exponent.at[i], exponent_sem.at[i]),
        )

    for i in range(min(ahead, count)):
        for copy in copies(i):
            copy.start()
    for i in range(count):
        for copy in copies(i):
            copy.wait()
        if i + ahead < count:
            for copy in copies(i + ahead):
                copy.start()
        factor = jnp.exp2(exponent[i].astype(f32) - 127.0).astype(bf16)
        weight = coded[i].reshape(units // block_units, block_units, columns)
        weight = (weight * factor[:, None, :]).reshape(units, columns)
        total = jnp.dot(tokens_ref[...], weight, preferred_element_type=f32)
        pieces[i // 2][i % 2] = total.astype(pieces[i // 2].dtype)


def down_pieces(blocks, tokens, coded_weight, block_exponent, kind):
    rows, units = tokens.shape
    width = coded_weight.shape[1] // (side * side)
    count = blocks.shape[0]
    anywhere = pl.BlockSpec(memory_space=pltpu.HBM)
    return pl.pallas_call(
        functools.partial(down_kernel, count),
        in_specs=[
            pl.BlockSpec(memory_space=pltpu.SMEM),
            pl.BlockSpec(memory_space=pltpu.VMEM),
            anywhere,
            anywhere,
        ],
        out_specs=[pl.BlockSpec(memory_space=pltpu.VMEM)] * (count // 2),
        out_shape=[jax.ShapeDtypeStruct((2, rows, width), kind)] * (count // 2),
        scratch_shapes=[
            pltpu.VMEM((count, units, width), bf16),
            pltpu.VMEM((count, units // block_units, width), jnp.int32),
            pltpu.SemaphoreType.DMA((count,)),
            pltpu.SemaphoreType.DMA((count,)),
        ],
        compiler_params=pltpu.CompilerParams(vmem_limit_bytes=vmem),
        cost_estimate=pl.CostEstimate(
            flops=2 * rows * units * width * count,
            bytes_accessed=3 * units * width * count,
            transcendentals=0,
        ),
        name="down_projection",
    )(blocks, tokens, coded_weight, block_exponent)


def reduce_blocks(near, direct, own, q):
    low_right = send(near[0], along_first(1))
    high_left = send(near[1], along_first(-1))
    high_right = send(direct[1], along_first(1))
    low_left = send(direct[2], along_first(-1))
    low_right = send(plus(direct[0], low_right).astype(bf16), along_first(1))
    high_left = send(plus(direct[3], high_left).astype(bf16), along_first(-1))
    summed = jnp.concatenate(
        [plus(own[0], low_right, low_left), plus(own[1], high_left, high_right)]
    )
    halved = summed.astype(bf16)

    def at(array, shift):
        return lax.dynamic_index_in_dim(array, (q + shift) % side, 0, keepdims=False)

    parts = [send(at(halved, shift), along_second(shift)) for shift in (1, 3, 2)]
    return plus(at(summed, 0), *parts), summed


def body(
    gated_hidden,
    coded_weight,
    block_exponent,
    stream_input,
    lower_layer,
    middle_layer,
    prior_lower,
    prior_middle,
    prior_upper,
    accepted,
    draft_input_weight,
    draft_gain,
):
    steps, rows, unit_count = gated_hidden.shape
    feature_slice = stream_input.shape[2]
    out_slice = draft_input_weight.shape[2]
    replicas = lax.axis_size("replica")
    tensors = lax.axis_size("tensor")
    width = feature_slice * tensors
    slots_all = steps * rows * replicas
    slots = rows * 3 // 4
    x, c, p, q = place()

    with jax.named_scope("down"):
        tokens = gated_hidden.reshape(steps * rows, unit_count)
        second = jnp.arange(side, dtype=jnp.int32)

        def columns(shift):
            first = (p + shift) % side
            return jnp.where(c == 0, first * side + second, second * side + first)

        near = down_pieces(columns(2), tokens, coded_weight, block_exponent, bf16)
        near, accepted = lax.optimization_barrier((near, accepted))

    with jax.named_scope("select"):
        row = jnp.arange(rows, dtype=jnp.int32)
        before = row[:, None] <= row[None, :]
        first_live = (accepted >= 1).astype(jnp.int32)
        second_live = (accepted >= 2).astype(jnp.int32)
        first_slot = jnp.sum(jnp.where(before, first_live[:, None], 0), axis=0) - 1
        second_slot = 2 * slots - jnp.sum(jnp.where(before, second_live[:, None], 0), axis=0)
        first_slot = jnp.where(first_live == 1, first_slot, -1)
        second_slot = jnp.where(second_live == 1, second_slot, -1)
        slot = jnp.arange(2 * slots, dtype=jnp.int32)[:, None]
        select = (slot == jnp.concatenate([first_slot, second_slot])[None, :]).astype(bf16)

        def pick(chosen, first, second):
            return jnp.dot(
                chosen, jnp.concatenate([first, second]), preferred_element_type=f32
            ).astype(bf16)

        pair = pick(
            select,
            jnp.concatenate([prior_lower, prior_middle], axis=1),
            jnp.concatenate([lower_layer, middle_layer], axis=1),
        )
        front = jnp.dot(
            select[:slots, :rows], prior_upper, preferred_element_type=f32
        ).astype(bf16)
        folded = jnp.concatenate([front[: slots // 2], front[slots // 2 :]], axis=1)
        payload = jnp.concatenate([pair, folded])
    gathered = lax.all_gather(payload, "replica", axis=0, tiled=True)

    with jax.named_scope("down"):
        others, payload = lax.optimization_barrier(
            (jnp.concatenate([columns(1), columns(3)]), payload)
        )
        direct = down_pieces(others, tokens, coded_weight, block_exponent, bf16)
        direct, mine = lax.optimization_barrier((direct, columns(0)))
        own = down_pieces(mine, tokens, coded_weight, block_exponent, f32)

    with jax.named_scope("reduce_down"):
        mixed, first_sum = reduce_blocks(near, direct, own, q)
    first_sum, draft_weight = lax.optimization_barrier((first_sum, draft_input_weight))
    rounded = draft_weight.astype(bf16)
    mixed, rounded = lax.optimization_barrier((mixed, rounded))
    upper_layer = (
        stream_input.astype(f32) + mixed.reshape(steps, rows, feature_slice)
    ).astype(bf16)

    with jax.named_scope("back"):
        back = pick(select[slots:], prior_upper, upper_layer[0])
        chosen = pick(select, upper_layer[0], upper_layer[1])
        parity = lax.axis_index("tensor") % 2
        even, odd = chosen[:slots], chosen[slots:]
        posted = [
            jnp.where((parity + turn) % 2 == 0, even, odd) for turn in range(2)
        ]
        gathered, _ = lax.optimization_barrier((gathered, (back, posted)))
        chips = [back] + [send(back, along_x(-shift)) for shift in (1, 2, 3)]

    with jax.named_scope("targets"):
        got = []
        for turn in range(2):
            routes = []
            for d in range(replicas * tensors):
                r, t = divmod(d, tensors)
                owner = t // 2
                taken = row_block(owner % cores, 2 * r + (t + turn) % 2)
                routes.append((d, owner * tensors + taken))
            got.append(send(posted[turn], routes))

    with jax.named_scope("back"):
        chips = jnp.stack(turned(chips, x))
        others = send(chips, other_core())
        backs = jnp.stack(
            [jnp.where(c == 0, chips, others), jnp.where(c == 0, others, chips)], axis=1
        ).reshape(replicas, slots, feature_slice)

    with jax.named_scope("forward"):
        pair_weight = rounded[:2].reshape(2 * feature_slice, out_slice)
        third_weight = rounded[2]
        by_replica = gathered.reshape(replicas, -1, 2 * feature_slice)
        stride = by_replica.shape[1]
        pairs, fronts = by_replica[:, : 2 * slots], by_replica[:, 2 * slots :]
        thirds = jnp.concatenate(
            [fronts[:, :, :feature_slice], fronts[:, :, feature_slice:], backs], axis=1
        ).reshape(-1, feature_slice)

        def drafted_piece(weights, shift, half, kind):
            replica = 2 * ((p + shift) % side) + half
            total = jnp.dot(
                lax.dynamic_slice_in_dim(gathered, replica * stride, 2 * slots, axis=0),
                weights[0],
                preferred_element_type=f32,
            ) + jnp.dot(
                lax.dynamic_slice_in_dim(thirds, replica * 2 * slots, 2 * slots, axis=0),
                weights[1],
                preferred_element_type=f32,
            )
            return total.astype(kind).reshape(2, slots, out_slice)

        weights = (pair_weight, third_weight)
        near = [drafted_piece(weights, 2, half, bf16) for half in range(2)]
        _, got, weights = lax.optimization_barrier((near, got, weights))
        direct = [
            drafted_piece(weights, shift, half, bf16) for shift in (1, 3) for half in range(2)
        ]
        _, weights = lax.optimization_barrier((direct, weights))
        own = [drafted_piece(weights, 0, half, f32) for half in range(2)]

    with jax.named_scope("reduce_draft"):
        drafted, _ = reduce_blocks(near, direct, own, q)

    with jax.named_scope("norm"):
        front_rows = q % 2 == 0
        targets = jnp.concatenate(
            [jnp.where(front_rows, got[0], got[1]), jnp.where(front_rows, got[1], got[0])],
            axis=1,
        ).astype(f32)
        gain = draft_gain[None, :]
        scaled = gain * drafted
        sums = jnp.stack(
            [
                jnp.sum(drafted * drafted, axis=1),
                jnp.sum(scaled * scaled, axis=1),
                jnp.sum(scaled * targets, axis=1),
            ]
        )
        sums = plus(
            sums,
            *[
                send(sums, other_replica(chips_on, cores_on))
                for cores_on in range(cores)
                for chips_on in range(side)
                if cores_on or chips_on
            ],
        )
        scale = lax.rsqrt(sums[0] / width + epsilon)
        inner = (scale * sums[1] - sums[2]) / slots_all
        error = gain * (scaled * scale[:, None] - targets) / slots_all
        slope = (scale[:, None] * error - drafted * (scale**3 * inner / width)[:, None]).astype(
            bf16
        )

    with jax.named_scope("gather_slope"):
        ring = [slope] + [send(slope, along_second(-shift)) for shift in (1, 2, 3)]
        ring = turned(ring, q)
        upper_half, lower_half = jnp.concatenate(ring[:2]), jnp.concatenate(ring[2:])
        previous_upper = send(upper_half, along_first(1))
        following_lower = send(lower_half, along_first(-1))
        previous_lower = send(lower_half, along_first(1))
        following_upper = send(upper_half, along_first(-1))
        low = send(previous_upper, along_first(1))
        high = send(following_lower, along_first(-1))

    with jax.named_scope("step"):
        features = jnp.concatenate([pairs.reshape(-1, 2 * feature_slice), thirds], axis=1)

        def product(places, slopes):
            inputs = [
                lax.dynamic_slice_in_dim(
                    features, (2 * ((p + shift) % side) + half) * 2 * slots, 2 * slots, axis=0
                )
                for shift, half in places
            ]
            return lax.dot_general(
                jnp.concatenate(inputs),
                jnp.concatenate(slopes),
                (((0,), (0,)), ((), ())),
                preferred_element_type=f32,
            )

        upper_half, lower_half, previous_upper, following_lower = lax.optimization_barrier(
            (upper_half, lower_half, previous_upper, following_lower)
        )
        total = product([(0, 0), (0, 1)], [upper_half, lower_half])
        total = lax.optimization_barrier(
            total + product([(3, 0), (1, 1)], [previous_upper, following_lower])
        )
        total = lax.optimization_barrier(
            total + product([(3, 1), (1, 0)], [previous_lower, following_upper])
        )
        total = total + product([(2, 0), (2, 1)], [low, high])
        new_weight = (draft_input_weight.reshape(total.shape) - step_rate * total).astype(bf16)
        new_weight = new_weight.reshape(draft_input_weight.shape)
    return (upper_layer, new_weight)


def solution(mesh):
    return jax.shard_map(
        body,
        mesh=mesh,
        in_specs=(
            P(None, "replica", "tensor"),
            P("tensor", None),
            P("tensor", None),
            P(None, "replica", "tensor"),
            P("replica", "tensor"),
            P("replica", "tensor"),
            P("replica", "tensor"),
            P("replica", "tensor"),
            P("replica", "tensor"),
            P("replica"),
            P(None, "tensor", "replica"),
            P("replica"),
        ),
        out_specs=(P(None, "replica", "tensor"), P(None, "tensor", "replica")),
        check_vma=False,
    )
```

```python
import functools

import jax
import jax.numpy as jnp
from jax import lax
from jax.experimental import pallas as pl
from jax.experimental.pallas import tpu as pltpu
from jax.sharding import PartitionSpec as P

step_rate = 8.0
epsilon = 1e-06
side = 4
cores = 2
block_units = 32
f32 = jnp.float32
bf16 = jnp.bfloat16
mesh_axes = ("replica", "tensor")
vmem = 56 * 1024 * 1024
ahead = 4


def coordinates(device):
    replica, tensor = divmod(device, side * side)
    x, c = divmod(replica, cores)
    z, y = divmod(tensor, side)
    return x, c, z, y


def device_at(x, c, z, y):
    return ((x % side) * cores + c % cores) * side * side + (z % side) * side + y % side


def moved(target):
    return [(d, target(*coordinates(d))) for d in range(side * cores * side * side)]


def along_first(shift):
    return moved(
        lambda x, c, z, y: device_at(x, c, z + shift * (c == 0), y + shift * (c == 1))
    )


def along_second(shift):
    return moved(
        lambda x, c, z, y: device_at(x, c, z + shift * (c == 1), y + shift * (c == 0))
    )


def along_x(shift):
    return moved(lambda x, c, z, y: device_at(x + shift, c, z, y))


def other_core():
    return moved(lambda x, c, z, y: device_at(x, 1 - c, z, y))


def send(array, pairs):
    return lax.ppermute(array, mesh_axes, pairs)


def plus(*terms):
    return functools.reduce(jnp.add, [term.astype(f32) for term in terms])


def other_core_rows():
    return moved(lambda x, c, z, y: device_at(x, 1 - c, y, z))


def row_block(c, tensor):
    z, y = tensor // side, tensor % side
    return z * side + y if c == 0 else y * side + z


def turned(pieces, places):
    for bit in (1, 2):
        moves = places // bit % 2 == 1
        pieces = [
            jnp.where(moves, pieces[(j - bit) % side], pieces[j]) for j in range(side)
        ]
    return pieces


def place():
    replica, tensor = lax.axis_index("replica"), lax.axis_index("tensor")
    x, c = replica // cores, replica % cores
    z, y = tensor // side, tensor % side
    return x, c, jnp.where(c == 0, z, y), jnp.where(c == 0, y, z)


def down_kernel(
    count, blocks_ref, tokens_ref, coded_ref, exponent_ref, *refs
):
    pieces, (coded, exponent, coded_sem, exponent_sem) = refs[:count], refs[count:]
    _, units, columns = coded.shape
    rows = pieces[0].shape[1]

    def copies(i):
        start = pl.multiple_of(blocks_ref[i] * columns, columns)
        taken = (slice(None), pl.ds(start, columns))
        return (
            pltpu.make_async_copy(coded_ref.at[taken], coded.at[i], coded_sem.at[i]),
            pltpu.make_async_copy(exponent_ref.at[taken], exponent.at[i], exponent_sem.at[i]),
        )

    for i in range(min(ahead, count)):
        for copy in copies(i):
            copy.start()
    for i in range(count):
        for copy in copies(i):
            copy.wait()
        if i + ahead < count:
            for copy in copies(i + ahead):
                copy.start()
        factor = jnp.exp2(exponent[i].astype(f32) - 127.0).astype(bf16)
        weight = coded[i].reshape(units // block_units, block_units, columns)
        weight = (weight * factor[:, None, :]).reshape(units, columns)
        total = jnp.dot(tokens_ref[...], weight, preferred_element_type=f32)
        for position in range(2):
            piece = pieces[i // 2 * 2 + position]
            piece[i % 2] = total[position * rows : (position + 1) * rows].astype(piece.dtype)


def down_pieces(blocks, tokens, coded_weight, block_exponent, kind):
    rows, units = tokens.shape
    width = coded_weight.shape[1] // (side * side)
    count = blocks.shape[0]
    anywhere = pl.BlockSpec(memory_space=pl.ANY)
    return pl.pallas_call(
        functools.partial(down_kernel, count),
        in_specs=[
            pl.BlockSpec(memory_space=pltpu.SMEM),
            pl.BlockSpec(memory_space=pltpu.VMEM),
            anywhere,
            anywhere,
        ],
        out_specs=[pl.BlockSpec(memory_space=pltpu.VMEM)] * count,
        out_shape=[jax.ShapeDtypeStruct((2, rows // 2, width), kind)] * count,
        scratch_shapes=[
            pltpu.VMEM((count, units, width), bf16),
            pltpu.VMEM((count, units // block_units, width), jnp.int32),
            pltpu.SemaphoreType.DMA((count,)),
            pltpu.SemaphoreType.DMA((count,)),
        ],
        compiler_params=pltpu.CompilerParams(vmem_limit_bytes=vmem),
        cost_estimate=pl.CostEstimate(
            flops=2 * rows * units * width * count,
            bytes_accessed=3 * units * width * count,
            transcendentals=0,
        ),
        name="down_projection",
    )(blocks, tokens, coded_weight, block_exponent)


def reduce_blocks(near, direct, own, q):
    low_right = send(near[0], along_first(1))
    high_left = send(near[1], along_first(-1))
    high_right = send(direct[1], along_first(1))
    low_left = send(direct[2], along_first(-1))
    low, high = plus(direct[0], low_right).astype(bf16), plus(direct[3], high_left).astype(bf16)
    low_right = send(low, along_first(1))
    high_left = send(high, along_first(-1))
    summed = jnp.concatenate(
        [plus(own[0], low_right, low_left), plus(own[1], high_left, high_right)]
    )
    halved = summed.astype(bf16)

    def at(array, shift):
        return lax.dynamic_index_in_dim(array, (q + shift) % side, 0, keepdims=False)

    parts = [send(at(halved, shift), along_second(shift)) for shift in (1, 3, 2)]
    return plus(at(summed, 0), *parts), (low, high)


def body(
    gated_hidden,
    coded_weight,
    block_exponent,
    stream_input,
    lower_layer,
    middle_layer,
    prior_lower,
    prior_middle,
    prior_upper,
    accepted,
    draft_input_weight,
    draft_gain,
):
    steps, rows, unit_count = gated_hidden.shape
    feature_slice = stream_input.shape[2]
    out_slice = draft_input_weight.shape[2]
    replicas = lax.axis_size("replica")
    tensors = lax.axis_size("tensor")
    width = feature_slice * tensors
    slots_all = steps * rows * replicas
    slots = rows * 3 // 4
    x, c, p, q = place()

    with jax.named_scope("down"):
        tokens = gated_hidden.reshape(steps * rows, unit_count)
        second = jnp.arange(side, dtype=jnp.int32)

        def columns(shift):
            first = (p + shift) % side
            return jnp.where(c == 0, first * side + second, second * side + first)

        near = down_pieces(columns(2), tokens, coded_weight, block_exponent, bf16)
        near, accepted = lax.optimization_barrier((near, accepted))

    with jax.named_scope("select"):
        row = jnp.arange(rows, dtype=jnp.int32)
        before = row[:, None] <= row[None, :]
        first_live = (accepted >= 1).astype(jnp.int32)
        second_live = (accepted >= 2).astype(jnp.int32)
        first_slot = jnp.sum(jnp.where(before, first_live[:, None], 0), axis=0) - 1
        second_slot = 2 * slots - jnp.sum(jnp.where(before, second_live[:, None], 0), axis=0)
        first_slot = jnp.where(first_live == 1, first_slot, -1)
        second_slot = jnp.where(second_live == 1, second_slot, -1)
        slot = jnp.arange(2 * slots, dtype=jnp.int32)[:, None]
        select = (slot == jnp.concatenate([first_slot, second_slot])[None, :]).astype(bf16)

        def pick(chosen, first, second):
            return jnp.dot(
                chosen, jnp.concatenate([first, second]), preferred_element_type=f32
            ).astype(bf16)

        pair = pick(
            select,
            jnp.concatenate([prior_lower, prior_middle], axis=1),
            jnp.concatenate([lower_layer, middle_layer], axis=1),
        )
        front = jnp.dot(
            select[:slots, :rows], prior_upper, preferred_element_type=f32
        ).astype(bf16)
        folded = jnp.concatenate([front[: slots // 2], front[slots // 2 :]], axis=1)
        payload = jnp.concatenate([pair, folded])
    gathered = lax.all_gather(payload, "replica", axis=0, tiled=True)

    with jax.named_scope("down"):
        others, payload = lax.optimization_barrier(
            (jnp.concatenate([columns(1), columns(3)]), payload)
        )
        direct = down_pieces(others, tokens, coded_weight, block_exponent, bf16)
        direct, mine = lax.optimization_barrier((direct, columns(0)))
        own = down_pieces(mine, tokens, coded_weight, block_exponent, f32)

    own, draft_weight = lax.optimization_barrier((own, draft_input_weight))
    pair_weight = draft_weight[:2].astype(bf16).reshape(2 * feature_slice, out_slice)
    third_weight = draft_weight[2].astype(bf16)
    with jax.named_scope("reduce_down"):
        mixed, begun = reduce_blocks(near[::2], direct[::2], own[::2], q)
        follow, _ = lax.optimization_barrier((near[1::2], begun))
        mixed_second, _ = reduce_blocks(follow, direct[1::2], own[1::2], q)
    upper = [(stream_input[0].astype(f32) + mixed).astype(bf16)]
    with jax.named_scope("back"):
        back = pick(select[slots:], prior_upper, upper[0])
    stream_second, _ = lax.optimization_barrier((stream_input[1], back))
    upper.append((stream_second.astype(f32) + mixed_second).astype(bf16))
    upper_layer = jnp.stack(upper)

    with jax.named_scope("back"):
        chips = [back] + [send(back, along_x(-shift)) for shift in (1, 2, 3)]
        chips = jnp.stack(turned(chips, x))
        others = send(chips, other_core())

    with jax.named_scope("targets"):
        chosen = pick(select, upper[0], upper[1])
        parity = lax.axis_index("tensor") % 2
        even, odd = chosen[:slots], chosen[slots:]
        posted = [jnp.where((parity + turn) % 2 == 0, even, odd) for turn in range(2)]
        got = []
        for turn in range(2):
            routes = []
            for d in range(replicas * tensors):
                r, t = divmod(d, tensors)
                owner = t // 2
                taken = row_block(owner % cores, 2 * r + (t + turn) % 2)
                routes.append((d, owner * tensors + taken))
            got.append(send(posted[turn], routes))

    with jax.named_scope("forward"):
        by_replica = gathered.reshape(replicas, -1, 2 * feature_slice)
        stride = by_replica.shape[1]
        pairs, fronts = by_replica[:, : 2 * slots], by_replica[:, 2 * slots :]
        fronts = jnp.concatenate(
            [fronts[:, :, :feature_slice], fronts[:, :, feature_slice:]], axis=1
        )

        def replica_of(shift, half):
            return 2 * ((p + shift) % side) + half

        def pair_product(weight, shift, half):
            rows_of = lax.dynamic_slice_in_dim(
                gathered, replica_of(shift, half) * stride, 2 * slots, axis=0
            )
            return jnp.dot(rows_of, weight, preferred_element_type=f32)

        def third_product(weight, shift, half):
            rows_of = lax.dynamic_slice_in_dim(
                thirds, replica_of(shift, half) * 2 * slots, 2 * slots, axis=0
            )
            return jnp.dot(rows_of, weight, preferred_element_type=f32)

        def piece(total, kind):
            return total.astype(kind).reshape(2, slots, out_slice)

        far_pairs = [pair_product(pair_weight, 2, half) for half in range(2)]
        others, fronts, far_pairs, _ = lax.optimization_barrier(
            (others, fronts, far_pairs, posted)
        )
        backs = jnp.stack(
            [jnp.where(c == 0, chips, others), jnp.where(c == 0, others, chips)], axis=1
        ).reshape(replicas, slots, feature_slice)
        thirds = jnp.concatenate([fronts, backs], axis=1).reshape(-1, feature_slice)
        near = [
            piece(far_pairs[half] + third_product(third_weight, 2, half), bf16)
            for half in range(2)
        ]
        _, got, pair_weight, third_weight = lax.optimization_barrier(
            (near, got, pair_weight, third_weight)
        )
        direct = [
            piece(
                pair_product(pair_weight, shift, half) + third_product(third_weight, shift, half),
                bf16,
            )
            for shift in (1, 3)
            for half in range(2)
        ]
        _, pair_weight, third_weight = lax.optimization_barrier(
            (direct, pair_weight, third_weight)
        )
        own = [
            piece(
                pair_product(pair_weight, 0, half) + third_product(third_weight, 0, half), f32
            )
            for half in range(2)
        ]

    with jax.named_scope("reduce_draft"):
        drafted, _ = reduce_blocks(near, direct, own, q)

    with jax.named_scope("norm"):
        front_rows = q % 2 == 0
        targets = jnp.concatenate(
            [jnp.where(front_rows, got[0], got[1]), jnp.where(front_rows, got[1], got[0])],
            axis=1,
        ).astype(f32)
        gain = draft_gain[None, :]
        scaled = gain * drafted
        sums = jnp.stack(
            [
                jnp.sum(drafted * drafted, axis=1),
                jnp.sum(scaled * scaled, axis=1),
                jnp.sum(scaled * targets, axis=1),
            ]
        )
        sums = sums + send(sums, other_core_rows())
        sums = sums + send(sums, along_x(1)) + send(sums, along_x(2)) + send(sums, along_x(3))
        scale = lax.rsqrt(sums[0] / width + epsilon)
        inner = (scale * sums[1] - sums[2]) / slots_all
        error = gain * (scaled * scale[:, None] - targets) / slots_all
        slope = (scale[:, None] * error - drafted * (scale**3 * inner / width)[:, None]).astype(
            bf16
        )

    with jax.named_scope("gather_slope"):
        ring = [slope] + [send(slope, along_second(-shift)) for shift in (1, 2, 3)]
        ring = turned(ring, q)
        upper_half, lower_half = jnp.concatenate(ring[:2]), jnp.concatenate(ring[2:])
        previous_upper = send(upper_half, along_first(1))
        following_lower = send(lower_half, along_first(-1))
        previous_lower = send(lower_half, along_first(1))
        following_upper = send(upper_half, along_first(-1))
        low = send(previous_upper, along_first(1))
        high = send(following_lower, along_first(-1))

    with jax.named_scope("step"):
        features = jnp.concatenate([pairs.reshape(-1, 2 * feature_slice), thirds], axis=1)

        def product(places, slopes):
            inputs = [
                lax.dynamic_slice_in_dim(
                    features, (2 * ((p + shift) % side) + half) * 2 * slots, 2 * slots, axis=0
                )
                for shift, half in places
            ]
            return lax.dot_general(
                jnp.concatenate(inputs),
                jnp.concatenate(slopes),
                (((0,), (0,)), ((), ())),
                preferred_element_type=f32,
            )

        upper_half, lower_half, previous_upper, following_lower = lax.optimization_barrier(
            (upper_half, lower_half, previous_upper, following_lower)
        )
        total = product([(0, 0), (0, 1)], [upper_half, lower_half])
        total = lax.optimization_barrier(
            total + product([(3, 0), (1, 1)], [previous_upper, following_lower])
        )
        total = lax.optimization_barrier(
            total + product([(3, 1), (1, 0)], [previous_lower, following_upper])
        )
        total = total + product([(2, 0), (2, 1)], [low, high])
        new_weight = (draft_input_weight.reshape(total.shape) - step_rate * total).astype(bf16)
        new_weight = new_weight.reshape(draft_input_weight.shape)
    return (upper_layer, new_weight)


def solution(mesh):
    return jax.shard_map(
        body,
        mesh=mesh,
        in_specs=(
            P(None, "replica", "tensor"),
            P("tensor", None),
            P("tensor", None),
            P(None, "replica", "tensor"),
            P("replica", "tensor"),
            P("replica", "tensor"),
            P("replica", "tensor"),
            P("replica", "tensor"),
            P("replica", "tensor"),
            P("replica"),
            P(None, "tensor", "replica"),
            P("replica"),
        ),
        out_specs=(P(None, "replica", "tensor"), P(None, "tensor", "replica")),
        check_vma=False,
    )
```

```python
import functools

import jax
import jax.numpy as jnp
from jax import lax
from jax.experimental import pallas as pl
from jax.experimental.pallas import tpu as pltpu
from jax.sharding import PartitionSpec as P

step_rate = 8.0
epsilon = 1e-06
side = 4
cores = 2
block_units = 32
f32 = jnp.float32
bf16 = jnp.bfloat16
mesh_axes = ("replica", "tensor")
vmem = 56 * 1024 * 1024
ahead = 4


def coordinates(device):
    replica, tensor = divmod(device, side * side)
    x, c = divmod(replica, cores)
    z, y = divmod(tensor, side)
    return x, c, z, y


def device_at(x, c, z, y):
    return ((x % side) * cores + c % cores) * side * side + (z % side) * side + y % side


def moved(target):
    return [(d, target(*coordinates(d))) for d in range(side * cores * side * side)]


def along_first(shift):
    return moved(
        lambda x, c, z, y: device_at(x, c, z + shift * (c == 0), y + shift * (c == 1))
    )


def along_second(shift):
    return moved(
        lambda x, c, z, y: device_at(x, c, z + shift * (c == 1), y + shift * (c == 0))
    )


def along_x(shift):
    return moved(lambda x, c, z, y: device_at(x + shift, c, z, y))


def other_core():
    return moved(lambda x, c, z, y: device_at(x, 1 - c, z, y))


def send(array, pairs):
    return lax.ppermute(array, mesh_axes, pairs)


def plus(*terms):
    return functools.reduce(jnp.add, [term.astype(f32) for term in terms])


def other_core_rows():
    return moved(lambda x, c, z, y: device_at(x, 1 - c, y, z))


def row_block(c, tensor):
    z, y = tensor // side, tensor % side
    return z * side + y if c == 0 else y * side + z


def turned(pieces, places):
    for bit in (1, 2):
        moves = places // bit % 2 == 1
        pieces = [
            jnp.where(moves, pieces[(j - bit) % side], pieces[j]) for j in range(side)
        ]
    return pieces


def place():
    replica, tensor = lax.axis_index("replica"), lax.axis_index("tensor")
    x, c = replica // cores, replica % cores
    z, y = tensor // side, tensor % side
    return x, c, jnp.where(c == 0, z, y), jnp.where(c == 0, y, z)


def down_kernel(
    count, blocks_ref, tokens_ref, coded_ref, exponent_ref, *refs
):
    pieces, (coded, exponent, coded_sem, exponent_sem) = refs[: count // 2], refs[count // 2 :]
    _, units, columns = coded.shape

    def copies(i):
        start = pl.multiple_of(blocks_ref[i] * columns, columns)
        taken = (slice(None), pl.ds(start, columns))
        return (
            pltpu.make_async_copy(coded_ref.at[taken], coded.at[i], coded_sem.at[i]),
            pltpu.make_async_copy(exponent_ref.at[taken], exponent.at[i], exponent_sem.at[i]),
        )

    for i in range(min(ahead, count)):
        for copy in copies(i):
            copy.start()
    for i in range(count):
        for copy in copies(i):
            copy.wait()
        if i + ahead < count:
            for copy in copies(i + ahead):
                copy.start()
        factor = jnp.exp2(exponent[i].astype(f32) - 127.0).astype(bf16)
        weight = coded[i].reshape(units // block_units, block_units, columns)
        weight = (weight * factor[:, None, :]).reshape(units, columns)
        total = jnp.dot(tokens_ref[...], weight, preferred_element_type=f32)
        pieces[i // 2][i % 2] = total.astype(pieces[i // 2].dtype)


def down_pieces(blocks, tokens, coded_weight, block_exponent, kind):
    rows, units = tokens.shape
    width = coded_weight.shape[1] // (side * side)
    count = blocks.shape[0]
    anywhere = pl.BlockSpec(memory_space=pl.ANY)
    return pl.pallas_call(
        functools.partial(down_kernel, count),
        in_specs=[
            pl.BlockSpec(memory_space=pltpu.SMEM),
            pl.BlockSpec(memory_space=pltpu.VMEM),
            anywhere,
            anywhere,
        ],
        out_specs=[pl.BlockSpec(memory_space=pltpu.VMEM)] * (count // 2),
        out_shape=[jax.ShapeDtypeStruct((2, rows, width), kind)] * (count // 2),
        scratch_shapes=[
            pltpu.VMEM((count, units, width), bf16),
            pltpu.VMEM((count, units // block_units, width), jnp.int32),
            pltpu.SemaphoreType.DMA((count,)),
            pltpu.SemaphoreType.DMA((count,)),
        ],
        compiler_params=pltpu.CompilerParams(vmem_limit_bytes=vmem),
        cost_estimate=pl.CostEstimate(
            flops=2 * rows * units * width * count,
            bytes_accessed=3 * units * width * count,
            transcendentals=0,
        ),
        name="down_projection",
    )(blocks, tokens, coded_weight, block_exponent)


def reduce_blocks(near, direct, own, q):
    low_right = send(near[0], along_first(1))
    high_left = send(near[1], along_first(-1))
    high_right = send(direct[1], along_first(1))
    low_left = send(direct[2], along_first(-1))
    low_right = send(direct[0] + low_right, along_first(1))
    high_left = send(direct[3] + high_left, along_first(-1))
    summed = jnp.concatenate(
        [plus(own[0], low_right, low_left), plus(own[1], high_left, high_right)]
    )
    halved = summed.astype(bf16)

    def at(array, shift):
        return lax.dynamic_index_in_dim(array, (q + shift) % side, 0, keepdims=False)

    parts = [send(at(halved, shift), along_second(shift)) for shift in (1, 3, 2)]
    return plus(at(summed, 0), *parts), summed


def body(
    gated_hidden,
    coded_weight,
    block_exponent,
    stream_input,
    lower_layer,
    middle_layer,
    prior_lower,
    prior_middle,
    prior_upper,
    accepted,
    draft_input_weight,
    draft_gain,
):
    steps, rows, unit_count = gated_hidden.shape
    feature_slice = stream_input.shape[2]
    out_slice = draft_input_weight.shape[2]
    replicas = lax.axis_size("replica")
    tensors = lax.axis_size("tensor")
    width = feature_slice * tensors
    slots_all = steps * rows * replicas
    slots = rows * 3 // 4
    x, c, p, q = place()

    with jax.named_scope("down"):
        tokens = gated_hidden.reshape(steps * rows, unit_count)
        second = jnp.arange(side, dtype=jnp.int32)

        def columns(shift):
            first = (p + shift) % side
            return jnp.where(c == 0, first * side + second, second * side + first)

        near = down_pieces(columns(2), tokens, coded_weight, block_exponent, bf16)
        near, accepted = lax.optimization_barrier((near, accepted))

    with jax.named_scope("select"):
        row = jnp.arange(rows, dtype=jnp.int32)
        before = row[:, None] <= row[None, :]
        first_live = (accepted >= 1).astype(jnp.int32)
        second_live = (accepted >= 2).astype(jnp.int32)
        first_slot = jnp.sum(jnp.where(before, first_live[:, None], 0), axis=0) - 1
        second_slot = 2 * slots - jnp.sum(jnp.where(before, second_live[:, None], 0), axis=0)
        first_slot = jnp.where(first_live == 1, first_slot, -1)
        second_slot = jnp.where(second_live == 1, second_slot, -1)
        slot = jnp.arange(2 * slots, dtype=jnp.int32)[:, None]
        select = (slot == jnp.concatenate([first_slot, second_slot])[None, :]).astype(bf16)

        def pick(chosen, first, second):
            return jnp.dot(
                chosen, jnp.concatenate([first, second]), preferred_element_type=f32
            ).astype(bf16)

        pair = pick(
            select,
            jnp.concatenate([prior_lower, prior_middle], axis=1),
            jnp.concatenate([lower_layer, middle_layer], axis=1),
        )
        front = jnp.dot(
            select[:slots, :rows], prior_upper, preferred_element_type=f32
        ).astype(bf16)
        folded = jnp.concatenate([front[: slots // 2], front[slots // 2 :]], axis=1)
        payload = jnp.concatenate([pair, folded])
    gathered = lax.all_gather(payload, "replica", axis=0, tiled=True)

    with jax.named_scope("down"):
        others, payload = lax.optimization_barrier(
            (jnp.concatenate([columns(1), columns(3)]), payload)
        )
        direct = down_pieces(others, tokens, coded_weight, block_exponent, bf16)
        direct, mine = lax.optimization_barrier((direct, columns(0)))
        own = down_pieces(mine, tokens, coded_weight, block_exponent, f32)

    with jax.named_scope("reduce_down"):
        mixed, first_sum = reduce_blocks(near, direct, own, q)
    _, draft_weight = lax.optimization_barrier((first_sum, draft_input_weight))
    pair_weight = draft_weight[:2].astype(bf16).reshape(2 * feature_slice, out_slice)
    third_weight = draft_weight[2].astype(bf16)
    mixed, pair_weight, third_weight = lax.optimization_barrier((mixed, pair_weight, third_weight))
    upper_layer = (
        stream_input.astype(f32) + mixed.reshape(steps, rows, feature_slice)
    ).astype(bf16)

    with jax.named_scope("back"):
        back = pick(select[slots:], prior_upper, upper_layer[0])
        chips = [back] + [send(back, along_x(-shift)) for shift in (1, 2, 3)]
        chips = jnp.stack(turned(chips, x))
        others = send(chips, other_core())

    with jax.named_scope("targets"):
        chosen = pick(select, upper_layer[0], upper_layer[1])
        parity = lax.axis_index("tensor") % 2
        even, odd = chosen[:slots], chosen[slots:]
        posted = [jnp.where((parity + turn) % 2 == 0, even, odd) for turn in range(2)]
        got = []
        for turn in range(2):
            routes = []
            for d in range(replicas * tensors):
                r, t = divmod(d, tensors)
                owner = t // 2
                taken = row_block(owner % cores, 2 * r + (t + turn) % 2)
                routes.append((d, owner * tensors + taken))
            got.append(send(posted[turn], routes))

    with jax.named_scope("forward"):
        by_replica = gathered.reshape(replicas, -1, 2 * feature_slice)
        stride = by_replica.shape[1]
        pairs, fronts = by_replica[:, : 2 * slots], by_replica[:, 2 * slots :]
        fronts = jnp.concatenate(
            [fronts[:, :, :feature_slice], fronts[:, :, feature_slice:]], axis=1
        )

        def replica_of(shift, half):
            return 2 * ((p + shift) % side) + half

        def pair_product(weight, shift, half):
            rows_of = lax.dynamic_slice_in_dim(
                gathered, replica_of(shift, half) * stride, 2 * slots, axis=0
            )
            return jnp.dot(rows_of, weight, preferred_element_type=f32)

        def third_product(weight, shift, half):
            rows_of = lax.dynamic_slice_in_dim(
                thirds, replica_of(shift, half) * 2 * slots, 2 * slots, axis=0
            )
            return jnp.dot(rows_of, weight, preferred_element_type=f32)

        def piece(total, kind):
            return total.astype(kind).reshape(2, slots, out_slice)

        far_pairs = [pair_product(pair_weight, 2, half) for half in range(2)]
        others, fronts, far_pairs, _ = lax.optimization_barrier(
            (others, fronts, far_pairs, posted)
        )
        backs = jnp.stack(
            [jnp.where(c == 0, chips, others), jnp.where(c == 0, others, chips)], axis=1
        ).reshape(replicas, slots, feature_slice)
        thirds = jnp.concatenate([fronts, backs], axis=1).reshape(-1, feature_slice)
        near = [
            piece(far_pairs[half] + third_product(third_weight, 2, half), bf16)
            for half in range(2)
        ]
        _, got, pair_weight, third_weight = lax.optimization_barrier(
            (near, got, pair_weight, third_weight)
        )
        direct = [
            piece(
                pair_product(pair_weight, shift, half) + third_product(third_weight, shift, half),
                bf16,
            )
            for shift in (1, 3)
            for half in range(2)
        ]
        _, pair_weight, third_weight = lax.optimization_barrier(
            (direct, pair_weight, third_weight)
        )
        own = [
            piece(
                pair_product(pair_weight, 0, half) + third_product(third_weight, 0, half), f32
            )
            for half in range(2)
        ]

    with jax.named_scope("reduce_draft"):
        drafted, _ = reduce_blocks(near, direct, own, q)

    with jax.named_scope("norm"):
        front_rows = q % 2 == 0
        targets = jnp.concatenate(
            [jnp.where(front_rows, got[0], got[1]), jnp.where(front_rows, got[1], got[0])],
            axis=1,
        ).astype(f32)
        gain = draft_gain[None, :]
        scaled = gain * drafted
        sums = jnp.stack(
            [
                jnp.sum(drafted * drafted, axis=1),
                jnp.sum(scaled * scaled, axis=1),
                jnp.sum(scaled * targets, axis=1),
            ]
        )
        sums = sums + send(sums, other_core_rows())
        sums = sums + send(sums, along_x(1)) + send(sums, along_x(2)) + send(sums, along_x(3))
        scale = lax.rsqrt(sums[0] / width + epsilon)
        inner = (scale * sums[1] - sums[2]) / slots_all
        error = gain * (scaled * scale[:, None] - targets) / slots_all
        slope = (scale[:, None] * error - drafted * (scale**3 * inner / width)[:, None]).astype(
            bf16
        )

    with jax.named_scope("gather_slope"):
        ring = [slope] + [send(slope, along_second(-shift)) for shift in (1, 2, 3)]
        ring = turned(ring, q)
        upper_half, lower_half = jnp.concatenate(ring[:2]), jnp.concatenate(ring[2:])
        previous_upper = send(upper_half, along_first(1))
        following_lower = send(lower_half, along_first(-1))
        previous_lower = send(lower_half, along_first(1))
        following_upper = send(upper_half, along_first(-1))
        low = send(previous_upper, along_first(1))
        high = send(following_lower, along_first(-1))

    with jax.named_scope("step"):
        features = jnp.concatenate([pairs.reshape(-1, 2 * feature_slice), thirds], axis=1)

        def product(places, slopes):
            inputs = [
                lax.dynamic_slice_in_dim(
                    features, (2 * ((p + shift) % side) + half) * 2 * slots, 2 * slots, axis=0
                )
                for shift, half in places
            ]
            return lax.dot_general(
                jnp.concatenate(inputs),
                jnp.concatenate(slopes),
                (((0,), (0,)), ((), ())),
                preferred_element_type=f32,
            )

        upper_half, lower_half, previous_upper, following_lower = lax.optimization_barrier(
            (upper_half, lower_half, previous_upper, following_lower)
        )
        total = product([(0, 0), (0, 1)], [upper_half, lower_half])
        total = lax.optimization_barrier(
            total + product([(3, 0), (1, 1)], [previous_upper, following_lower])
        )
        total = lax.optimization_barrier(
            total + product([(3, 1), (1, 0)], [previous_lower, following_upper])
        )
        total = total + product([(2, 0), (2, 1)], [low, high])
        new_weight = (draft_input_weight.reshape(total.shape) - step_rate * total).astype(bf16)
        new_weight = new_weight.reshape(draft_input_weight.shape)
    return (upper_layer, new_weight)


def solution(mesh):
    return jax.shard_map(
        body,
        mesh=mesh,
        in_specs=(
            P(None, "replica", "tensor"),
            P("tensor", None),
            P("tensor", None),
            P(None, "replica", "tensor"),
            P("replica", "tensor"),
            P("replica", "tensor"),
            P("replica", "tensor"),
            P("replica", "tensor"),
            P("replica", "tensor"),
            P("replica"),
            P(None, "tensor", "replica"),
            P("replica"),
        ),
        out_specs=(P(None, "replica", "tensor"), P(None, "tensor", "replica")),
        check_vma=False,
    )
```

```python
import functools

import jax
import jax.numpy as jnp
from jax import lax
from jax.experimental import pallas as pl
from jax.experimental.pallas import tpu as pltpu
from jax.sharding import PartitionSpec as P

step_rate = 8.0
epsilon = 1e-06
side = 4
cores = 2
block_units = 32
f32 = jnp.float32
bf16 = jnp.bfloat16
mesh_axes = ("replica", "tensor")
vmem = 56 * 1024 * 1024


def coordinates(device):
    replica, tensor = divmod(device, side * side)
    x, c = divmod(replica, cores)
    z, y = divmod(tensor, side)
    return x, c, z, y


def device_at(x, c, z, y):
    return ((x % side) * cores + c % cores) * side * side + (z % side) * side + y % side


def moved(target):
    return [(d, target(*coordinates(d))) for d in range(side * cores * side * side)]


def along_first(shift):
    return moved(
        lambda x, c, z, y: device_at(x, c, z + shift * (c == 0), y + shift * (c == 1))
    )


def along_second(shift):
    return moved(
        lambda x, c, z, y: device_at(x, c, z + shift * (c == 1), y + shift * (c == 0))
    )


def along_x(shift):
    return moved(lambda x, c, z, y: device_at(x + shift, c, z, y))


def other_core():
    return moved(lambda x, c, z, y: device_at(x, 1 - c, z, y))


def send(array, pairs):
    return lax.ppermute(array, mesh_axes, pairs)


def plus(*terms):
    return functools.reduce(jnp.add, [term.astype(f32) for term in terms])


def other_core_rows():
    return moved(lambda x, c, z, y: device_at(x, 1 - c, y, z))


def row_block(c, tensor):
    z, y = tensor // side, tensor % side
    return z * side + y if c == 0 else y * side + z


def turned(pieces, places):
    for bit in (1, 2):
        moves = places // bit % 2 == 1
        pieces = [
            jnp.where(moves, pieces[(j - bit) % side], pieces[j]) for j in range(side)
        ]
    return pieces


def place():
    replica, tensor = lax.axis_index("replica"), lax.axis_index("tensor")
    x, c = replica // cores, replica % cores
    z, y = tensor // side, tensor % side
    return x, c, jnp.where(c == 0, z, y), jnp.where(c == 0, y, z)


def down_kernel(blocks_ref, tokens_ref, *refs):
    coded_refs, exponent_refs, pieces = refs[:2], refs[2:4], refs[4:]
    i = pl.program_id(0)
    totals = []
    for coded_ref, exponent_ref in zip(coded_refs, exponent_refs):
        units, columns = coded_ref.shape
        factor = jnp.exp2(exponent_ref[...].astype(f32) - 127.0).astype(bf16)
        weight = coded_ref[...].reshape(units // block_units, block_units, columns)
        weight = (weight * factor[:, None, :]).reshape(units, columns)
        totals.append(jnp.dot(tokens_ref[...], weight, preferred_element_type=f32))
    for k, piece in enumerate(pieces):

        @pl.when(i == k)
        def _():
            for half, total in enumerate(totals):
                piece[half] = total.astype(piece.dtype)


def down_pieces(blocks, tokens, coded_weight, block_exponent, kind):
    rows, units = tokens.shape
    width = coded_weight.shape[1] // (side * side)
    count = blocks.shape[0]

    def column_block(height, half):
        return pl.BlockSpec((height, width), lambda i, blocks: (0, blocks[2 * i + half]))

    return pl.pallas_call(
        down_kernel,
        grid_spec=pltpu.PrefetchScalarGridSpec(
            num_scalar_prefetch=1,
            grid=(count // 2,),
            in_specs=[
                pl.BlockSpec((rows, units), lambda i, blocks: (0, 0)),
                column_block(units, 0),
                column_block(units, 1),
                column_block(units // block_units, 0),
                column_block(units // block_units, 1),
            ],
            out_specs=[
                pl.BlockSpec((2, rows, width), lambda i, blocks: (0, 0, 0))
                for _ in range(count // 2)
            ],
        ),
        out_shape=[jax.ShapeDtypeStruct((2, rows, width), kind)] * (count // 2),
        compiler_params=pltpu.CompilerParams(vmem_limit_bytes=vmem),
        cost_estimate=pl.CostEstimate(
            flops=2 * rows * units * width * count,
            bytes_accessed=3 * units * width * count,
            transcendentals=0,
        ),
        name="down_projection",
    )(blocks, tokens, coded_weight, coded_weight, block_exponent, block_exponent)


def round_kernel(after_ref, wide_ref, out_ref):
    out_ref[...] = wide_ref[...].astype(bf16)


def rounded_rows(wide, start, count, after):
    step, columns = min(256, count), wide.shape[1]
    return pl.pallas_call(
        round_kernel,
        grid=(count // step,),
        in_specs=[
            pl.BlockSpec(memory_space=pl.ANY),
            pl.BlockSpec((step, columns), lambda i: (start // step + i, 0)),
        ],
        out_specs=pl.BlockSpec((step, columns), lambda i: (i, 0)),
        out_shape=jax.ShapeDtypeStruct((count, columns), bf16),
        compiler_params=pltpu.CompilerParams(vmem_limit_bytes=vmem),
        cost_estimate=pl.CostEstimate(
            flops=count * columns, bytes_accessed=6 * count * columns, transcendentals=0
        ),
        name="round_weight",
    )(after, wide)


def reduce_blocks(near, direct, own, q):
    low_right = send(near[0], along_first(1))
    high_left = send(near[1], along_first(-1))
    high_right = send(direct[1], along_first(1))
    low_left = send(direct[2], along_first(-1))
    low_right = send(direct[0] + low_right, along_first(1))
    high_left = send(direct[3] + high_left, along_first(-1))
    summed = jnp.concatenate(
        [plus(own[0], low_right, low_left), plus(own[1], high_left, high_right)]
    )
    halved = summed.astype(bf16)

    def at(array, shift):
        return lax.dynamic_index_in_dim(array, (q + shift) % side, 0, keepdims=False)

    parts = [send(at(halved, shift), along_second(shift)) for shift in (1, 3, 2)]
    return plus(at(summed, 0), *parts), summed[0, :8, :128]


def body(
    gated_hidden,
    coded_weight,
    block_exponent,
    stream_input,
    lower_layer,
    middle_layer,
    prior_lower,
    prior_middle,
    prior_upper,
    accepted,
    draft_input_weight,
    draft_gain,
):
    steps, rows, unit_count = gated_hidden.shape
    feature_slice = stream_input.shape[2]
    out_slice = draft_input_weight.shape[2]
    replicas = lax.axis_size("replica")
    tensors = lax.axis_size("tensor")
    width = feature_slice * tensors
    slots_all = steps * rows * replicas
    slots = rows * 3 // 4
    x, c, p, q = place()

    with jax.named_scope("down"):
        tokens = gated_hidden.reshape(steps * rows, unit_count)
        second = jnp.arange(side, dtype=jnp.int32)

        def columns(shift):
            first = (p + shift) % side
            return jnp.where(c == 0, first * side + second, second * side + first)

        near = down_pieces(columns(2), tokens, coded_weight, block_exponent, bf16)
        near, accepted = lax.optimization_barrier((near, accepted))

    with jax.named_scope("select"):
        row = jnp.arange(rows, dtype=jnp.int32)
        before = row[:, None] <= row[None, :]
        first_live = (accepted >= 1).astype(jnp.int32)
        second_live = (accepted >= 2).astype(jnp.int32)
        first_slot = jnp.sum(jnp.where(before, first_live[:, None], 0), axis=0) - 1
        second_slot = 2 * slots - jnp.sum(jnp.where(before, second_live[:, None], 0), axis=0)
        first_slot = jnp.where(first_live == 1, first_slot, -1)
        second_slot = jnp.where(second_live == 1, second_slot, -1)
        slot = jnp.arange(2 * slots, dtype=jnp.int32)[:, None]
        select = (slot == jnp.concatenate([first_slot, second_slot])[None, :]).astype(bf16)

        def pick(chosen, first, second):
            return jnp.dot(
                chosen, jnp.concatenate([first, second]), preferred_element_type=f32
            ).astype(bf16)

        pair = pick(
            select,
            jnp.concatenate([prior_lower, prior_middle], axis=1),
            jnp.concatenate([lower_layer, middle_layer], axis=1),
        )
        front = jnp.dot(
            select[:slots, :rows], prior_upper, preferred_element_type=f32
        ).astype(bf16)
        folded = jnp.concatenate([front[: slots // 2], front[slots // 2 :]], axis=1)
        payload = jnp.concatenate([pair, folded])
    gathered = lax.all_gather(payload, "replica", axis=0, tiled=True)

    with jax.named_scope("down"):
        others, payload = lax.optimization_barrier(
            (jnp.concatenate([columns(1), columns(3)]), payload)
        )
        direct = down_pieces(others, tokens, coded_weight, block_exponent, bf16)
        direct, mine = lax.optimization_barrier((direct, columns(0)))
        own = down_pieces(mine, tokens, coded_weight, block_exponent, f32)

    with jax.named_scope("reduce_down"):
        mixed, first_sum = reduce_blocks(near, direct, own, q)
    flat_weight = draft_input_weight.reshape(3 * feature_slice, out_slice)
    pair_weight = rounded_rows(flat_weight, 0, 2 * feature_slice, first_sum)
    third_weight = rounded_rows(flat_weight, 2 * feature_slice, feature_slice, first_sum)
    upper_layer = (
        stream_input.astype(f32) + mixed.reshape(steps, rows, feature_slice)
    ).astype(bf16)

    with jax.named_scope("back"):
        back = pick(select[slots:], prior_upper, upper_layer[0])
        chips = [back] + [send(back, along_x(-shift)) for shift in (1, 2, 3)]
        chips = jnp.stack(turned(chips, x))
        others = send(chips, other_core())

    with jax.named_scope("targets"):
        chosen = pick(select, upper_layer[0], upper_layer[1])
        parity = lax.axis_index("tensor") % 2
        even, odd = chosen[:slots], chosen[slots:]
        posted = [jnp.where((parity + turn) % 2 == 0, even, odd) for turn in range(2)]
        got = []
        for turn in range(2):
            routes = []
            for d in range(replicas * tensors):
                r, t = divmod(d, tensors)
                owner = t // 2
                taken = row_block(owner % cores, 2 * r + (t + turn) % 2)
                routes.append((d, owner * tensors + taken))
            got.append(send(posted[turn], routes))

    with jax.named_scope("forward"):
        by_replica = gathered.reshape(replicas, -1, 2 * feature_slice)
        stride = by_replica.shape[1]
        pairs, fronts = by_replica[:, : 2 * slots], by_replica[:, 2 * slots :]
        fronts = jnp.concatenate(
            [fronts[:, :, :feature_slice], fronts[:, :, feature_slice:]], axis=1
        )

        def replica_of(shift, half):
            return 2 * ((p + shift) % side) + half

        def pair_product(weight, shift, half):
            rows_of = lax.dynamic_slice_in_dim(
                gathered, replica_of(shift, half) * stride, 2 * slots, axis=0
            )
            return jnp.dot(rows_of, weight, preferred_element_type=f32)

        def third_product(weight, shift, half):
            rows_of = lax.dynamic_slice_in_dim(
                thirds, replica_of(shift, half) * 2 * slots, 2 * slots, axis=0
            )
            return jnp.dot(rows_of, weight, preferred_element_type=f32)

        def piece(total, kind):
            return total.astype(kind).reshape(2, slots, out_slice)

        far_pairs = [pair_product(pair_weight, 2, half) for half in range(2)]
        others, fronts, far_pairs, _ = lax.optimization_barrier(
            (others, fronts, far_pairs, posted)
        )
        backs = jnp.stack(
            [jnp.where(c == 0, chips, others), jnp.where(c == 0, others, chips)], axis=1
        ).reshape(replicas, slots, feature_slice)
        thirds = jnp.concatenate([fronts, backs], axis=1).reshape(-1, feature_slice)
        near = [
            piece(far_pairs[half] + third_product(third_weight, 2, half), bf16)
            for half in range(2)
        ]
        _, got, pair_weight, third_weight = lax.optimization_barrier(
            (near, got, pair_weight, third_weight)
        )
        direct = [
            piece(
                pair_product(pair_weight, shift, half) + third_product(third_weight, shift, half),
                bf16,
            )
            for shift in (1, 3)
            for half in range(2)
        ]
        _, pair_weight, third_weight = lax.optimization_barrier(
            (direct, pair_weight, third_weight)
        )
        own = [
            piece(
                pair_product(pair_weight, 0, half) + third_product(third_weight, 0, half), f32
            )
            for half in range(2)
        ]

    with jax.named_scope("reduce_draft"):
        drafted, _ = reduce_blocks(near, direct, own, q)

    with jax.named_scope("norm"):
        front_rows = q % 2 == 0
        targets = jnp.concatenate(
            [jnp.where(front_rows, got[0], got[1]), jnp.where(front_rows, got[1], got[0])],
            axis=1,
        ).astype(f32)
        gain = draft_gain[None, :]
        scaled = gain * drafted
        sums = jnp.stack(
            [
                jnp.sum(drafted * drafted, axis=1),
                jnp.sum(scaled * scaled, axis=1),
                jnp.sum(scaled * targets, axis=1),
            ]
        )
        sums = sums + send(sums, other_core_rows())
        sums = sums + send(sums, along_x(1)) + send(sums, along_x(2)) + send(sums, along_x(3))
        scale = lax.rsqrt(sums[0] / width + epsilon)
        inner = (scale * sums[1] - sums[2]) / slots_all
        error = gain * (scaled * scale[:, None] - targets) / slots_all
        slope = (scale[:, None] * error - drafted * (scale**3 * inner / width)[:, None]).astype(
            bf16
        )

    with jax.named_scope("gather_slope"):
        ring = [slope] + [send(slope, along_second(-shift)) for shift in (1, 2, 3)]
        ring = turned(ring, q)
        upper_half, lower_half = jnp.concatenate(ring[:2]), jnp.concatenate(ring[2:])
        previous_upper = send(upper_half, along_first(1))
        following_lower = send(lower_half, along_first(-1))
        previous_lower = send(lower_half, along_first(1))
        following_upper = send(upper_half, along_first(-1))
        low = send(previous_upper, along_first(1))
        high = send(following_lower, along_first(-1))

    with jax.named_scope("step"):
        features = jnp.concatenate([pairs.reshape(-1, 2 * feature_slice), thirds], axis=1)

        def product(places, slopes):
            inputs = [
                lax.dynamic_slice_in_dim(
                    features, (2 * ((p + shift) % side) + half) * 2 * slots, 2 * slots, axis=0
                )
                for shift, half in places
            ]
            return lax.dot_general(
                jnp.concatenate(inputs),
                jnp.concatenate(slopes),
                (((0,), (0,)), ((), ())),
                preferred_element_type=f32,
            )

        upper_half, lower_half, previous_upper, following_lower = lax.optimization_barrier(
            (upper_half, lower_half, previous_upper, following_lower)
        )
        total = product([(0, 0), (0, 1)], [upper_half, lower_half])
        total = lax.optimization_barrier(
            total + product([(3, 0), (1, 1)], [previous_upper, following_lower])
        )
        total = lax.optimization_barrier(
            total + product([(3, 1), (1, 0)], [previous_lower, following_upper])
        )
        total = total + product([(2, 0), (2, 1)], [low, high])
        new_weight = (flat_weight - step_rate * total).astype(bf16)
        new_weight = new_weight.reshape(draft_input_weight.shape)
    return (upper_layer, new_weight)


def solution(mesh):
    return jax.shard_map(
        body,
        mesh=mesh,
        in_specs=(
            P(None, "replica", "tensor"),
            P("tensor", None),
            P("tensor", None),
            P(None, "replica", "tensor"),
            P("replica", "tensor"),
            P("replica", "tensor"),
            P("replica", "tensor"),
            P("replica", "tensor"),
            P("replica", "tensor"),
            P("replica"),
            P(None, "tensor", "replica"),
            P("replica"),
        ),
        out_specs=(P(None, "replica", "tensor"), P(None, "tensor", "replica")),
        check_vma=False,
    )
```

```python
import functools

import jax
import jax.numpy as jnp
from jax import lax
from jax.experimental import pallas as pl
from jax.experimental.pallas import tpu as pltpu
from jax.sharding import PartitionSpec as P

step_rate = 8.0
epsilon = 1e-06
side = 4
cores = 2
block_units = 32
f32 = jnp.float32
bf16 = jnp.bfloat16
mesh_axes = ("replica", "tensor")
vmem = 56 * 1024 * 1024


def coordinates(device):
    replica, tensor = divmod(device, side * side)
    x, c = divmod(replica, cores)
    z, y = divmod(tensor, side)
    return x, c, z, y


def device_at(x, c, z, y):
    return ((x % side) * cores + c % cores) * side * side + (z % side) * side + y % side


def moved(target):
    return [(d, target(*coordinates(d))) for d in range(side * cores * side * side)]


def along_first(shift):
    return moved(
        lambda x, c, z, y: device_at(x, c, z + shift * (c == 0), y + shift * (c == 1))
    )


def along_second(shift):
    return moved(
        lambda x, c, z, y: device_at(x, c, z + shift * (c == 1), y + shift * (c == 0))
    )


def along_x(shift):
    return moved(lambda x, c, z, y: device_at(x + shift, c, z, y))


def other_core():
    return moved(lambda x, c, z, y: device_at(x, 1 - c, z, y))


def send(array, pairs):
    return lax.ppermute(array, mesh_axes, pairs)


def plus(*terms):
    return functools.reduce(jnp.add, [term.astype(f32) for term in terms])


def other_core_rows():
    return moved(lambda x, c, z, y: device_at(x, 1 - c, y, z))


def row_block(c, tensor):
    z, y = tensor // side, tensor % side
    return z * side + y if c == 0 else y * side + z


def turned(pieces, places):
    for bit in (1, 2):
        moves = places // bit % 2 == 1
        pieces = [
            jnp.where(moves, pieces[(j - bit) % side], pieces[j]) for j in range(side)
        ]
    return pieces


def place():
    replica, tensor = lax.axis_index("replica"), lax.axis_index("tensor")
    x, c = replica // cores, replica % cores
    z, y = tensor // side, tensor % side
    return x, c, jnp.where(c == 0, z, y), jnp.where(c == 0, y, z)


def down_kernel(blocks_ref, tokens_ref, *refs):
    coded_refs, exponent_refs, pieces = refs[:2], refs[2:4], refs[4:]
    i = pl.program_id(0)
    totals = []
    for coded_ref, exponent_ref in zip(coded_refs, exponent_refs):
        units, columns = coded_ref.shape
        factor = jnp.exp2(exponent_ref[...].astype(f32) - 127.0).astype(bf16)
        weight = coded_ref[...].reshape(units // block_units, block_units, columns)
        weight = (weight * factor[:, None, :]).reshape(units, columns)
        totals.append(jnp.dot(tokens_ref[...], weight, preferred_element_type=f32))
    for k, piece in enumerate(pieces):

        @pl.when(i == k)
        def _():
            for half, total in enumerate(totals):
                piece[half] = total.astype(piece.dtype)


def down_pieces(blocks, tokens, coded_weight, block_exponent, kind):
    rows, units = tokens.shape
    width = coded_weight.shape[1] // (side * side)
    count = blocks.shape[0]

    def column_block(height, half):
        return pl.BlockSpec((height, width), lambda i, blocks: (0, blocks[2 * i + half]))

    return pl.pallas_call(
        down_kernel,
        grid_spec=pltpu.PrefetchScalarGridSpec(
            num_scalar_prefetch=1,
            grid=(count // 2,),
            in_specs=[
                pl.BlockSpec((rows, units), lambda i, blocks: (0, 0)),
                column_block(units, 0),
                column_block(units, 1),
                column_block(units // block_units, 0),
                column_block(units // block_units, 1),
            ],
            out_specs=[
                pl.BlockSpec((2, rows, width), lambda i, blocks: (0, 0, 0))
                for _ in range(count // 2)
            ],
        ),
        out_shape=[jax.ShapeDtypeStruct((2, rows, width), kind)] * (count // 2),
        compiler_params=pltpu.CompilerParams(vmem_limit_bytes=vmem),
        cost_estimate=pl.CostEstimate(
            flops=2 * rows * units * width * count,
            bytes_accessed=3 * units * width * count,
            transcendentals=0,
        ),
        name="down_projection",
    )(blocks, tokens, coded_weight, coded_weight, block_exponent, block_exponent)


def round_kernel(pair_steps, after_ref, wide_ref, pair_ref, third_ref):
    narrow = wide_ref[...].astype(bf16)

    @pl.when(pl.program_id(0) < pair_steps)
    def _():
        pair_ref[...] = narrow

    @pl.when(pl.program_id(0) >= pair_steps)
    def _():
        third_ref[...] = narrow


def rounded_weight(wide, after):
    rows, columns = wide.shape
    step = rows // 6
    pair_steps = 4
    return pl.pallas_call(
        functools.partial(round_kernel, pair_steps),
        grid=(6,),
        in_specs=[
            pl.BlockSpec(memory_space=pl.ANY),
            pl.BlockSpec((step, columns), lambda i: (i, 0)),
        ],
        out_specs=[
            pl.BlockSpec((step, columns), lambda i: (jnp.minimum(i, pair_steps - 1), 0)),
            pl.BlockSpec((step, columns), lambda i: (jnp.maximum(i - pair_steps, 0), 0)),
        ],
        out_shape=[
            jax.ShapeDtypeStruct((step * pair_steps, columns), bf16),
            jax.ShapeDtypeStruct((rows - step * pair_steps, columns), bf16),
        ],
        compiler_params=pltpu.CompilerParams(vmem_limit_bytes=vmem),
        cost_estimate=pl.CostEstimate(
            flops=rows * columns, bytes_accessed=6 * rows * columns, transcendentals=0
        ),
        name="round_weight",
    )(after, wide)


def held_kernel(after_ref, value_ref, out_ref):
    out_ref[...] = value_ref[...]


def held(value, after):
    return pl.pallas_call(
        held_kernel,
        in_specs=[pl.BlockSpec(memory_space=pl.ANY), pl.BlockSpec(memory_space=pltpu.VMEM)],
        out_specs=pl.BlockSpec(memory_space=pltpu.VMEM),
        out_shape=jax.ShapeDtypeStruct(value.shape, value.dtype),
        name="held",
    )(after, value)


def reduce_blocks(near, direct, own, q):
    low_right = send(near[0], along_first(1))
    high_left = send(near[1], along_first(-1))
    high_right = send(direct[1], along_first(1))
    low_left = send(direct[2], along_first(-1))
    low_right, high_left = direct[0] + low_right, direct[3] + high_left
    forwarded = high_left[0, :16, :128]
    low_right = send(low_right, along_first(1))
    high_left = send(high_left, along_first(-1))
    summed = jnp.concatenate(
        [plus(own[0], low_right, low_left), plus(own[1], high_left, high_right)]
    )
    halved = summed.astype(bf16)

    def at(array, shift):
        return lax.dynamic_index_in_dim(array, (q + shift) % side, 0, keepdims=False)

    parts = [send(at(halved, shift), along_second(shift)) for shift in (1, 3, 2)]
    return plus(at(summed, 0), *parts), forwarded, summed[0, :8, :128]


def body(
    gated_hidden,
    coded_weight,
    block_exponent,
    stream_input,
    lower_layer,
    middle_layer,
    prior_lower,
    prior_middle,
    prior_upper,
    accepted,
    draft_input_weight,
    draft_gain,
):
    steps, rows, unit_count = gated_hidden.shape
    feature_slice = stream_input.shape[2]
    out_slice = draft_input_weight.shape[2]
    replicas = lax.axis_size("replica")
    tensors = lax.axis_size("tensor")
    width = feature_slice * tensors
    slots_all = steps * rows * replicas
    slots = rows * 3 // 4
    x, c, p, q = place()

    with jax.named_scope("down"):
        tokens = gated_hidden.reshape(steps * rows, unit_count)
        second = jnp.arange(side, dtype=jnp.int32)

        def columns(shift):
            first = (p + shift) % side
            return jnp.where(c == 0, first * side + second, second * side + first)

        near = down_pieces(columns(2), tokens, coded_weight, block_exponent, bf16)
        near, accepted = lax.optimization_barrier((near, accepted))

    with jax.named_scope("select"):
        row = jnp.arange(rows, dtype=jnp.int32)
        before = row[:, None] <= row[None, :]
        first_live = (accepted >= 1).astype(jnp.int32)
        second_live = (accepted >= 2).astype(jnp.int32)
        first_slot = jnp.sum(jnp.where(before, first_live[:, None], 0), axis=0) - 1
        second_slot = 2 * slots - jnp.sum(jnp.where(before, second_live[:, None], 0), axis=0)
        first_slot = jnp.where(first_live == 1, first_slot, -1)
        second_slot = jnp.where(second_live == 1, second_slot, -1)
        slot = jnp.arange(2 * slots, dtype=jnp.int32)[:, None]
        slot_of = jnp.concatenate([first_slot, second_slot])
        select = (slot == slot_of[None, :]).astype(bf16)

        def pick(chosen, first, second):
            return jnp.dot(
                chosen, jnp.concatenate([first, second]), preferred_element_type=f32
            ).astype(bf16)

        pair = pick(
            select,
            jnp.concatenate([prior_lower, prior_middle], axis=1),
            jnp.concatenate([lower_layer, middle_layer], axis=1),
        )
        front = jnp.dot(
            select[:slots, :rows], prior_upper, preferred_element_type=f32
        ).astype(bf16)
        folded = jnp.concatenate([front[: slots // 2], front[slots // 2 :]], axis=1)
        payload = jnp.concatenate([pair, folded])
    gathered = lax.all_gather(payload, "replica", axis=0, tiled=True)

    with jax.named_scope("down"):
        others, payload = lax.optimization_barrier(
            (jnp.concatenate([columns(1), columns(3)]), payload)
        )
        direct = down_pieces(others, tokens, coded_weight, block_exponent, bf16)
        direct, mine = lax.optimization_barrier((direct, columns(0)))
        own = down_pieces(mine, tokens, coded_weight, block_exponent, f32)
    with jax.named_scope("reduce_down"):
        mixed, _, first_sum = reduce_blocks(near, direct, own, q)

    flat_weight = draft_input_weight.reshape(3 * feature_slice, out_slice)
    pair_weight, third_weight = rounded_weight(flat_weight, first_sum)
    upper_layer = (
        stream_input.astype(f32) + mixed.reshape(steps, rows, feature_slice)
    ).astype(bf16)

    with jax.named_scope("back"):
        back = pick(select[slots:], prior_upper, upper_layer[0])
        chips = [back] + [send(back, along_x(-shift)) for shift in (1, 2, 3)]
        chips = jnp.stack(turned(chips, x))
        others = send(chips, other_core())

    with jax.named_scope("forward"):
        by_replica = gathered.reshape(replicas, -1, 2 * feature_slice)
        stride = by_replica.shape[1]
        pairs, fronts = by_replica[:, : 2 * slots], by_replica[:, 2 * slots :]
        fronts = jnp.concatenate(
            [fronts[:, :, :feature_slice], fronts[:, :, feature_slice:]], axis=1
        )

        def replica_of(shift, half):
            return 2 * ((p + shift) % side) + half

        def pair_product(weight, shift, half):
            rows_of = lax.dynamic_slice_in_dim(
                gathered, replica_of(shift, half) * stride, 2 * slots, axis=0
            )
            return jnp.dot(rows_of, weight, preferred_element_type=f32)

        def third_product(weight, shift, half):
            rows_of = lax.dynamic_slice_in_dim(
                thirds, replica_of(shift, half) * 2 * slots, 2 * slots, axis=0
            )
            return jnp.dot(rows_of, weight, preferred_element_type=f32)

        def piece(total, kind):
            return total.astype(kind).reshape(2, slots, out_slice)

        far_pairs = [pair_product(pair_weight, 2, half) for half in range(2)]
        others, fronts, far_pairs = lax.optimization_barrier((others, fronts, far_pairs))
        backs = jnp.stack(
            [jnp.where(c == 0, chips, others), jnp.where(c == 0, others, chips)], axis=1
        ).reshape(replicas, slots, feature_slice)
        thirds = jnp.concatenate([fronts, backs], axis=1).reshape(-1, feature_slice)
        near = [
            piece(far_pairs[half] + third_product(third_weight, 2, half), bf16)
            for half in range(2)
        ]
        _, pair_weight, third_weight = lax.optimization_barrier(
            (near, pair_weight, third_weight)
        )
        direct = [
            piece(
                pair_product(pair_weight, shift, half) + third_product(third_weight, shift, half),
                bf16,
            )
            for shift in (1, 3)
            for half in range(2)
        ]
        _, pair_weight, third_weight = lax.optimization_barrier(
            (direct, pair_weight, third_weight)
        )
        own = [
            piece(
                pair_product(pair_weight, 0, half) + third_product(third_weight, 0, half), f32
            )
            for half in range(2)
        ]

    with jax.named_scope("reduce_draft"):
        drafted, forwarded, _ = reduce_blocks(near, direct, own, q)

    with jax.named_scope("targets"):
        slot_of = held(slot_of.reshape(1, -1), forwarded)
        select = (slot == slot_of).astype(bf16)
        chosen = pick(select, upper_layer[0], upper_layer[1])
        parity = lax.axis_index("tensor") % 2
        even, odd = chosen[:slots], chosen[slots:]
        posted = [jnp.where((parity + turn) % 2 == 0, even, odd) for turn in range(2)]
        got = []
        for turn in range(2):
            routes = []
            for d in range(replicas * tensors):
                r, t = divmod(d, tensors)
                owner = t // 2
                taken = row_block(owner % cores, 2 * r + (t + turn) % 2)
                routes.append((d, owner * tensors + taken))
            got.append(send(posted[turn], routes))

    with jax.named_scope("norm"):
        front_rows = q % 2 == 0
        targets = jnp.concatenate(
            [jnp.where(front_rows, got[0], got[1]), jnp.where(front_rows, got[1], got[0])],
            axis=1,
        ).astype(f32)
        gain = draft_gain[None, :]
        scaled = gain * drafted
        sums = jnp.stack(
            [
                jnp.sum(drafted * drafted, axis=1),
                jnp.sum(scaled * scaled, axis=1),
                jnp.sum(scaled * targets, axis=1),
            ]
        )
        sums = sums + send(sums, other_core_rows())
        sums = sums + send(sums, along_x(1)) + send(sums, along_x(2)) + send(sums, along_x(3))
        scale = lax.rsqrt(sums[0] / width + epsilon)
        inner = (scale * sums[1] - sums[2]) / slots_all
        error = gain * (scaled * scale[:, None] - targets) / slots_all
        slope = (scale[:, None] * error - drafted * (scale**3 * inner / width)[:, None]).astype(
            bf16
        )

    with jax.named_scope("gather_slope"):
        ring = [slope] + [send(slope, along_second(-shift)) for shift in (1, 2, 3)]
        ring = turned(ring, q)
        upper_half, lower_half = jnp.concatenate(ring[:2]), jnp.concatenate(ring[2:])
        previous_upper = send(upper_half, along_first(1))
        following_lower = send(lower_half, along_first(-1))
        previous_lower = send(lower_half, along_first(1))
        following_upper = send(upper_half, along_first(-1))
        low = send(previous_upper, along_first(1))
        high = send(following_lower, along_first(-1))

    with jax.named_scope("step"):
        features = jnp.concatenate([pairs.reshape(-1, 2 * feature_slice), thirds], axis=1)

        def product(places, slopes):
            inputs = [
                lax.dynamic_slice_in_dim(
                    features, (2 * ((p + shift) % side) + half) * 2 * slots, 2 * slots, axis=0
                )
                for shift, half in places
            ]
            return lax.dot_general(
                jnp.concatenate(inputs),
                jnp.concatenate(slopes),
                (((0,), (0,)), ((), ())),
                preferred_element_type=f32,
            )

        total = product([(0, 0), (0, 1)], [upper_half, lower_half])
        total = lax.optimization_barrier(
            total
            + product(
                [(3, 0), (3, 1), (1, 0), (1, 1)],
                [previous_upper, previous_lower, following_upper, following_lower],
            )
        )
        total = total + product([(2, 0), (2, 1)], [low, high])
        new_weight = (flat_weight - step_rate * total).astype(bf16)
        new_weight = new_weight.reshape(draft_input_weight.shape)
    return (upper_layer, new_weight)


def solution(mesh):
    return jax.shard_map(
        body,
        mesh=mesh,
        in_specs=(
            P(None, "replica", "tensor"),
            P("tensor", None),
            P("tensor", None),
            P(None, "replica", "tensor"),
            P("replica", "tensor"),
            P("replica", "tensor"),
            P("replica", "tensor"),
            P("replica", "tensor"),
            P("replica", "tensor"),
            P("replica"),
            P(None, "tensor", "replica"),
            P("replica"),
        ),
        out_specs=(P(None, "replica", "tensor"), P(None, "tensor", "replica")),
        check_vma=False,
    )
```

```python
import functools

import jax
import jax.numpy as jnp
from jax import lax
from jax.experimental import pallas as pl
from jax.experimental.pallas import tpu as pltpu
from jax.sharding import PartitionSpec as P

step_rate = 8.0
epsilon = 1e-06
side = 4
cores = 2
block_units = 32
f32 = jnp.float32
bf16 = jnp.bfloat16
mesh_axes = ("replica", "tensor")
vmem = 56 * 1024 * 1024


def coordinates(device):
    replica, tensor = divmod(device, side * side)
    x, c = divmod(replica, cores)
    z, y = divmod(tensor, side)
    return x, c, z, y


def device_at(x, c, z, y):
    return ((x % side) * cores + c % cores) * side * side + (z % side) * side + y % side


def moved(target):
    return [(d, target(*coordinates(d))) for d in range(side * cores * side * side)]


def along_first(shift):
    return moved(
        lambda x, c, z, y: device_at(x, c, z + shift * (c == 0), y + shift * (c == 1))
    )


def along_second(shift):
    return moved(
        lambda x, c, z, y: device_at(x, c, z + shift * (c == 1), y + shift * (c == 0))
    )


def along_x(shift):
    return moved(lambda x, c, z, y: device_at(x + shift, c, z, y))


def other_core():
    return moved(lambda x, c, z, y: device_at(x, 1 - c, z, y))


def send(array, pairs):
    return lax.ppermute(array, mesh_axes, pairs)


def plus(*terms):
    return functools.reduce(jnp.add, [term.astype(f32) for term in terms])


def other_core_rows():
    return moved(lambda x, c, z, y: device_at(x, 1 - c, y, z))


def row_block(c, tensor):
    z, y = tensor // side, tensor % side
    return z * side + y if c == 0 else y * side + z


def turned(pieces, places):
    for bit in (1, 2):
        moves = places // bit % 2 == 1
        pieces = [
            jnp.where(moves, pieces[(j - bit) % side], pieces[j]) for j in range(side)
        ]
    return pieces


def place():
    replica, tensor = lax.axis_index("replica"), lax.axis_index("tensor")
    x, c = replica // cores, replica % cores
    z, y = tensor // side, tensor % side
    return x, c, jnp.where(c == 0, z, y), jnp.where(c == 0, y, z)


def down_kernel(blocks_ref, tokens_ref, *refs):
    coded_refs, exponent_refs, pieces = refs[:2], refs[2:4], refs[4:]
    i = pl.program_id(0)
    totals = []
    for coded_ref, exponent_ref in zip(coded_refs, exponent_refs):
        units, columns = coded_ref.shape
        factor = jnp.exp2(exponent_ref[...].astype(f32) - 127.0).astype(bf16)
        weight = coded_ref[...].reshape(units // block_units, block_units, columns)
        weight = (weight * factor[:, None, :]).reshape(units, columns)
        totals.append(jnp.dot(tokens_ref[...], weight, preferred_element_type=f32))
    for k, piece in enumerate(pieces):

        @pl.when(i == k)
        def _():
            for half, total in enumerate(totals):
                piece[half] = total.astype(piece.dtype)


def down_pieces(blocks, tokens, coded_weight, block_exponent, kind):
    rows, units = tokens.shape
    width = coded_weight.shape[1] // (side * side)
    count = blocks.shape[0]

    def column_block(height, half):
        return pl.BlockSpec((height, width), lambda i, blocks: (0, blocks[2 * i + half]))

    return pl.pallas_call(
        down_kernel,
        grid_spec=pltpu.PrefetchScalarGridSpec(
            num_scalar_prefetch=1,
            grid=(count // 2,),
            in_specs=[
                pl.BlockSpec((rows, units), lambda i, blocks: (0, 0)),
                column_block(units, 0),
                column_block(units, 1),
                column_block(units // block_units, 0),
                column_block(units // block_units, 1),
            ],
            out_specs=[
                pl.BlockSpec((2, rows, width), lambda i, blocks: (0, 0, 0))
                for _ in range(count // 2)
            ],
        ),
        out_shape=[jax.ShapeDtypeStruct((2, rows, width), kind)] * (count // 2),
        compiler_params=pltpu.CompilerParams(vmem_limit_bytes=vmem),
        cost_estimate=pl.CostEstimate(
            flops=2 * rows * units * width * count,
            bytes_accessed=3 * units * width * count,
            transcendentals=0,
        ),
        name="down_projection",
    )(blocks, tokens, coded_weight, coded_weight, block_exponent, block_exponent)


def round_kernel(after_ref, upper_ref, lower_ref, out_ref):
    half = upper_ref.shape[0]
    out_ref[:half] = upper_ref[...].astype(bf16)
    out_ref[half:] = lower_ref[...].astype(bf16)


def rounded_layers(wide, layers, start, after):
    rows, columns = wide.shape
    step = rows // 3

    def half_layer(half):
        return pl.BlockSpec((step // 2, columns), lambda i: (2 * (start + i) + half, 0))

    return pl.pallas_call(
        round_kernel,
        grid=(layers,),
        in_specs=[pl.BlockSpec(memory_space=pl.ANY), half_layer(0), half_layer(1)],
        out_specs=pl.BlockSpec((step, columns), lambda i: (i, 0)),
        out_shape=jax.ShapeDtypeStruct((step * layers, columns), bf16),
        compiler_params=pltpu.CompilerParams(vmem_limit_bytes=vmem),
        cost_estimate=pl.CostEstimate(
            flops=layers * step * columns,
            bytes_accessed=6 * layers * step * columns,
            transcendentals=0,
        ),
        name="round_weight",
    )(after, wide, wide)


def together_kernel(first_ref, second_ref, first_out_ref, second_out_ref):
    first_out_ref[...] = first_ref[...]
    second_out_ref[...] = second_ref[...]


def together(first, second):
    return pl.pallas_call(
        together_kernel,
        in_specs=[pl.BlockSpec(memory_space=pltpu.VMEM)] * 2,
        out_specs=[pl.BlockSpec(memory_space=pltpu.VMEM)] * 2,
        out_shape=[jax.ShapeDtypeStruct(a.shape, a.dtype) for a in (first, second)],
        name="together",
    )(first, second)


def reduce_blocks(near, direct, own, q):
    low_right = send(near[0], along_first(1))
    high_left = send(near[1], along_first(-1))
    high_right = send(direct[1], along_first(1))
    low_left = send(direct[2], along_first(-1))
    low_right, high_left = direct[0] + low_right, direct[3] + high_left
    low_right = send(low_right, along_first(1))
    high_left = send(high_left, along_first(-1))
    summed = jnp.concatenate(
        [plus(own[0], low_right, low_left), plus(own[1], high_left, high_right)]
    )
    halved = summed.astype(bf16)

    def at(array, shift):
        return lax.dynamic_index_in_dim(array, (q + shift) % side, 0, keepdims=False)

    parts = [send(at(halved, shift), along_second(shift)) for shift in (1, 3, 2)]
    return plus(at(summed, 0), *parts), summed[0, :8, :128]


def body(
    gated_hidden,
    coded_weight,
    block_exponent,
    stream_input,
    lower_layer,
    middle_layer,
    prior_lower,
    prior_middle,
    prior_upper,
    accepted,
    draft_input_weight,
    draft_gain,
):
    steps, rows, unit_count = gated_hidden.shape
    feature_slice = stream_input.shape[2]
    out_slice = draft_input_weight.shape[2]
    replicas = lax.axis_size("replica")
    tensors = lax.axis_size("tensor")
    width = feature_slice * tensors
    slots_all = steps * rows * replicas
    slots = rows * 3 // 4
    x, c, p, q = place()

    with jax.named_scope("down"):
        tokens = gated_hidden.reshape(steps * rows, unit_count)
        second = jnp.arange(side, dtype=jnp.int32)

        def columns(shift):
            first = (p + shift) % side
            return jnp.where(c == 0, first * side + second, second * side + first)

        near = down_pieces(columns(2), tokens, coded_weight, block_exponent, bf16)
        near, accepted = lax.optimization_barrier((near, accepted))

    with jax.named_scope("select"):
        row = jnp.arange(rows, dtype=jnp.int32)
        before = row[:, None] <= row[None, :]
        first_live = (accepted >= 1).astype(jnp.int32)
        second_live = (accepted >= 2).astype(jnp.int32)
        first_slot = jnp.sum(jnp.where(before, first_live[:, None], 0), axis=0) - 1
        second_slot = 2 * slots - jnp.sum(jnp.where(before, second_live[:, None], 0), axis=0)
        first_slot = jnp.where(first_live == 1, first_slot, -1)
        second_slot = jnp.where(second_live == 1, second_slot, -1)
        slot = jnp.arange(2 * slots, dtype=jnp.int32)[:, None]
        slot_of = jnp.concatenate([first_slot, second_slot])
        select = (slot == slot_of[None, :]).astype(bf16)

        def pick(chosen, first, second):
            return jnp.dot(
                chosen, jnp.concatenate([first, second]), preferred_element_type=f32
            ).astype(bf16)

        pair = pick(
            select,
            jnp.concatenate([prior_lower, prior_middle], axis=1),
            jnp.concatenate([lower_layer, middle_layer], axis=1),
        )
        front = jnp.dot(
            select[:slots, :rows], prior_upper, preferred_element_type=f32
        ).astype(bf16)
        folded = jnp.concatenate([front[: slots // 2], front[slots // 2 :]], axis=1)
        payload = jnp.concatenate([pair, folded])
    gathered = lax.all_gather(payload, "replica", axis=0, tiled=True)

    with jax.named_scope("down"):
        others, payload = lax.optimization_barrier(
            (jnp.concatenate([columns(1), columns(3)]), payload)
        )
        direct = down_pieces(others, tokens, coded_weight, block_exponent, bf16)
        direct, mine = lax.optimization_barrier((direct, columns(0)))
        own = down_pieces(mine, tokens, coded_weight, block_exponent, f32)
    with jax.named_scope("reduce_down"):
        mixed, first_sum = reduce_blocks(near, direct, own, q)

    flat_weight = draft_input_weight.reshape(3 * feature_slice, out_slice)
    pair_weight = rounded_layers(flat_weight, 2, 0, first_sum)
    third_weight = rounded_layers(flat_weight, 1, 2, first_sum)
    upper_layer = (
        stream_input.astype(f32) + mixed.reshape(steps, rows, feature_slice)
    ).astype(bf16)

    with jax.named_scope("back"):
        back = pick(select[slots:], prior_upper, upper_layer[0])
        chips = [back] + [send(back, along_x(-shift)) for shift in (1, 2, 3)]
        chips = jnp.stack(turned(chips, x))
        others = send(chips, other_core())

    with jax.named_scope("targets"):
        chosen = pick(select, upper_layer[0], upper_layer[1])
        parity = lax.axis_index("tensor") % 2
        even, odd = chosen[:slots], chosen[slots:]
        posted = [jnp.where((parity + turn) % 2 == 0, even, odd) for turn in range(2)]
        got = []
        for turn in range(2):
            routes = []
            for d in range(replicas * tensors):
                r, t = divmod(d, tensors)
                owner = t // 2
                taken = row_block(owner % cores, 2 * r + (t + turn) % 2)
                routes.append((d, owner * tensors + taken))
            got.append(send(posted[turn], routes))

    with jax.named_scope("forward"):
        by_replica = gathered.reshape(replicas, -1, 2 * feature_slice)
        stride = by_replica.shape[1]
        pairs, fronts = by_replica[:, : 2 * slots], by_replica[:, 2 * slots :]
        fronts = jnp.concatenate(
            [fronts[:, :, :feature_slice], fronts[:, :, feature_slice:]], axis=1
        )

        def replica_of(shift, half):
            return 2 * ((p + shift) % side) + half

        def pair_product(weight, shift, half):
            rows_of = lax.dynamic_slice_in_dim(
                gathered, replica_of(shift, half) * stride, 2 * slots, axis=0
            )
            return jnp.dot(rows_of, weight, preferred_element_type=f32)

        def third_product(weight, shift, half):
            rows_of = lax.dynamic_slice_in_dim(
                thirds, replica_of(shift, half) * 2 * slots, 2 * slots, axis=0
            )
            return jnp.dot(rows_of, weight, preferred_element_type=f32)

        def piece(total, kind):
            return total.astype(kind).reshape(2, slots, out_slice)

        far_pairs = [
            pair_product(pair_weight, shift, half) for shift in (2, 1, 3) for half in range(2)
        ]
        others, fronts, far_pairs, _ = lax.optimization_barrier(
            (others, fronts, far_pairs, posted)
        )
        backs = jnp.stack(
            [jnp.where(c == 0, chips, others), jnp.where(c == 0, others, chips)], axis=1
        ).reshape(replicas, slots, feature_slice)
        thirds = jnp.concatenate([fronts, backs], axis=1).reshape(-1, feature_slice)
        near = [
            piece(far_pairs[half] + third_product(third_weight, 2, half), bf16)
            for half in range(2)
        ]
        _, got, pair_weight, third_weight = lax.optimization_barrier(
            (near, got, pair_weight, third_weight)
        )
        direct = [
            piece(far_pairs[2 + k] + third_product(third_weight, (1, 3)[k // 2], k % 2), bf16)
            for k in range(4)
        ]
        _, pair_weight, third_weight = lax.optimization_barrier(
            (direct, pair_weight, third_weight)
        )
        own = [
            piece(
                pair_product(pair_weight, 0, half) + third_product(third_weight, 0, half), f32
            )
            for half in range(2)
        ]

    with jax.named_scope("reduce_draft"):
        drafted, _ = reduce_blocks(near, direct, own, q)

    with jax.named_scope("norm"):
        front_rows = q % 2 == 0
        targets = jnp.concatenate(
            [jnp.where(front_rows, got[0], got[1]), jnp.where(front_rows, got[1], got[0])],
            axis=1,
        ).astype(f32)
        gain = draft_gain[None, :]
        scaled = gain * drafted
        sums = jnp.stack(
            [
                jnp.sum(drafted * drafted, axis=1),
                jnp.sum(scaled * scaled, axis=1),
                jnp.sum(scaled * targets, axis=1),
            ]
        )
        sums = sums + send(sums, other_core_rows())
        sums = sums + send(sums, along_x(1)) + send(sums, along_x(2)) + send(sums, along_x(3))
        scale = lax.rsqrt(sums[0] / width + epsilon)
        inner = (scale * sums[1] - sums[2]) / slots_all
        error = gain * (scaled * scale[:, None] - targets) / slots_all
        slope = (scale[:, None] * error - drafted * (scale**3 * inner / width)[:, None]).astype(
            bf16
        )

    with jax.named_scope("gather_slope"):
        ring = [slope] + [send(slope, along_second(-shift)) for shift in (1, 2, 3)]
        ring = turned(ring, q)
        upper_half, lower_half = jnp.concatenate(ring[:2]), jnp.concatenate(ring[2:])
        previous_upper = send(upper_half, along_first(1))
        following_lower = send(lower_half, along_first(-1))
        upper_again, lower_again = together(upper_half, lower_half)
        previous_lower = send(lower_again, along_first(1))
        following_upper = send(upper_again, along_first(-1))
        low = send(previous_upper, along_first(1))
        high = send(following_lower, along_first(-1))

    with jax.named_scope("step"):
        features = jnp.concatenate([pairs.reshape(-1, 2 * feature_slice), thirds], axis=1)

        def product(places, slopes):
            inputs = [
                lax.dynamic_slice_in_dim(
                    features, (2 * ((p + shift) % side) + half) * 2 * slots, 2 * slots, axis=0
                )
                for shift, half in places
            ]
            return lax.dot_general(
                jnp.concatenate(inputs),
                jnp.concatenate(slopes),
                (((0,), (0,)), ((), ())),
                preferred_element_type=f32,
            )

        total = product([(0, 0), (0, 1)], [upper_half, lower_half])
        total = lax.optimization_barrier(
            total
            + product(
                [(3, 0), (3, 1), (1, 0), (1, 1)],
                [previous_upper, previous_lower, following_upper, following_lower],
            )
        )
        total = total + product([(2, 0), (2, 1)], [low, high])
        new_weight = (flat_weight - step_rate * total).astype(bf16)
        new_weight = new_weight.reshape(draft_input_weight.shape)
    return (upper_layer, new_weight)


def solution(mesh):
    return jax.shard_map(
        body,
        mesh=mesh,
        in_specs=(
            P(None, "replica", "tensor"),
            P("tensor", None),
            P("tensor", None),
            P(None, "replica", "tensor"),
            P("replica", "tensor"),
            P("replica", "tensor"),
            P("replica", "tensor"),
            P("replica", "tensor"),
            P("replica", "tensor"),
            P("replica"),
            P(None, "tensor", "replica"),
            P("replica"),
        ),
        out_specs=(P(None, "replica", "tensor"), P(None, "tensor", "replica")),
        check_vma=False,
    )
```

```python
import functools

import jax
import jax.numpy as jnp
from jax import lax
from jax.experimental import pallas as pl
from jax.experimental.pallas import tpu as pltpu
from jax.sharding import PartitionSpec as P

step_rate = 8.0
epsilon = 1e-06
side = 4
cores = 2
block_units = 32
f32 = jnp.float32
bf16 = jnp.bfloat16
mesh_axes = ("replica", "tensor")
vmem = 56 * 1024 * 1024


def coordinates(device):
    replica, tensor = divmod(device, side * side)
    x, c = divmod(replica, cores)
    z, y = divmod(tensor, side)
    return x, c, z, y


def device_at(x, c, z, y):
    return ((x % side) * cores + c % cores) * side * side + (z % side) * side + y % side


def moved(target):
    return [(d, target(*coordinates(d))) for d in range(side * cores * side * side)]


def along_first(shift):
    return moved(
        lambda x, c, z, y: device_at(x, c, z + shift * (c == 0), y + shift * (c == 1))
    )


def along_second(shift):
    return moved(
        lambda x, c, z, y: device_at(x, c, z + shift * (c == 1), y + shift * (c == 0))
    )


def along_x(shift):
    return moved(lambda x, c, z, y: device_at(x + shift, c, z, y))


def other_core():
    return moved(lambda x, c, z, y: device_at(x, 1 - c, z, y))


def send(array, pairs):
    return lax.ppermute(array, mesh_axes, pairs)


def plus(*terms):
    return functools.reduce(jnp.add, [term.astype(f32) for term in terms])


def other_core_rows():
    return moved(lambda x, c, z, y: device_at(x, 1 - c, y, z))


def row_block(c, tensor):
    z, y = tensor // side, tensor % side
    return z * side + y if c == 0 else y * side + z


def turned(pieces, places):
    for bit in (1, 2):
        moves = places // bit % 2 == 1
        pieces = [
            jnp.where(moves, pieces[(j - bit) % side], pieces[j]) for j in range(side)
        ]
    return pieces


def place():
    replica, tensor = lax.axis_index("replica"), lax.axis_index("tensor")
    x, c = replica // cores, replica % cores
    z, y = tensor // side, tensor % side
    return x, c, jnp.where(c == 0, z, y), jnp.where(c == 0, y, z)


def down_kernel(blocks_ref, tokens_ref, *refs):
    coded_refs, exponent_refs, pieces = refs[:2], refs[2:4], refs[4:]
    i = pl.program_id(0)
    totals = []
    for coded_ref, exponent_ref in zip(coded_refs, exponent_refs):
        units, columns = coded_ref.shape
        factor = jnp.exp2(exponent_ref[...].astype(f32) - 127.0).astype(bf16)
        weight = coded_ref[...].reshape(units // block_units, block_units, columns)
        weight = (weight * factor[:, None, :]).reshape(units, columns)
        totals.append(jnp.dot(tokens_ref[...], weight, preferred_element_type=f32))
    for k, piece in enumerate(pieces):

        @pl.when(i == k)
        def _():
            for half, total in enumerate(totals):
                piece[half] = total.astype(piece.dtype)


def down_pieces(blocks, tokens, coded_weight, block_exponent, kind):
    rows, units = tokens.shape
    width = coded_weight.shape[1] // (side * side)
    count = blocks.shape[0]

    def column_block(height, half):
        return pl.BlockSpec((height, width), lambda i, blocks: (0, blocks[2 * i + half]))

    return pl.pallas_call(
        down_kernel,
        grid_spec=pltpu.PrefetchScalarGridSpec(
            num_scalar_prefetch=1,
            grid=(count // 2,),
            in_specs=[
                pl.BlockSpec((rows, units), lambda i, blocks: (0, 0)),
                column_block(units, 0),
                column_block(units, 1),
                column_block(units // block_units, 0),
                column_block(units // block_units, 1),
            ],
            out_specs=[
                pl.BlockSpec((2, rows, width), lambda i, blocks: (0, 0, 0))
                for _ in range(count // 2)
            ],
        ),
        out_shape=[jax.ShapeDtypeStruct((2, rows, width), kind)] * (count // 2),
        compiler_params=pltpu.CompilerParams(vmem_limit_bytes=vmem),
        cost_estimate=pl.CostEstimate(
            flops=2 * rows * units * width * count,
            bytes_accessed=3 * units * width * count,
            transcendentals=0,
        ),
        name="down_projection",
    )(blocks, tokens, coded_weight, coded_weight, block_exponent, block_exponent)


def round_kernel(after_ref, upper_ref, lower_ref, out_ref):
    half = upper_ref.shape[0]
    out_ref[:half] = upper_ref[...].astype(bf16)
    out_ref[half:] = lower_ref[...].astype(bf16)


def rounded(wide, after):
    rows, columns = wide.shape
    layers = 3
    step = rows // layers

    def half_layer(half):
        return pl.BlockSpec((step // 2, columns), lambda i: (2 * i + half, 0))

    return pl.pallas_call(
        round_kernel,
        grid=(layers,),
        in_specs=[pl.BlockSpec(memory_space=pl.ANY), half_layer(0), half_layer(1)],
        out_specs=pl.BlockSpec((step, columns), lambda i: (i, 0)),
        out_shape=jax.ShapeDtypeStruct((step * layers, columns), bf16),
        compiler_params=pltpu.CompilerParams(vmem_limit_bytes=vmem),
        cost_estimate=pl.CostEstimate(
            flops=layers * step * columns,
            bytes_accessed=6 * layers * step * columns,
            transcendentals=0,
        ),
        name="round_weight",
    )(after, wide, wide)


def held_kernel(after_ref, value_ref, out_ref):
    out_ref[...] = value_ref[...]


def held(value, after):
    return pl.pallas_call(
        held_kernel,
        in_specs=[pl.BlockSpec(memory_space=pl.ANY), pl.BlockSpec(memory_space=pltpu.VMEM)],
        out_specs=pl.BlockSpec(memory_space=pltpu.VMEM),
        out_shape=jax.ShapeDtypeStruct((8, 128), jnp.int32),
        name="held",
    )(after, jnp.full((8, 128), value, jnp.int32))[0, 0]


def together_kernel(first_ref, second_ref, first_out_ref, second_out_ref):
    first_out_ref[...] = first_ref[...]
    second_out_ref[...] = second_ref[...]


def together(first, second):
    return pl.pallas_call(
        together_kernel,
        in_specs=[pl.BlockSpec(memory_space=pltpu.VMEM)] * 2,
        out_specs=[pl.BlockSpec(memory_space=pltpu.VMEM)] * 2,
        out_shape=[jax.ShapeDtypeStruct(a.shape, a.dtype) for a in (first, second)],
        name="together",
    )(first, second)


def reduce_blocks(near, direct, own, q, after=None):
    low_right = send(near[0], along_first(1))
    high_left = send(near[1], along_first(-1))
    high_right = send(direct[1], along_first(1))
    low_left = send(direct[2], along_first(-1))
    low_right, high_left = direct[0] + low_right, direct[3] + high_left
    low_right = send(low_right, along_first(1))
    high_left = send(high_left, along_first(-1))
    summed = jnp.concatenate(
        [plus(own[0], low_right, low_left), plus(own[1], high_left, high_right)]
    )
    halved = summed.astype(bf16)

    def at(array, index):
        return lax.dynamic_index_in_dim(array, index % side, 0, keepdims=False)

    parts = [send(at(halved, q + shift), along_second(shift)) for shift in (1, 3, 2)]
    return plus(at(summed, q if after is None else held(q, after)), *parts)


def body(
    gated_hidden,
    coded_weight,
    block_exponent,
    stream_input,
    lower_layer,
    middle_layer,
    prior_lower,
    prior_middle,
    prior_upper,
    accepted,
    draft_input_weight,
    draft_gain,
):
    steps, rows, unit_count = gated_hidden.shape
    feature_slice = stream_input.shape[2]
    out_slice = draft_input_weight.shape[2]
    replicas = lax.axis_size("replica")
    tensors = lax.axis_size("tensor")
    width = feature_slice * tensors
    slots_all = steps * rows * replicas
    slots = rows * 3 // 4
    x, c, p, q = place()

    with jax.named_scope("down"):
        tokens = gated_hidden.reshape(steps * rows, unit_count)
        second = jnp.arange(side, dtype=jnp.int32)

        def columns(shift):
            first = (p + shift) % side
            return jnp.where(c == 0, first * side + second, second * side + first)

        near = down_pieces(columns(2), tokens, coded_weight, block_exponent, bf16)
        near, accepted = lax.optimization_barrier((near, accepted))

    with jax.named_scope("select"):
        row = jnp.arange(rows, dtype=jnp.int32)
        before = row[:, None] <= row[None, :]
        first_live = (accepted >= 1).astype(jnp.int32)
        second_live = (accepted >= 2).astype(jnp.int32)
        first_slot = jnp.sum(jnp.where(before, first_live[:, None], 0), axis=0) - 1
        second_slot = 2 * slots - jnp.sum(jnp.where(before, second_live[:, None], 0), axis=0)
        first_slot = jnp.where(first_live == 1, first_slot, -1)
        second_slot = jnp.where(second_live == 1, second_slot, -1)
        slot = jnp.arange(2 * slots, dtype=jnp.int32)[:, None]
        slot_of = jnp.concatenate([first_slot, second_slot])
        select = (slot == slot_of[None, :]).astype(bf16)

        def pick(chosen, first, second):
            return jnp.dot(
                chosen, jnp.concatenate([first, second]), preferred_element_type=f32
            ).astype(bf16)

        pair = pick(
            select,
            jnp.concatenate([prior_lower, prior_middle], axis=1),
            jnp.concatenate([lower_layer, middle_layer], axis=1),
        )
        front = jnp.dot(
            select[:slots, :rows], prior_upper, preferred_element_type=f32
        ).astype(bf16)
        folded = jnp.concatenate([front[: slots // 2], front[slots // 2 :]], axis=1)
        payload = jnp.concatenate([pair, folded])
    gathered = lax.all_gather(payload, "replica", axis=0, tiled=True)

    with jax.named_scope("down"):
        others, payload = lax.optimization_barrier(
            (jnp.concatenate([columns(1), columns(3)]), payload)
        )
        direct = down_pieces(others, tokens, coded_weight, block_exponent, bf16)
        direct, mine = lax.optimization_barrier((direct, columns(0)))
        own = down_pieces(mine, tokens, coded_weight, block_exponent, f32)
    flat_weight = draft_input_weight.reshape(3 * feature_slice, out_slice)
    narrow_weight = rounded(flat_weight, own[0])
    third_weight = narrow_weight[2 * feature_slice :]
    with jax.named_scope("early"):
        early = jnp.dot(
            gathered, narrow_weight[: 2 * feature_slice], preferred_element_type=f32
        )
    with jax.named_scope("reduce_down"):
        mixed = reduce_blocks(near, direct, own, q, early[:8, :128])
    upper_layer = (
        stream_input.astype(f32) + mixed.reshape(steps, rows, feature_slice)
    ).astype(bf16)

    with jax.named_scope("back"):
        back = pick(select[slots:], prior_upper, upper_layer[0])
        chips = [back] + [send(back, along_x(-shift)) for shift in (1, 2, 3)]
        chips = jnp.stack(turned(chips, x))
        others = send(chips, other_core())

    with jax.named_scope("targets"):
        chosen = pick(select, upper_layer[0], upper_layer[1])
        parity = lax.axis_index("tensor") % 2
        even, odd = chosen[:slots], chosen[slots:]
        posted = [jnp.where((parity + turn) % 2 == 0, even, odd) for turn in range(2)]
        got = []
        for turn in range(2):
            routes = []
            for d in range(replicas * tensors):
                r, t = divmod(d, tensors)
                owner = t // 2
                taken = row_block(owner % cores, 2 * r + (t + turn) % 2)
                routes.append((d, owner * tensors + taken))
            got.append(send(posted[turn], routes))

    with jax.named_scope("forward"):
        by_replica = gathered.reshape(replicas, -1, 2 * feature_slice)
        stride = by_replica.shape[1]
        pairs, fronts = by_replica[:, : 2 * slots], by_replica[:, 2 * slots :]
        fronts = jnp.concatenate(
            [fronts[:, :, :feature_slice], fronts[:, :, feature_slice:]], axis=1
        )

        def replica_of(shift, half):
            return 2 * ((p + shift) % side) + half

        def pair_product(shift, half):
            return lax.dynamic_slice_in_dim(
                early, replica_of(shift, half) * stride, 2 * slots, axis=0
            )

        def third_product(weight, shift, half):
            rows_of = lax.dynamic_slice_in_dim(
                thirds, replica_of(shift, half) * 2 * slots, 2 * slots, axis=0
            )
            return jnp.dot(rows_of, weight, preferred_element_type=f32)

        def piece(total, kind):
            return total.astype(kind).reshape(2, slots, out_slice)

        others, fronts, _ = lax.optimization_barrier((others, fronts, posted))
        backs = jnp.stack(
            [jnp.where(c == 0, chips, others), jnp.where(c == 0, others, chips)], axis=1
        ).reshape(replicas, slots, feature_slice)
        thirds = jnp.concatenate([fronts, backs], axis=1).reshape(-1, feature_slice)
        near = [
            piece(pair_product(2, half) + third_product(third_weight, 2, half), bf16)
            for half in range(2)
        ]
        _, got, third_weight = lax.optimization_barrier((near, got, third_weight))
        direct = [
            piece(pair_product(shift, half) + third_product(third_weight, shift, half), bf16)
            for shift in (1, 3)
            for half in range(2)
        ]
        _, third_weight = lax.optimization_barrier((direct, third_weight))
        own = [
            piece(pair_product(0, half) + third_product(third_weight, 0, half), f32)
            for half in range(2)
        ]

    with jax.named_scope("reduce_draft"):
        drafted = reduce_blocks(near, direct, own, q)

    with jax.named_scope("norm"):
        front_rows = q % 2 == 0
        targets = jnp.concatenate(
            [jnp.where(front_rows, got[0], got[1]), jnp.where(front_rows, got[1], got[0])],
            axis=1,
        ).astype(f32)
        gain = draft_gain[None, :]
        scaled = gain * drafted
        sums = jnp.stack(
            [
                jnp.sum(drafted * drafted, axis=1),
                jnp.sum(scaled * scaled, axis=1),
                jnp.sum(scaled * targets, axis=1),
            ]
        )
        sums = sums + send(sums, other_core_rows())
        sums = sums + send(sums, along_x(1)) + send(sums, along_x(2)) + send(sums, along_x(3))
        scale = lax.rsqrt(sums[0] / width + epsilon)
        inner = (scale * sums[1] - sums[2]) / slots_all
        error = gain * (scaled * scale[:, None] - targets) / slots_all
        slope = (scale[:, None] * error - drafted * (scale**3 * inner / width)[:, None]).astype(
            bf16
        )

    with jax.named_scope("gather_slope"):
        ring = [slope] + [send(slope, along_second(-shift)) for shift in (1, 2, 3)]
        ring = turned(ring, q)
        upper_half, lower_half = jnp.concatenate(ring[:2]), jnp.concatenate(ring[2:])
        previous_upper = send(upper_half, along_first(1))
        following_lower = send(lower_half, along_first(-1))
        upper_again, lower_again = together(upper_half, lower_half)
        previous_lower = send(lower_again, along_first(1))
        following_upper = send(upper_again, along_first(-1))
        low = send(previous_upper, along_first(1))
        high = send(following_lower, along_first(-1))

    with jax.named_scope("step"):
        features = jnp.concatenate([pairs.reshape(-1, 2 * feature_slice), thirds], axis=1)

        def product(places, slopes):
            inputs = [
                lax.dynamic_slice_in_dim(
                    features, (2 * ((p + shift) % side) + half) * 2 * slots, 2 * slots, axis=0
                )
                for shift, half in places
            ]
            return lax.dot_general(
                jnp.concatenate(inputs),
                jnp.concatenate(slopes),
                (((0,), (0,)), ((), ())),
                preferred_element_type=f32,
            )

        updated = lax.optimization_barrier(
            flat_weight - step_rate * product([(0, 0), (0, 1)], [upper_half, lower_half])
        )
        updated = lax.optimization_barrier(
            updated
            - step_rate
            * product(
                [(3, 0), (3, 1), (1, 0), (1, 1)],
                [previous_upper, previous_lower, following_upper, following_lower],
            )
        )
        updated = updated - step_rate * product([(2, 0), (2, 1)], [low, high])
        new_weight = updated.astype(bf16).reshape(draft_input_weight.shape)
    return (upper_layer, new_weight)


def solution(mesh):
    return jax.shard_map(
        body,
        mesh=mesh,
        in_specs=(
            P(None, "replica", "tensor"),
            P("tensor", None),
            P("tensor", None),
            P(None, "replica", "tensor"),
            P("replica", "tensor"),
            P("replica", "tensor"),
            P("replica", "tensor"),
            P("replica", "tensor"),
            P("replica", "tensor"),
            P("replica"),
            P(None, "tensor", "replica"),
            P("replica"),
        ),
        out_specs=(P(None, "replica", "tensor"), P(None, "tensor", "replica")),
        check_vma=False,
    )
```

```python
import functools

import jax
import jax.numpy as jnp
from jax import lax
from jax.experimental import pallas as pl
from jax.experimental.pallas import tpu as pltpu
from jax.sharding import PartitionSpec as P

step_rate = 8.0
epsilon = 1e-06
side = 4
cores = 2
block_units = 32
f32 = jnp.float32
bf16 = jnp.bfloat16
mesh_axes = ("replica", "tensor")
vmem = 56 * 1024 * 1024


def coordinates(device):
    replica, tensor = divmod(device, side * side)
    x, c = divmod(replica, cores)
    z, y = divmod(tensor, side)
    return x, c, z, y


def device_at(x, c, z, y):
    return ((x % side) * cores + c % cores) * side * side + (z % side) * side + y % side


def moved(target):
    return [(d, target(*coordinates(d))) for d in range(side * cores * side * side)]


def along_first(shift):
    return moved(
        lambda x, c, z, y: device_at(x, c, z + shift * (c == 0), y + shift * (c == 1))
    )


def along_second(shift):
    return moved(
        lambda x, c, z, y: device_at(x, c, z + shift * (c == 1), y + shift * (c == 0))
    )


def along_x(shift):
    return moved(lambda x, c, z, y: device_at(x + shift, c, z, y))


def other_core():
    return moved(lambda x, c, z, y: device_at(x, 1 - c, z, y))


def send(array, pairs):
    return lax.ppermute(array, mesh_axes, pairs)


def plus(*terms):
    return functools.reduce(jnp.add, [term.astype(f32) for term in terms])


def other_core_rows():
    return moved(lambda x, c, z, y: device_at(x, 1 - c, y, z))


def row_block(c, tensor):
    z, y = tensor // side, tensor % side
    return z * side + y if c == 0 else y * side + z


def turned(pieces, places):
    for bit in (1, 2):
        moves = places // bit % 2 == 1
        pieces = [
            jnp.where(moves, pieces[(j - bit) % side], pieces[j]) for j in range(side)
        ]
    return pieces


def place():
    replica, tensor = lax.axis_index("replica"), lax.axis_index("tensor")
    x, c = replica // cores, replica % cores
    z, y = tensor // side, tensor % side
    return x, c, jnp.where(c == 0, z, y), jnp.where(c == 0, y, z)


def down_kernel(blocks_ref, tokens_ref, *refs):
    coded_refs, exponent_refs, pieces = refs[:2], refs[2:4], refs[4:]
    i = pl.program_id(0)
    totals = []
    for coded_ref, exponent_ref in zip(coded_refs, exponent_refs):
        units, columns = coded_ref.shape
        factor = jnp.exp2(exponent_ref[...].astype(f32) - 127.0).astype(bf16)
        weight = coded_ref[...].reshape(units // block_units, block_units, columns)
        weight = (weight * factor[:, None, :]).reshape(units, columns)
        totals.append(jnp.dot(tokens_ref[...], weight, preferred_element_type=f32))
    for k, piece in enumerate(pieces):

        @pl.when(i == k)
        def _():
            for half, total in enumerate(totals):
                piece[half] = total.astype(piece.dtype)


def down_pieces(blocks, tokens, coded_weight, block_exponent, kind):
    rows, units = tokens.shape
    width = coded_weight.shape[1] // (side * side)
    count = blocks.shape[0]

    def column_block(height, half):
        return pl.BlockSpec((height, width), lambda i, blocks: (0, blocks[2 * i + half]))

    return pl.pallas_call(
        down_kernel,
        grid_spec=pltpu.PrefetchScalarGridSpec(
            num_scalar_prefetch=1,
            grid=(count // 2,),
            in_specs=[
                pl.BlockSpec((rows, units), lambda i, blocks: (0, 0)),
                column_block(units, 0),
                column_block(units, 1),
                column_block(units // block_units, 0),
                column_block(units // block_units, 1),
            ],
            out_specs=[
                pl.BlockSpec((2, rows, width), lambda i, blocks: (0, 0, 0))
                for _ in range(count // 2)
            ],
        ),
        out_shape=[jax.ShapeDtypeStruct((2, rows, width), kind)] * (count // 2),
        compiler_params=pltpu.CompilerParams(vmem_limit_bytes=vmem),
        cost_estimate=pl.CostEstimate(
            flops=2 * rows * units * width * count,
            bytes_accessed=3 * units * width * count,
            transcendentals=0,
        ),
        name="down_projection",
    )(blocks, tokens, coded_weight, coded_weight, block_exponent, block_exponent)


def round_kernel(after_ref, upper_ref, lower_ref, out_ref):
    half = upper_ref.shape[0]
    out_ref[:half] = upper_ref[...].astype(bf16)
    out_ref[half:] = lower_ref[...].astype(bf16)


def rounded_pair(wide, after):
    rows, columns = wide.shape
    layers, step = 2, rows // 3

    def half_layer(half):
        return pl.BlockSpec((step // 2, columns), lambda i: (2 * i + half, 0))

    return pl.pallas_call(
        round_kernel,
        grid=(layers,),
        in_specs=[pl.BlockSpec(memory_space=pl.ANY), half_layer(0), half_layer(1)],
        out_specs=pl.BlockSpec((step, columns), lambda i: (i, 0)),
        out_shape=jax.ShapeDtypeStruct((step * layers, columns), bf16),
        compiler_params=pltpu.CompilerParams(vmem_limit_bytes=vmem),
        cost_estimate=pl.CostEstimate(
            flops=layers * step * columns,
            bytes_accessed=6 * layers * step * columns,
            transcendentals=0,
        ),
        name="round_weight",
    )(after, wide, wide)


def reduce_blocks(near, direct, own, q):
    low_right = send(near[0], along_first(1))
    high_left = send(near[1], along_first(-1))
    high_right = send(direct[1], along_first(1))
    low_left = send(direct[2], along_first(-1))
    low_right, high_left = direct[0] + low_right, direct[3] + high_left
    low_right = send(low_right, along_first(1))
    high_left = send(high_left, along_first(-1))
    summed = jnp.concatenate(
        [plus(own[0], low_right, low_left), plus(own[1], high_left, high_right)]
    )
    halved = summed.astype(bf16)

    def at(array, shift):
        return lax.dynamic_index_in_dim(array, (q + shift) % side, 0, keepdims=False)

    parts = [send(at(halved, shift), along_second(shift)) for shift in (1, 3, 2)]
    return plus(at(summed, 0), *parts), summed[0, :8, :128]


def body(
    gated_hidden,
    coded_weight,
    block_exponent,
    stream_input,
    lower_layer,
    middle_layer,
    prior_lower,
    prior_middle,
    prior_upper,
    accepted,
    draft_input_weight,
    draft_gain,
):
    steps, rows, unit_count = gated_hidden.shape
    feature_slice = stream_input.shape[2]
    out_slice = draft_input_weight.shape[2]
    replicas = lax.axis_size("replica")
    tensors = lax.axis_size("tensor")
    width = feature_slice * tensors
    slots_all = steps * rows * replicas
    slots = rows * 3 // 4
    x, c, p, q = place()

    with jax.named_scope("down"):
        tokens = gated_hidden.reshape(steps * rows, unit_count)
        second = jnp.arange(side, dtype=jnp.int32)

        def columns(shift):
            first = (p + shift) % side
            return jnp.where(c == 0, first * side + second, second * side + first)

        near = down_pieces(columns(2), tokens, coded_weight, block_exponent, bf16)
        near, accepted = lax.optimization_barrier((near, accepted))

    with jax.named_scope("select"):
        row = jnp.arange(rows, dtype=jnp.int32)
        before = row[:, None] <= row[None, :]
        first_live = (accepted >= 1).astype(jnp.int32)
        second_live = (accepted >= 2).astype(jnp.int32)
        first_slot = jnp.sum(jnp.where(before, first_live[:, None], 0), axis=0) - 1
        second_slot = 2 * slots - jnp.sum(jnp.where(before, second_live[:, None], 0), axis=0)
        first_slot = jnp.where(first_live == 1, first_slot, -1)
        second_slot = jnp.where(second_live == 1, second_slot, -1)
        slot = jnp.arange(2 * slots, dtype=jnp.int32)[:, None]
        slot_of = jnp.concatenate([first_slot, second_slot])
        select = (slot == slot_of[None, :]).astype(bf16)

        def pick(chosen, first, second):
            return jnp.dot(
                chosen, jnp.concatenate([first, second]), preferred_element_type=f32
            ).astype(bf16)

        pair = pick(
            select,
            jnp.concatenate([prior_lower, prior_middle], axis=1),
            jnp.concatenate([lower_layer, middle_layer], axis=1),
        )
        front = jnp.dot(
            select[:slots, :rows], prior_upper, preferred_element_type=f32
        ).astype(bf16)
        folded = jnp.concatenate([front[: slots // 2], front[slots // 2 :]], axis=1)
        payload = jnp.concatenate([pair, folded])
    gathered = lax.all_gather(payload, "replica", axis=0, tiled=True)

    with jax.named_scope("down"):
        others, payload = lax.optimization_barrier(
            (jnp.concatenate([columns(1), columns(3)]), payload)
        )
        direct = down_pieces(others, tokens, coded_weight, block_exponent, bf16)
        direct, mine = lax.optimization_barrier((direct, columns(0)))
        own = down_pieces(mine, tokens, coded_weight, block_exponent, f32)
    with jax.named_scope("reduce_down"):
        mixed, first_sum = reduce_blocks(near, direct, own, q)

    flat_weight = draft_input_weight.reshape(3 * feature_slice, out_slice)
    pair_weight = rounded_pair(flat_weight, first_sum)
    third_weight = draft_input_weight[2].astype(bf16)
    upper_layer = (
        stream_input.astype(f32) + mixed.reshape(steps, rows, feature_slice)
    ).astype(bf16)

    with jax.named_scope("back"):
        back = pick(select[slots:], prior_upper, upper_layer[0])
        chips = [back] + [send(back, along_x(-shift)) for shift in (1, 2, 3)]
        chips = jnp.stack(turned(chips, x))
        others = send(chips, other_core())

    with jax.named_scope("targets"):
        chosen = pick(select, upper_layer[0], upper_layer[1])
        parity = lax.axis_index("tensor") % 2
        even, odd = chosen[:slots], chosen[slots:]
        posted = [jnp.where((parity + turn) % 2 == 0, even, odd) for turn in range(2)]
        got = []
        for turn in range(2):
            routes = []
            for d in range(replicas * tensors):
                r, t = divmod(d, tensors)
                owner = t // 2
                taken = row_block(owner % cores, 2 * r + (t + turn) % 2)
                routes.append((d, owner * tensors + taken))
            got.append(send(posted[turn], routes))

    with jax.named_scope("forward"):
        by_replica = gathered.reshape(replicas, -1, 2 * feature_slice)
        stride = by_replica.shape[1]
        pairs, fronts = by_replica[:, : 2 * slots], by_replica[:, 2 * slots :]
        fronts = jnp.concatenate(
            [fronts[:, :, :feature_slice], fronts[:, :, feature_slice:]], axis=1
        )

        def replica_of(shift, half):
            return 2 * ((p + shift) % side) + half

        def pair_product(weight, shift, half):
            rows_of = lax.dynamic_slice_in_dim(
                gathered, replica_of(shift, half) * stride, 2 * slots, axis=0
            )
            return jnp.dot(rows_of, weight, preferred_element_type=f32)

        def third_product(weight, shift, half):
            rows_of = lax.dynamic_slice_in_dim(
                thirds, replica_of(shift, half) * 2 * slots, 2 * slots, axis=0
            )
            return jnp.dot(rows_of, weight, preferred_element_type=f32)

        def piece(total, kind):
            return total.astype(kind).reshape(2, slots, out_slice)

        far_pairs = [pair_product(pair_weight, 2, half) for half in range(2)]
        others, fronts, far_pairs, _ = lax.optimization_barrier(
            (others, fronts, far_pairs, posted)
        )
        backs = jnp.stack(
            [jnp.where(c == 0, chips, others), jnp.where(c == 0, others, chips)], axis=1
        ).reshape(replicas, slots, feature_slice)
        thirds = jnp.concatenate([fronts, backs], axis=1).reshape(-1, feature_slice)
        near = [
            piece(far_pairs[half] + third_product(third_weight, 2, half), bf16)
            for half in range(2)
        ]
        _, got, pair_weight, third_weight = lax.optimization_barrier(
            (near, got, pair_weight, third_weight)
        )
        direct = [
            piece(
                pair_product(pair_weight, shift, half) + third_product(third_weight, shift, half),
                bf16,
            )
            for shift in (1, 3)
            for half in range(2)
        ]
        _, pair_weight, third_weight = lax.optimization_barrier(
            (direct, pair_weight, third_weight)
        )
        own = [
            piece(
                pair_product(pair_weight, 0, half) + third_product(third_weight, 0, half), f32
            )
            for half in range(2)
        ]

    with jax.named_scope("reduce_draft"):
        drafted, _ = reduce_blocks(near, direct, own, q)

    with jax.named_scope("norm"):
        front_rows = q % 2 == 0
        targets = jnp.concatenate(
            [jnp.where(front_rows, got[0], got[1]), jnp.where(front_rows, got[1], got[0])],
            axis=1,
        ).astype(f32)
        gain = draft_gain[None, :]
        scaled = gain * drafted
        sums = jnp.stack(
            [
                jnp.sum(drafted * drafted, axis=1),
                jnp.sum(scaled * scaled, axis=1),
                jnp.sum(scaled * targets, axis=1),
            ]
        )
        sums = sums + send(sums, other_core_rows())
        sums = sums + send(sums, along_x(1)) + send(sums, along_x(2)) + send(sums, along_x(3))
        scale = lax.rsqrt(sums[0] / width + epsilon)
        inner = (scale * sums[1] - sums[2]) / slots_all
        error = gain * (scaled * scale[:, None] - targets) / slots_all
        slope = (scale[:, None] * error - drafted * (scale**3 * inner / width)[:, None]).astype(
            bf16
        )

    with jax.named_scope("gather_slope"):
        ring = [slope] + [send(slope, along_second(-shift)) for shift in (1, 2, 3)]
        ring = turned(ring, q)
        upper_half, lower_half = jnp.concatenate(ring[:2]), jnp.concatenate(ring[2:])
        previous_upper = send(upper_half, along_first(1))
        following_upper = send(upper_half, along_first(-1))
        previous_lower = send(lower_half, along_first(1))
        following_lower = send(lower_half, along_first(-1))
        upper, lower = [
            lax.optimization_barrier(
                jnp.concatenate(
                    [
                        send(previous[:slots], along_first(1)),
                        send(following[slots:], along_first(-1)),
                    ]
                )
            )
            for previous, following in (
                (previous_upper, following_upper),
                (previous_lower, following_lower),
            )
        ]

    with jax.named_scope("step"):
        features = jnp.concatenate([pairs.reshape(-1, 2 * feature_slice), thirds], axis=1)

        def product(places, slopes):
            inputs = [
                lax.dynamic_slice_in_dim(
                    features, (2 * ((p + shift) % side) + half) * 2 * slots, 2 * slots, axis=0
                )
                for shift, half in places
            ]
            return lax.dot_general(
                jnp.concatenate(inputs),
                jnp.concatenate(slopes),
                (((0,), (0,)), ((), ())),
                preferred_element_type=f32,
            )

        total = product([(0, 0), (0, 1)], [upper_half, lower_half])
        total = lax.optimization_barrier(
            total
            + product(
                [(3, 0), (3, 1), (1, 0), (1, 1)],
                [previous_upper, previous_lower, following_upper, following_lower],
            )
        )
        total = total + product([(2, 0), (2, 1)], [upper, lower])
        new_weight = (flat_weight - step_rate * total).astype(bf16)
        new_weight = new_weight.reshape(draft_input_weight.shape)
    return (upper_layer, new_weight)


def solution(mesh):
    return jax.shard_map(
        body,
        mesh=mesh,
        in_specs=(
            P(None, "replica", "tensor"),
            P("tensor", None),
            P("tensor", None),
            P(None, "replica", "tensor"),
            P("replica", "tensor"),
            P("replica", "tensor"),
            P("replica", "tensor"),
            P("replica", "tensor"),
            P("replica", "tensor"),
            P("replica"),
            P(None, "tensor", "replica"),
            P("replica"),
        ),
        out_specs=(P(None, "replica", "tensor"), P(None, "tensor", "replica")),
        check_vma=False,
    )
```

```python
import functools

import jax
import jax.numpy as jnp
from jax import lax
from jax.experimental import pallas as pl
from jax.experimental.pallas import tpu as pltpu
from jax.sharding import PartitionSpec as P

step_rate = 8.0
epsilon = 1e-06
side = 4
cores = 2
block_units = 32
f32 = jnp.float32
bf16 = jnp.bfloat16
mesh_axes = ("replica", "tensor")
vmem = 56 * 1024 * 1024


def coordinates(device):
    replica, tensor = divmod(device, side * side)
    x, c = divmod(replica, cores)
    z, y = divmod(tensor, side)
    return x, c, z, y


def device_at(x, c, z, y):
    return ((x % side) * cores + c % cores) * side * side + (z % side) * side + y % side


def moved(target):
    return [(d, target(*coordinates(d))) for d in range(side * cores * side * side)]


def along_first(shift):
    return moved(
        lambda x, c, z, y: device_at(x, c, z + shift * (c == 0), y + shift * (c == 1))
    )


def along_second(shift):
    return moved(
        lambda x, c, z, y: device_at(x, c, z + shift * (c == 1), y + shift * (c == 0))
    )


def along_x(shift):
    return moved(lambda x, c, z, y: device_at(x + shift, c, z, y))


def other_core():
    return moved(lambda x, c, z, y: device_at(x, 1 - c, z, y))


def send(array, pairs):
    return lax.ppermute(array, mesh_axes, pairs)


def plus(*terms):
    return functools.reduce(jnp.add, [term.astype(f32) for term in terms])


def other_core_rows():
    return moved(lambda x, c, z, y: device_at(x, 1 - c, y, z))


def row_block(c, tensor):
    z, y = tensor // side, tensor % side
    return z * side + y if c == 0 else y * side + z


def turned(pieces, places):
    for bit in (1, 2):
        moves = places // bit % 2 == 1
        pieces = [
            jnp.where(moves, pieces[(j - bit) % side], pieces[j]) for j in range(side)
        ]
    return pieces


def place():
    replica, tensor = lax.axis_index("replica"), lax.axis_index("tensor")
    x, c = replica // cores, replica % cores
    z, y = tensor // side, tensor % side
    return x, c, jnp.where(c == 0, z, y), jnp.where(c == 0, y, z)


def down_kernel(blocks_ref, tokens_ref, *refs):
    coded_refs, exponent_refs, pieces = refs[:2], refs[2:4], refs[4:]
    i = pl.program_id(0)
    totals = []
    for coded_ref, exponent_ref in zip(coded_refs, exponent_refs):
        units, columns = coded_ref.shape
        factor = jnp.exp2(exponent_ref[...].astype(f32) - 127.0).astype(bf16)
        weight = coded_ref[...].reshape(units // block_units, block_units, columns)
        weight = (weight * factor[:, None, :]).reshape(units, columns)
        totals.append(jnp.dot(tokens_ref[...], weight, preferred_element_type=f32))
    for k, piece in enumerate(pieces):

        @pl.when(i == k)
        def _():
            for half, total in enumerate(totals):
                piece[half] = total.astype(piece.dtype)


def down_pieces(blocks, tokens, coded_weight, block_exponent, kind):
    rows, units = tokens.shape
    width = coded_weight.shape[1] // (side * side)
    count = blocks.shape[0]

    def column_block(height, half):
        return pl.BlockSpec((height, width), lambda i, blocks: (0, blocks[2 * i + half]))

    return pl.pallas_call(
        down_kernel,
        grid_spec=pltpu.PrefetchScalarGridSpec(
            num_scalar_prefetch=1,
            grid=(count // 2,),
            in_specs=[
                pl.BlockSpec((rows, units), lambda i, blocks: (0, 0)),
                column_block(units, 0),
                column_block(units, 1),
                column_block(units // block_units, 0),
                column_block(units // block_units, 1),
            ],
            out_specs=[
                pl.BlockSpec((2, rows, width), lambda i, blocks: (0, 0, 0))
                for _ in range(count // 2)
            ],
        ),
        out_shape=[jax.ShapeDtypeStruct((2, rows, width), kind)] * (count // 2),
        compiler_params=pltpu.CompilerParams(vmem_limit_bytes=vmem),
        cost_estimate=pl.CostEstimate(
            flops=2 * rows * units * width * count,
            bytes_accessed=3 * units * width * count,
            transcendentals=0,
        ),
        name="down_projection",
    )(blocks, tokens, coded_weight, coded_weight, block_exponent, block_exponent)


def round_kernel(after_ref, upper_ref, lower_ref, out_ref):
    half = upper_ref.shape[0]
    out_ref[:half] = upper_ref[...].astype(bf16)
    out_ref[half:] = lower_ref[...].astype(bf16)


def rounded_pair(wide, after):
    rows, columns = wide.shape
    layers, step = 2, rows // 3

    def half_layer(half):
        return pl.BlockSpec((step // 2, columns), lambda i: (2 * i + half, 0))

    return pl.pallas_call(
        round_kernel,
        grid=(layers,),
        in_specs=[pl.BlockSpec(memory_space=pl.ANY), half_layer(0), half_layer(1)],
        out_specs=pl.BlockSpec((step, columns), lambda i: (i, 0)),
        out_shape=jax.ShapeDtypeStruct((step * layers, columns), bf16),
        compiler_params=pltpu.CompilerParams(vmem_limit_bytes=vmem),
        cost_estimate=pl.CostEstimate(
            flops=layers * step * columns,
            bytes_accessed=6 * layers * step * columns,
            transcendentals=0,
        ),
        name="round_weight",
    )(after, wide, wide)


def together_kernel(first_ref, second_ref, first_out_ref, second_out_ref):
    first_out_ref[...] = first_ref[...]
    second_out_ref[...] = second_ref[...]


def together(first, second):
    return pl.pallas_call(
        together_kernel,
        in_specs=[pl.BlockSpec(memory_space=pltpu.VMEM)] * 2,
        out_specs=[pl.BlockSpec(memory_space=pltpu.VMEM)] * 2,
        out_shape=[jax.ShapeDtypeStruct(a.shape, a.dtype) for a in (first, second)],
        name="together",
    )(first, second)


def reduce_blocks(near, direct, own, q):
    low_right = send(near[0], along_first(1))
    high_left = send(near[1], along_first(-1))
    high_right = send(direct[1], along_first(1))
    low_left = send(direct[2], along_first(-1))
    low_right, high_left = direct[0] + low_right, direct[3] + high_left
    low_right = send(low_right, along_first(1))
    high_left = send(high_left, along_first(-1))
    summed = jnp.concatenate(
        [plus(own[0], low_right, low_left), plus(own[1], high_left, high_right)]
    )
    halved = summed.astype(bf16)

    def at(array, shift):
        return lax.dynamic_index_in_dim(array, (q + shift) % side, 0, keepdims=False)

    parts = [send(at(halved, shift), along_second(shift)) for shift in (1, 3, 2)]
    return plus(at(summed, 0), *parts), summed[0, :8, :128]


def body(
    gated_hidden,
    coded_weight,
    block_exponent,
    stream_input,
    lower_layer,
    middle_layer,
    prior_lower,
    prior_middle,
    prior_upper,
    accepted,
    draft_input_weight,
    draft_gain,
):
    steps, rows, unit_count = gated_hidden.shape
    feature_slice = stream_input.shape[2]
    out_slice = draft_input_weight.shape[2]
    replicas = lax.axis_size("replica")
    tensors = lax.axis_size("tensor")
    width = feature_slice * tensors
    slots_all = steps * rows * replicas
    slots = rows * 3 // 4
    x, c, p, q = place()

    with jax.named_scope("down"):
        tokens = gated_hidden.reshape(steps * rows, unit_count)
        second = jnp.arange(side, dtype=jnp.int32)

        def columns(shift):
            first = (p + shift) % side
            return jnp.where(c == 0, first * side + second, second * side + first)

        near = down_pieces(columns(2), tokens, coded_weight, block_exponent, bf16)
        near, accepted = lax.optimization_barrier((near, accepted))

    with jax.named_scope("select"):
        row = jnp.arange(rows, dtype=jnp.int32)
        before = row[:, None] <= row[None, :]
        first_live = (accepted >= 1).astype(jnp.int32)
        second_live = (accepted >= 2).astype(jnp.int32)
        first_slot = jnp.sum(jnp.where(before, first_live[:, None], 0), axis=0) - 1
        second_slot = 2 * slots - jnp.sum(jnp.where(before, second_live[:, None], 0), axis=0)
        first_slot = jnp.where(first_live == 1, first_slot, -1)
        second_slot = jnp.where(second_live == 1, second_slot, -1)
        slot = jnp.arange(2 * slots, dtype=jnp.int32)[:, None]
        slot_of = jnp.concatenate([first_slot, second_slot])
        select = (slot == slot_of[None, :]).astype(bf16)

        def pick(chosen, first, second):
            return jnp.dot(
                chosen, jnp.concatenate([first, second]), preferred_element_type=f32
            ).astype(bf16)

        pair = pick(
            select,
            jnp.concatenate([prior_lower, prior_middle], axis=1),
            jnp.concatenate([lower_layer, middle_layer], axis=1),
        )
        front = jnp.dot(
            select[:slots, :rows], prior_upper, preferred_element_type=f32
        ).astype(bf16)
        folded = jnp.concatenate([front[: slots // 2], front[slots // 2 :]], axis=1)
        payload = jnp.concatenate([pair, folded])
    gathered = lax.all_gather(payload, "replica", axis=0, tiled=True)

    with jax.named_scope("down"):
        others, payload = lax.optimization_barrier(
            (jnp.concatenate([columns(1), columns(3)]), payload)
        )
        direct = down_pieces(others, tokens, coded_weight, block_exponent, bf16)
        direct, mine = lax.optimization_barrier((direct, columns(0)))
        own = down_pieces(mine, tokens, coded_weight, block_exponent, f32)
    with jax.named_scope("reduce_down"):
        mixed, first_sum = reduce_blocks(near, direct, own, q)

    flat_weight = draft_input_weight.reshape(3 * feature_slice, out_slice)
    pair_weight = rounded_pair(flat_weight, first_sum)
    third_weight = draft_input_weight[2].astype(bf16)
    upper_layer = (
        stream_input.astype(f32) + mixed.reshape(steps, rows, feature_slice)
    ).astype(bf16)

    with jax.named_scope("back"):
        back = pick(select[slots:], prior_upper, upper_layer[0])
        chips = [back] + [send(back, along_x(-shift)) for shift in (1, 2, 3)]
        chips = jnp.stack(turned(chips, x))
        others = send(chips, other_core())

    with jax.named_scope("targets"):
        chosen = pick(select, upper_layer[0], upper_layer[1])
        parity = lax.axis_index("tensor") % 2
        even, odd = chosen[:slots], chosen[slots:]
        posted = [jnp.where((parity + turn) % 2 == 0, even, odd) for turn in range(2)]
        got = []
        for turn in range(2):
            routes = []
            for d in range(replicas * tensors):
                r, t = divmod(d, tensors)
                owner = t // 2
                taken = row_block(owner % cores, 2 * r + (t + turn) % 2)
                routes.append((d, owner * tensors + taken))
            got.append(send(posted[turn], routes))

    with jax.named_scope("forward"):
        by_replica = gathered.reshape(replicas, -1, 2 * feature_slice)
        stride = by_replica.shape[1]
        pairs, fronts = by_replica[:, : 2 * slots], by_replica[:, 2 * slots :]
        fronts = jnp.concatenate(
            [fronts[:, :, :feature_slice], fronts[:, :, feature_slice:]], axis=1
        )

        def replica_of(shift, half):
            return 2 * ((p + shift) % side) + half

        def pair_product(weight, shift, half):
            rows_of = lax.dynamic_slice_in_dim(
                gathered, replica_of(shift, half) * stride, 2 * slots, axis=0
            )
            return jnp.dot(rows_of, weight, preferred_element_type=f32)

        def third_product(weight, shift, half):
            rows_of = lax.dynamic_slice_in_dim(
                thirds, replica_of(shift, half) * 2 * slots, 2 * slots, axis=0
            )
            return jnp.dot(rows_of, weight, preferred_element_type=f32)

        def piece(total, kind):
            return total.astype(kind).reshape(2, slots, out_slice)

        far_pairs = [pair_product(pair_weight, 2, half) for half in range(2)]
        others, fronts, far_pairs, _ = lax.optimization_barrier(
            (others, fronts, far_pairs, posted)
        )
        backs = jnp.stack(
            [jnp.where(c == 0, chips, others), jnp.where(c == 0, others, chips)], axis=1
        ).reshape(replicas, slots, feature_slice)
        thirds = jnp.concatenate([fronts, backs], axis=1).reshape(-1, feature_slice)

        def far_third(half):
            chip = (p + 2) % side
            rows_of = [
                fronts[replica_of(2, half)],
                jnp.where(c == half, chips[chip], others[chip]),
            ]
            return jnp.dot(
                jnp.concatenate(rows_of), third_weight, preferred_element_type=f32
            )

        near = [piece(far_pairs[half] + far_third(half), bf16) for half in range(2)]
        _, got, pair_weight, third_weight = lax.optimization_barrier(
            (near, got, pair_weight, third_weight)
        )
        direct = [
            piece(
                pair_product(pair_weight, shift, half) + third_product(third_weight, shift, half),
                bf16,
            )
            for shift in (1, 3)
            for half in range(2)
        ]
        _, pair_weight, third_weight = lax.optimization_barrier(
            (direct, pair_weight, third_weight)
        )
        own = [
            piece(
                pair_product(pair_weight, 0, half) + third_product(third_weight, 0, half), f32
            )
            for half in range(2)
        ]

    with jax.named_scope("reduce_draft"):
        drafted, _ = reduce_blocks(near, direct, own, q)

    with jax.named_scope("norm"):
        front_rows = q % 2 == 0
        targets = jnp.concatenate(
            [jnp.where(front_rows, got[0], got[1]), jnp.where(front_rows, got[1], got[0])],
            axis=1,
        ).astype(f32)
        gain = draft_gain[None, :]
        scaled = gain * drafted
        sums = jnp.stack(
            [
                jnp.sum(drafted * drafted, axis=1),
                jnp.sum(scaled * scaled, axis=1),
                jnp.sum(scaled * targets, axis=1),
            ]
        )
        sums = sums + send(sums, other_core_rows())
        sums = sums + send(sums, along_x(1)) + send(sums, along_x(2)) + send(sums, along_x(3))
        scale = lax.rsqrt(sums[0] / width + epsilon)
        inner = (scale * sums[1] - sums[2]) / slots_all
        error = gain * (scaled * scale[:, None] - targets) / slots_all
        slope = (scale[:, None] * error - drafted * (scale**3 * inner / width)[:, None]).astype(
            bf16
        )

    with jax.named_scope("gather_slope"):
        ring = [slope] + [send(slope, along_second(-shift)) for shift in (1, 2, 3)]
        ring = turned(ring, q)
        upper_half, lower_half = jnp.concatenate(ring[:2]), jnp.concatenate(ring[2:])
        previous_upper = send(upper_half, along_first(1))
        following_lower = send(lower_half, along_first(-1))
        upper_again, lower_again = together(upper_half, lower_half)
        previous_lower = send(lower_again, along_first(1))
        following_upper = send(upper_again, along_first(-1))
        low = send(previous_upper, along_first(1))
        high = send(following_lower, along_first(-1))

    with jax.named_scope("step"):
        features = jnp.concatenate([pairs.reshape(-1, 2 * feature_slice), thirds], axis=1)

        def product(places, slopes):
            inputs = [
                lax.dynamic_slice_in_dim(
                    features, (2 * ((p + shift) % side) + half) * 2 * slots, 2 * slots, axis=0
                )
                for shift, half in places
            ]
            return lax.dot_general(
                jnp.concatenate(inputs),
                jnp.concatenate(slopes),
                (((0,), (0,)), ((), ())),
                preferred_element_type=f32,
            )

        total = lax.optimization_barrier(product([(0, 0), (0, 1)], [upper_half, lower_half]))
        total = lax.optimization_barrier(
            total + product([(3, 0), (1, 1)], [previous_upper, following_lower])
        )
        total = lax.optimization_barrier(
            total + product([(3, 1), (1, 0)], [previous_lower, following_upper])
        )
        total = total + product([(2, 0), (2, 1)], [low, high])
        new_weight = (flat_weight - step_rate * total).astype(bf16)
        new_weight = new_weight.reshape(draft_input_weight.shape)
    return (upper_layer, new_weight)


def solution(mesh):
    return jax.shard_map(
        body,
        mesh=mesh,
        in_specs=(
            P(None, "replica", "tensor"),
            P("tensor", None),
            P("tensor", None),
            P(None, "replica", "tensor"),
            P("replica", "tensor"),
            P("replica", "tensor"),
            P("replica", "tensor"),
            P("replica", "tensor"),
            P("replica", "tensor"),
            P("replica"),
            P(None, "tensor", "replica"),
            P("replica"),
        ),
        out_specs=(P(None, "replica", "tensor"), P(None, "tensor", "replica")),
        check_vma=False,
    )
```

```python
import functools

import jax
import jax.numpy as jnp
from jax import lax
from jax.experimental import pallas as pl
from jax.experimental.pallas import tpu as pltpu
from jax.sharding import PartitionSpec as P

step_rate = 8.0
epsilon = 1e-06
side = 4
cores = 2
block_units = 32
f32 = jnp.float32
bf16 = jnp.bfloat16
mesh_axes = ("replica", "tensor")
vmem = 56 * 1024 * 1024


def coordinates(device):
    replica, tensor = divmod(device, side * side)
    x, c = divmod(replica, cores)
    z, y = divmod(tensor, side)
    return x, c, z, y


def device_at(x, c, z, y):
    return ((x % side) * cores + c % cores) * side * side + (z % side) * side + y % side


def moved(target):
    return [(d, target(*coordinates(d))) for d in range(side * cores * side * side)]


def along_first(shift):
    return moved(
        lambda x, c, z, y: device_at(x, c, z + shift * (c == 0), y + shift * (c == 1))
    )


def along_second(shift):
    return moved(
        lambda x, c, z, y: device_at(x, c, z + shift * (c == 1), y + shift * (c == 0))
    )


def along_x(shift):
    return moved(lambda x, c, z, y: device_at(x + shift, c, z, y))


def other_core():
    return moved(lambda x, c, z, y: device_at(x, 1 - c, z, y))


def send(array, pairs):
    return lax.ppermute(array, mesh_axes, pairs)


def plus(*terms):
    return functools.reduce(jnp.add, [term.astype(f32) for term in terms])


def other_core_rows():
    return moved(lambda x, c, z, y: device_at(x, 1 - c, y, z))


def row_block(c, tensor):
    z, y = tensor // side, tensor % side
    return z * side + y if c == 0 else y * side + z


def turned(pieces, places):
    for bit in (1, 2):
        moves = places // bit % 2 == 1
        pieces = [
            jnp.where(moves, pieces[(j - bit) % side], pieces[j]) for j in range(side)
        ]
    return pieces


def place():
    replica, tensor = lax.axis_index("replica"), lax.axis_index("tensor")
    x, c = replica // cores, replica % cores
    z, y = tensor // side, tensor % side
    return x, c, jnp.where(c == 0, z, y), jnp.where(c == 0, y, z)


def down_kernel(blocks_ref, tokens_ref, *refs):
    coded_refs, exponent_refs, pieces = refs[:side], refs[side : 2 * side], refs[2 * side :]
    i = pl.program_id(0)
    totals = []
    for coded_ref, exponent_ref in zip(coded_refs, exponent_refs):
        units, columns = coded_ref.shape
        factor = jnp.exp2(exponent_ref[...].astype(f32) - 127.0).astype(bf16)
        weight = coded_ref[...].reshape(units // block_units, block_units, columns)
        weight = (weight * factor[:, None, :]).reshape(units, columns)
        totals.append(jnp.dot(tokens_ref[...], weight, preferred_element_type=f32))
    for k, piece in enumerate(pieces):

        @pl.when(i == k // 2)
        def _():
            for half in range(2):
                piece[half] = totals[k % 2 * 2 + half].astype(piece.dtype)


def down_pieces(blocks, tokens, coded_weight, block_exponent, kind):
    rows, units = tokens.shape
    width = coded_weight.shape[1] // (side * side)
    count = blocks.shape[0]

    def column_block(height, turn):
        return pl.BlockSpec((height, width), lambda i, blocks: (0, blocks[side * i + turn]))

    return pl.pallas_call(
        down_kernel,
        grid_spec=pltpu.PrefetchScalarGridSpec(
            num_scalar_prefetch=1,
            grid=(count // side,),
            in_specs=[pl.BlockSpec((rows, units), lambda i, blocks: (0, 0))]
            + [column_block(units, turn) for turn in range(side)]
            + [column_block(units // block_units, turn) for turn in range(side)],
            out_specs=[
                pl.BlockSpec((2, rows, width), lambda i, blocks: (0, 0, 0))
                for _ in range(count // 2)
            ],
        ),
        out_shape=[jax.ShapeDtypeStruct((2, rows, width), kind)] * (count // 2),
        compiler_params=pltpu.CompilerParams(vmem_limit_bytes=vmem),
        cost_estimate=pl.CostEstimate(
            flops=2 * rows * units * width * count,
            bytes_accessed=3 * units * width * count,
            transcendentals=0,
        ),
        name="down_projection",
    )(blocks, tokens, *[coded_weight] * side, *[block_exponent] * side)


def round_kernel(after_ref, upper_ref, lower_ref, out_ref):
    half = upper_ref.shape[0]
    out_ref[:half] = upper_ref[...].astype(bf16)
    out_ref[half:] = lower_ref[...].astype(bf16)


def rounded_pair(wide, after):
    rows, columns = wide.shape
    layers, step = 2, rows // 3

    def half_layer(half):
        return pl.BlockSpec((step // 2, columns), lambda i: (2 * i + half, 0))

    return pl.pallas_call(
        round_kernel,
        grid=(layers,),
        in_specs=[pl.BlockSpec(memory_space=pl.ANY), half_layer(0), half_layer(1)],
        out_specs=pl.BlockSpec((step, columns), lambda i: (i, 0)),
        out_shape=jax.ShapeDtypeStruct((step * layers, columns), bf16),
        compiler_params=pltpu.CompilerParams(vmem_limit_bytes=vmem),
        cost_estimate=pl.CostEstimate(
            flops=layers * step * columns,
            bytes_accessed=6 * layers * step * columns,
            transcendentals=0,
        ),
        name="round_weight",
    )(after, wide, wide)


def together_kernel(first_ref, second_ref, first_out_ref, second_out_ref):
    first_out_ref[...] = first_ref[...]
    second_out_ref[...] = second_ref[...]


def together(first, second):
    return pl.pallas_call(
        together_kernel,
        in_specs=[pl.BlockSpec(memory_space=pltpu.VMEM)] * 2,
        out_specs=[pl.BlockSpec(memory_space=pltpu.VMEM)] * 2,
        out_shape=[jax.ShapeDtypeStruct(a.shape, a.dtype) for a in (first, second)],
        name="together",
    )(first, second)


def reduce_blocks(near, direct, own, q):
    low_right = send(near[0], along_first(1))
    high_left = send(near[1], along_first(-1))
    high_right = send(direct[1], along_first(1))
    low_left = send(direct[2], along_first(-1))
    low_right, high_left = direct[0] + low_right, direct[3] + high_left
    low_right = send(low_right, along_first(1))
    high_left = send(high_left, along_first(-1))
    summed = jnp.concatenate(
        [plus(own[0], low_right, low_left), plus(own[1], high_left, high_right)]
    )
    halved = summed.astype(bf16)

    def at(array, shift):
        return lax.dynamic_index_in_dim(array, (q + shift) % side, 0, keepdims=False)

    parts = [send(at(halved, shift), along_second(shift)) for shift in (1, 3, 2)]
    return plus(at(summed, 0), *parts), summed[0, :8, :128]


def body(
    gated_hidden,
    coded_weight,
    block_exponent,
    stream_input,
    lower_layer,
    middle_layer,
    prior_lower,
    prior_middle,
    prior_upper,
    accepted,
    draft_input_weight,
    draft_gain,
):
    steps, rows, unit_count = gated_hidden.shape
    feature_slice = stream_input.shape[2]
    out_slice = draft_input_weight.shape[2]
    replicas = lax.axis_size("replica")
    tensors = lax.axis_size("tensor")
    width = feature_slice * tensors
    slots_all = steps * rows * replicas
    slots = rows * 3 // 4
    x, c, p, q = place()

    with jax.named_scope("down"):
        tokens = gated_hidden.reshape(steps * rows, unit_count)
        second = jnp.arange(side, dtype=jnp.int32)

        def columns(shift):
            first = (p + shift) % side
            return jnp.where(c == 0, first * side + second, second * side + first)

        near = down_pieces(columns(2), tokens, coded_weight, block_exponent, bf16)
        near, accepted = lax.optimization_barrier((near, accepted))

    with jax.named_scope("select"):
        row = jnp.arange(rows, dtype=jnp.int32)
        before = row[:, None] <= row[None, :]
        first_live = (accepted >= 1).astype(jnp.int32)
        second_live = (accepted >= 2).astype(jnp.int32)
        first_slot = jnp.sum(jnp.where(before, first_live[:, None], 0), axis=0) - 1
        second_slot = 2 * slots - jnp.sum(jnp.where(before, second_live[:, None], 0), axis=0)
        first_slot = jnp.where(first_live == 1, first_slot, -1)
        second_slot = jnp.where(second_live == 1, second_slot, -1)
        slot = jnp.arange(2 * slots, dtype=jnp.int32)[:, None]
        slot_of = jnp.concatenate([first_slot, second_slot])
        select = (slot == slot_of[None, :]).astype(bf16)

        def pick(chosen, first, second):
            return jnp.dot(
                chosen, jnp.concatenate([first, second]), preferred_element_type=f32
            ).astype(bf16)

        pair = pick(
            select,
            jnp.concatenate([prior_lower, prior_middle], axis=1),
            jnp.concatenate([lower_layer, middle_layer], axis=1),
        )
        front = jnp.dot(
            select[:slots, :rows], prior_upper, preferred_element_type=f32
        ).astype(bf16)
        folded = jnp.concatenate([front[: slots // 2], front[slots // 2 :]], axis=1)
        payload = jnp.concatenate([pair, folded])
    gathered = lax.all_gather(payload, "replica", axis=0, tiled=True)

    with jax.named_scope("down"):
        others, payload = lax.optimization_barrier(
            (jnp.concatenate([columns(1), columns(3)]), payload)
        )
        direct = down_pieces(others, tokens, coded_weight, block_exponent, bf16)
        direct, mine = lax.optimization_barrier((direct, columns(0)))
        own = down_pieces(mine, tokens, coded_weight, block_exponent, f32)
    with jax.named_scope("reduce_down"):
        mixed, first_sum = reduce_blocks(near, direct, own, q)

    flat_weight = draft_input_weight.reshape(3 * feature_slice, out_slice)
    pair_weight = rounded_pair(flat_weight, first_sum)
    third_weight = draft_input_weight[2].astype(bf16)
    upper_layer = (
        stream_input.astype(f32) + mixed.reshape(steps, rows, feature_slice)
    ).astype(bf16)

    with jax.named_scope("back"):
        back = pick(select[slots:], prior_upper, upper_layer[0])
        chips = [back] + [send(back, along_x(-shift)) for shift in (1, 2, 3)]
        chips = jnp.stack(turned(chips, x))
        others = send(chips, other_core())

    with jax.named_scope("targets"):
        chosen = pick(select, upper_layer[0], upper_layer[1])
        parity = lax.axis_index("tensor") % 2
        even, odd = chosen[:slots], chosen[slots:]
        posted = [jnp.where((parity + turn) % 2 == 0, even, odd) for turn in range(2)]
        got = []
        for turn in range(2):
            routes = []
            for d in range(replicas * tensors):
                r, t = divmod(d, tensors)
                owner = t // 2
                taken = row_block(owner % cores, 2 * r + (t + turn) % 2)
                routes.append((d, owner * tensors + taken))
            got.append(send(posted[turn], routes))

    with jax.named_scope("forward"):
        by_replica = gathered.reshape(replicas, -1, 2 * feature_slice)
        stride = by_replica.shape[1]
        pairs, fronts = by_replica[:, : 2 * slots], by_replica[:, 2 * slots :]
        fronts = jnp.concatenate(
            [fronts[:, :, :feature_slice], fronts[:, :, feature_slice:]], axis=1
        )

        def replica_of(shift, half):
            return 2 * ((p + shift) % side) + half

        def pair_product(weight, shift, half):
            rows_of = lax.dynamic_slice_in_dim(
                gathered, replica_of(shift, half) * stride, 2 * slots, axis=0
            )
            return jnp.dot(rows_of, weight, preferred_element_type=f32)

        def third_product(weight, shift, half):
            rows_of = lax.dynamic_slice_in_dim(
                thirds, replica_of(shift, half) * 2 * slots, 2 * slots, axis=0
            )
            return jnp.dot(rows_of, weight, preferred_element_type=f32)

        def piece(total, kind):
            return total.astype(kind).reshape(2, slots, out_slice)

        far_pairs = [
            pair_product(pair_weight, shift, half) for shift in (2, 1, 3) for half in range(2)
        ]
        others, fronts, far_pairs, _ = lax.optimization_barrier(
            (others, fronts, far_pairs, posted)
        )
        backs = jnp.stack(
            [jnp.where(c == 0, chips, others), jnp.where(c == 0, others, chips)], axis=1
        ).reshape(replicas, slots, feature_slice)
        thirds = jnp.concatenate([fronts, backs], axis=1).reshape(-1, feature_slice)
        near = [
            piece(far_pairs[half] + third_product(third_weight, 2, half), bf16)
            for half in range(2)
        ]
        _, got, pair_weight, third_weight = lax.optimization_barrier(
            (near, got, pair_weight, third_weight)
        )
        direct = [
            piece(far_pairs[2 + k] + third_product(third_weight, (1, 3)[k // 2], k % 2), bf16)
            for k in range(4)
        ]
        _, pair_weight, third_weight = lax.optimization_barrier(
            (direct, pair_weight, third_weight)
        )
        own = [
            piece(
                pair_product(pair_weight, 0, half) + third_product(third_weight, 0, half), f32
            )
            for half in range(2)
        ]

    with jax.named_scope("reduce_draft"):
        drafted, _ = reduce_blocks(near, direct, own, q)

    with jax.named_scope("norm"):
        front_rows = q % 2 == 0
        targets = jnp.concatenate(
            [jnp.where(front_rows, got[0], got[1]), jnp.where(front_rows, got[1], got[0])],
            axis=1,
        ).astype(f32)
        gain = draft_gain[None, :]
        scaled = gain * drafted
        sums = jnp.stack(
            [
                jnp.sum(drafted * drafted, axis=1),
                jnp.sum(scaled * scaled, axis=1),
                jnp.sum(scaled * targets, axis=1),
            ]
        )
        sums = sums + send(sums, other_core_rows())
        sums = sums + send(sums, along_x(1)) + send(sums, along_x(2)) + send(sums, along_x(3))
        scale = lax.rsqrt(sums[0] / width + epsilon)
        inner = (scale * sums[1] - sums[2]) / slots_all
        error = gain * (scaled * scale[:, None] - targets) / slots_all
        slope = (scale[:, None] * error - drafted * (scale**3 * inner / width)[:, None]).astype(
            bf16
        )

    with jax.named_scope("gather_slope"):
        ring = [slope] + [send(slope, along_second(-shift)) for shift in (1, 2, 3)]
        ring = turned(ring, q)
        upper_half, lower_half = jnp.concatenate(ring[:2]), jnp.concatenate(ring[2:])
        previous_upper = send(upper_half, along_first(1))
        following_lower = send(lower_half, along_first(-1))
        upper_again, lower_again = together(upper_half, lower_half)
        previous_lower = send(lower_again, along_first(1))
        following_upper = send(upper_again, along_first(-1))
        low = send(previous_upper, along_first(1))
        high = send(following_lower, along_first(-1))

    with jax.named_scope("step"):
        features = jnp.concatenate([pairs.reshape(-1, 2 * feature_slice), thirds], axis=1)

        def product(places, slopes):
            inputs = [
                lax.dynamic_slice_in_dim(
                    features, (2 * ((p + shift) % side) + half) * 2 * slots, 2 * slots, axis=0
                )
                for shift, half in places
            ]
            return lax.dot_general(
                jnp.concatenate(inputs),
                jnp.concatenate(slopes),
                (((0,), (0,)), ((), ())),
                preferred_element_type=f32,
            )

        total = product([(0, 0), (0, 1)], [upper_half, lower_half])
        total = lax.optimization_barrier(
            total
            + product(
                [(3, 0), (3, 1), (1, 0), (1, 1)],
                [previous_upper, previous_lower, following_upper, following_lower],
            )
        )
        total = total + product([(2, 0), (2, 1)], [low, high])
        new_weight = (flat_weight - step_rate * total).astype(bf16)
        new_weight = new_weight.reshape(draft_input_weight.shape)
    return (upper_layer, new_weight)


def solution(mesh):
    return jax.shard_map(
        body,
        mesh=mesh,
        in_specs=(
            P(None, "replica", "tensor"),
            P("tensor", None),
            P("tensor", None),
            P(None, "replica", "tensor"),
            P("replica", "tensor"),
            P("replica", "tensor"),
            P("replica", "tensor"),
            P("replica", "tensor"),
            P("replica", "tensor"),
            P("replica"),
            P(None, "tensor", "replica"),
            P("replica"),
        ),
        out_specs=(P(None, "replica", "tensor"), P(None, "tensor", "replica")),
        check_vma=False,
    )
```

```python
import functools

import jax
import jax.numpy as jnp
from jax import lax
from jax.experimental import pallas as pl
from jax.experimental.pallas import tpu as pltpu
from jax.sharding import PartitionSpec as P

step_rate = 8.0
epsilon = 1e-06
side = 4
cores = 2
block_units = 32
f32 = jnp.float32
bf16 = jnp.bfloat16
mesh_axes = ("replica", "tensor")
vmem = 56 * 1024 * 1024


def coordinates(device):
    replica, tensor = divmod(device, side * side)
    x, c = divmod(replica, cores)
    z, y = divmod(tensor, side)
    return x, c, z, y


def device_at(x, c, z, y):
    return ((x % side) * cores + c % cores) * side * side + (z % side) * side + y % side


def moved(target):
    return [(d, target(*coordinates(d))) for d in range(side * cores * side * side)]


def along_first(shift):
    return moved(
        lambda x, c, z, y: device_at(x, c, z + shift * (c == 1), y + shift * (c == 0))
    )


def along_second(shift):
    return moved(
        lambda x, c, z, y: device_at(x, c, z + shift * (c == 0), y + shift * (c == 1))
    )


def along_x(shift):
    return moved(lambda x, c, z, y: device_at(x + shift, c, z, y))


def other_core():
    return moved(lambda x, c, z, y: device_at(x, 1 - c, z, y))


def send(array, pairs):
    return lax.ppermute(array, mesh_axes, pairs)


def plus(*terms):
    return functools.reduce(jnp.add, [term.astype(f32) for term in terms])


def other_core_rows():
    return moved(lambda x, c, z, y: device_at(x, 1 - c, y, z))


def row_block(c, tensor):
    z, y = tensor // side, tensor % side
    return y * side + z if c == 0 else z * side + y


def turned(pieces, places):
    for bit in (1, 2):
        moves = places // bit % 2 == 1
        pieces = [
            jnp.where(moves, pieces[(j - bit) % side], pieces[j]) for j in range(side)
        ]
    return pieces


def place():
    replica, tensor = lax.axis_index("replica"), lax.axis_index("tensor")
    x, c = replica // cores, replica % cores
    z, y = tensor // side, tensor % side
    return x, c, jnp.where(c == 0, y, z), jnp.where(c == 0, z, y)


def down_kernel(blocks_ref, tokens_ref, *refs):
    coded_refs, exponent_refs, pieces = refs[:2], refs[2:4], refs[4:]
    i = pl.program_id(0)
    totals = []
    for coded_ref, exponent_ref in zip(coded_refs, exponent_refs):
        units, columns = coded_ref.shape
        factor = jnp.exp2(exponent_ref[...].astype(f32) - 127.0).astype(bf16)
        weight = coded_ref[...].reshape(units // block_units, block_units, columns)
        weight = (weight * factor[:, None, :]).reshape(units, columns)
        totals.append(jnp.dot(tokens_ref[...], weight, preferred_element_type=f32))
    for k, piece in enumerate(pieces):

        @pl.when(i == k)
        def _():
            for half, total in enumerate(totals):
                piece[half] = total.astype(piece.dtype)


def down_pieces(blocks, tokens, coded_weight, block_exponent, kind):
    rows, units = tokens.shape
    width = coded_weight.shape[1] // (side * side)
    count = blocks.shape[0]

    def column_block(height, half):
        return pl.BlockSpec((height, width), lambda i, blocks: (0, blocks[2 * i + half]))

    return pl.pallas_call(
        down_kernel,
        grid_spec=pltpu.PrefetchScalarGridSpec(
            num_scalar_prefetch=1,
            grid=(count // 2,),
            in_specs=[
                pl.BlockSpec((rows, units), lambda i, blocks: (0, 0)),
                column_block(units, 0),
                column_block(units, 1),
                column_block(units // block_units, 0),
                column_block(units // block_units, 1),
            ],
            out_specs=[
                pl.BlockSpec((2, rows, width), lambda i, blocks: (0, 0, 0))
                for _ in range(count // 2)
            ],
        ),
        out_shape=[jax.ShapeDtypeStruct((2, rows, width), kind)] * (count // 2),
        compiler_params=pltpu.CompilerParams(vmem_limit_bytes=vmem),
        cost_estimate=pl.CostEstimate(
            flops=2 * rows * units * width * count,
            bytes_accessed=3 * units * width * count,
            transcendentals=0,
        ),
        name="down_projection",
    )(blocks, tokens, coded_weight, coded_weight, block_exponent, block_exponent)


def round_kernel(after_ref, upper_ref, lower_ref, out_ref):
    half = upper_ref.shape[0]
    out_ref[:half] = upper_ref[...].astype(bf16)
    out_ref[half:] = lower_ref[...].astype(bf16)


def rounded_layers(wide, layers, start, after):
    rows, columns = wide.shape
    step = rows // 3

    def half_layer(half):
        return pl.BlockSpec((step // 2, columns), lambda i: (2 * (start + i) + half, 0))

    return pl.pallas_call(
        round_kernel,
        grid=(layers,),
        in_specs=[pl.BlockSpec(memory_space=pl.ANY), half_layer(0), half_layer(1)],
        out_specs=pl.BlockSpec((step, columns), lambda i: (i, 0)),
        out_shape=jax.ShapeDtypeStruct((step * layers, columns), bf16),
        compiler_params=pltpu.CompilerParams(vmem_limit_bytes=vmem),
        cost_estimate=pl.CostEstimate(
            flops=layers * step * columns,
            bytes_accessed=6 * layers * step * columns,
            transcendentals=0,
        ),
        name="round_weight",
    )(after, wide, wide)


def together_kernel(first_ref, second_ref, first_out_ref, second_out_ref):
    first_out_ref[...] = first_ref[...]
    second_out_ref[...] = second_ref[...]


def together(first, second):
    return pl.pallas_call(
        together_kernel,
        in_specs=[pl.BlockSpec(memory_space=pltpu.VMEM)] * 2,
        out_specs=[pl.BlockSpec(memory_space=pltpu.VMEM)] * 2,
        out_shape=[jax.ShapeDtypeStruct(a.shape, a.dtype) for a in (first, second)],
        name="together",
    )(first, second)


def reduce_blocks(near, direct, own, q):
    low_right = send(near[0], along_first(1))
    high_left = send(near[1], along_first(-1))
    high_right = send(direct[1], along_first(1))
    low_left = send(direct[2], along_first(-1))
    low_right, high_left = direct[0] + low_right, direct[3] + high_left
    low_right = send(low_right, along_first(1))
    high_left = send(high_left, along_first(-1))
    summed = jnp.concatenate(
        [plus(own[0], low_right, low_left), plus(own[1], high_left, high_right)]
    )
    halved = summed.astype(bf16)

    def at(array, shift):
        return lax.dynamic_index_in_dim(array, (q + shift) % side, 0, keepdims=False)

    parts = [send(at(halved, shift), along_second(shift)) for shift in (1, 3, 2)]
    return plus(at(summed, 0), *parts), summed[0, :8, :128]


def body(
    gated_hidden,
    coded_weight,
    block_exponent,
    stream_input,
    lower_layer,
    middle_layer,
    prior_lower,
    prior_middle,
    prior_upper,
    accepted,
    draft_input_weight,
    draft_gain,
):
    steps, rows, unit_count = gated_hidden.shape
    feature_slice = stream_input.shape[2]
    out_slice = draft_input_weight.shape[2]
    replicas = lax.axis_size("replica")
    tensors = lax.axis_size("tensor")
    width = feature_slice * tensors
    slots_all = steps * rows * replicas
    slots = rows * 3 // 4
    x, c, p, q = place()

    with jax.named_scope("down"):
        tokens = gated_hidden.reshape(steps * rows, unit_count)
        second = jnp.arange(side, dtype=jnp.int32)

        def columns(shift):
            first = (p + shift) % side
            return jnp.where(c == 0, second * side + first, first * side + second)

        near = down_pieces(columns(2), tokens, coded_weight, block_exponent, bf16)
        near, accepted = lax.optimization_barrier((near, accepted))

    with jax.named_scope("select"):
        row = jnp.arange(rows, dtype=jnp.int32)
        before = row[:, None] <= row[None, :]
        first_live = (accepted >= 1).astype(jnp.int32)
        second_live = (accepted >= 2).astype(jnp.int32)
        first_slot = jnp.sum(jnp.where(before, first_live[:, None], 0), axis=0) - 1
        second_slot = 2 * slots - jnp.sum(jnp.where(before, second_live[:, None], 0), axis=0)
        first_slot = jnp.where(first_live == 1, first_slot, -1)
        second_slot = jnp.where(second_live == 1, second_slot, -1)
        slot = jnp.arange(2 * slots, dtype=jnp.int32)[:, None]
        slot_of = jnp.concatenate([first_slot, second_slot])
        select = (slot == slot_of[None, :]).astype(bf16)

        def pick(chosen, first, second):
            return jnp.dot(
                chosen, jnp.concatenate([first, second]), preferred_element_type=f32
            ).astype(bf16)

        pair = pick(
            select,
            jnp.concatenate([prior_lower, prior_middle], axis=1),
            jnp.concatenate([lower_layer, middle_layer], axis=1),
        )
        front = jnp.dot(
            select[:slots, :rows], prior_upper, preferred_element_type=f32
        ).astype(bf16)
        folded = jnp.concatenate([front[: slots // 2], front[slots // 2 :]], axis=1)
        payload = jnp.concatenate([pair, folded])
    gathered = lax.all_gather(payload, "replica", axis=0, tiled=True)

    with jax.named_scope("down"):
        others, payload = lax.optimization_barrier(
            (jnp.concatenate([columns(1), columns(3)]), payload)
        )
        direct = down_pieces(others, tokens, coded_weight, block_exponent, bf16)
        direct, mine = lax.optimization_barrier((direct, columns(0)))
        own = down_pieces(mine, tokens, coded_weight, block_exponent, f32)
    with jax.named_scope("reduce_down"):
        mixed, first_sum = reduce_blocks(near, direct, own, q)

    flat_weight = draft_input_weight.reshape(3 * feature_slice, out_slice)
    pair_weight = rounded_layers(flat_weight, 2, 0, first_sum)
    third_weight = rounded_layers(flat_weight, 1, 2, first_sum)
    upper_layer = (
        stream_input.astype(f32) + mixed.reshape(steps, rows, feature_slice)
    ).astype(bf16)

    with jax.named_scope("back"):
        back = pick(select[slots:], prior_upper, upper_layer[0])
        chips = [back] + [send(back, along_x(-shift)) for shift in (1, 2, 3)]
        chips = jnp.stack(turned(chips, x))
        others = send(chips, other_core())

    with jax.named_scope("targets"):
        chosen = pick(select, upper_layer[0], upper_layer[1])
        parity = lax.axis_index("tensor") % 2
        even, odd = chosen[:slots], chosen[slots:]
        posted = [jnp.where((parity + turn) % 2 == 0, even, odd) for turn in range(2)]
        got = []
        for turn in range(2):
            routes = []
            for d in range(replicas * tensors):
                r, t = divmod(d, tensors)
                owner = t // 2
                taken = row_block(owner % cores, 2 * r + (t + turn) % 2)
                routes.append((d, owner * tensors + taken))
            got.append(send(posted[turn], routes))

    with jax.named_scope("forward"):
        by_replica = gathered.reshape(replicas, -1, 2 * feature_slice)
        stride = by_replica.shape[1]
        pairs, fronts = by_replica[:, : 2 * slots], by_replica[:, 2 * slots :]
        fronts = jnp.concatenate(
            [fronts[:, :, :feature_slice], fronts[:, :, feature_slice:]], axis=1
        )

        def replica_of(shift, half):
            return 2 * ((p + shift) % side) + half

        def pair_product(weight, shift, half):
            rows_of = lax.dynamic_slice_in_dim(
                gathered, replica_of(shift, half) * stride, 2 * slots, axis=0
            )
            return jnp.dot(rows_of, weight, preferred_element_type=f32)

        def third_product(weight, shift, half):
            rows_of = lax.dynamic_slice_in_dim(
                thirds, replica_of(shift, half) * 2 * slots, 2 * slots, axis=0
            )
            return jnp.dot(rows_of, weight, preferred_element_type=f32)

        def piece(total, kind):
            return total.astype(kind).reshape(2, slots, out_slice)

        far_pairs = [
            pair_product(pair_weight, shift, half) for shift in (2, 1, 3) for half in range(2)
        ]
        others, fronts, far_pairs, _ = lax.optimization_barrier(
            (others, fronts, far_pairs, posted)
        )
        backs = jnp.stack(
            [jnp.where(c == 0, chips, others), jnp.where(c == 0, others, chips)], axis=1
        ).reshape(replicas, slots, feature_slice)
        thirds = jnp.concatenate([fronts, backs], axis=1).reshape(-1, feature_slice)
        near = [
            piece(far_pairs[half] + third_product(third_weight, 2, half), bf16)
            for half in range(2)
        ]
        _, got, pair_weight, third_weight = lax.optimization_barrier(
            (near, got, pair_weight, third_weight)
        )
        direct = [
            piece(far_pairs[2 + k] + third_product(third_weight, (1, 3)[k // 2], k % 2), bf16)
            for k in range(4)
        ]
        _, pair_weight, third_weight = lax.optimization_barrier(
            (direct, pair_weight, third_weight)
        )
        own = [
            piece(
                pair_product(pair_weight, 0, half) + third_product(third_weight, 0, half), f32
            )
            for half in range(2)
        ]

    with jax.named_scope("reduce_draft"):
        drafted, _ = reduce_blocks(near, direct, own, q)

    with jax.named_scope("norm"):
        front_rows = q % 2 == 0
        targets = jnp.concatenate(
            [jnp.where(front_rows, got[0], got[1]), jnp.where(front_rows, got[1], got[0])],
            axis=1,
        ).astype(f32)
        gain = draft_gain[None, :]
        scaled = gain * drafted
        sums = jnp.stack(
            [
                jnp.sum(drafted * drafted, axis=1),
                jnp.sum(scaled * scaled, axis=1),
                jnp.sum(scaled * targets, axis=1),
            ]
        )
        sums = sums + send(sums, other_core_rows())
        sums = sums + send(sums, along_x(1)) + send(sums, along_x(2)) + send(sums, along_x(3))
        scale = lax.rsqrt(sums[0] / width + epsilon)
        inner = (scale * sums[1] - sums[2]) / slots_all
        error = gain * (scaled * scale[:, None] - targets) / slots_all
        slope = (scale[:, None] * error - drafted * (scale**3 * inner / width)[:, None]).astype(
            bf16
        )

    with jax.named_scope("gather_slope"):
        ring = [slope] + [send(slope, along_second(-shift)) for shift in (1, 2, 3)]
        ring = turned(ring, q)
        upper_half, lower_half = jnp.concatenate(ring[:2]), jnp.concatenate(ring[2:])
        previous_upper = send(upper_half, along_first(1))
        following_lower = send(lower_half, along_first(-1))
        upper_again, lower_again = together(upper_half, lower_half)
        previous_lower = send(lower_again, along_first(1))
        following_upper = send(upper_again, along_first(-1))
        low = send(previous_upper, along_first(1))
        high = send(following_lower, along_first(-1))

    with jax.named_scope("step"):
        features = jnp.concatenate([pairs.reshape(-1, 2 * feature_slice), thirds], axis=1)

        def product(places, slopes):
            inputs = [
                lax.dynamic_slice_in_dim(
                    features, (2 * ((p + shift) % side) + half) * 2 * slots, 2 * slots, axis=0
                )
                for shift, half in places
            ]
            return lax.dot_general(
                jnp.concatenate(inputs),
                jnp.concatenate(slopes),
                (((0,), (0,)), ((), ())),
                preferred_element_type=f32,
            )

        total = product([(0, 0), (0, 1)], [upper_half, lower_half])
        total = lax.optimization_barrier(
            total
            + product(
                [(3, 0), (3, 1), (1, 0), (1, 1)],
                [previous_upper, previous_lower, following_upper, following_lower],
            )
        )
        total = total + product([(2, 0), (2, 1)], [low, high])
        new_weight = (flat_weight - step_rate * total).astype(bf16)
        new_weight = new_weight.reshape(draft_input_weight.shape)
    return (upper_layer, new_weight)


def solution(mesh):
    return jax.shard_map(
        body,
        mesh=mesh,
        in_specs=(
            P(None, "replica", "tensor"),
            P("tensor", None),
            P("tensor", None),
            P(None, "replica", "tensor"),
            P("replica", "tensor"),
            P("replica", "tensor"),
            P("replica", "tensor"),
            P("replica", "tensor"),
            P("replica", "tensor"),
            P("replica"),
            P(None, "tensor", "replica"),
            P("replica"),
        ),
        out_specs=(P(None, "replica", "tensor"), P(None, "tensor", "replica")),
        check_vma=False,
    )
```
